32 devices in a mesh: half: 2 (over x), batch: 16 (over z, y, core).
Axes of the slice: x: 2, y: 2, z: 4, core: 2. Of those that a mesh axis runs over, the one named last changes fastest.
Arguments:
- block_input: bfloat16 [2, 16, 1024, 512], P('half', 'batch'), may hold values from -6 to 6
- memory: bfloat16 [2, 16, 1024, 512], P(None, 'batch', 'half'), may hold values from -6 to 6
- memory_grad_rest: float32 [2, 16, 1024, 512], P(None, 'batch', 'half'), may hold values from -0.625 to 0.625
- output_grad: bfloat16 [2, 16, 1024, 512], P('half', 'batch'), may hold values from -8 to 8
- target_length: int32 [2, 16], P('half', 'batch'), may hold values from 512 to 1024, as said below
- source_length: int32 [2, 16], P('half', 'batch'), may hold values from 256 to 1024, as said below
- self_maps: bfloat16 [3, 512, 512], replicated, may hold values from -0.25 to 0.25
- self_output: bfloat16 [512, 512], replicated, may hold values from -1 to 1
- cross_maps: bfloat16 [3, 512, 512], replicated, may hold values from -0.25 to 0.25
- cross_output: bfloat16 [512, 512], replicated, may hold values from -1 to 1
- attention_bias: float32 [6, 512], replicated, may hold values from -1.25 to 1.25
- expand_weight: bfloat16 [512, 2048], replicated, may hold values from -0.25 to 0.25
- expand_bias: float32 [2048], replicated, may hold values from -1.25 to 1.25
- shrink_weight: bfloat16 [2048, 512], replicated, may hold values from -0.125 to 0.125
- shrink_bias: float32 [512], replicated, may hold values from -1.25 to 1.25
- norm_gain: float32 [3, 512], replicated, may hold values from 0.5 to 1.5
- norm_bias: float32 [3, 512], replicated, may hold values from -1.25 to 1.25
- residual_scale: float32 [3, 512], replicated, may hold values from 0.8 to 2
Outputs:
- layer_output: float32 [2, 16, 1024, 512], P('half', 'batch')
- input_grad: float32 [2, 16, 1024, 512], P('half', 'batch')
- memory_grad: float32 [2, 16, 1024, 512], P(None, 'batch', 'half')
- self_maps_grad: float32 [3, 512, 512], P(None, 'batch')
- self_output_grad: float32 [512, 512], P('batch')
- cross_maps_grad: float32 [3, 512, 512], P(None, 'batch')
- cross_output_grad: float32 [512, 512], P('batch')
- attention_bias_grad: float32 [6, 512], P(None, 'batch')
- expand_weight_grad: float32 [512, 2048], P('batch')
- expand_bias_grad: float32 [2048], P('batch')
- shrink_weight_grad: float32 [2048, 512], P('batch')
- shrink_bias_grad: float32 [512], P('batch')
- norm_gain_grad: float32 [3, 512], P(None, 'batch')
- norm_bias_grad: float32 [3, 512], P(None, 'batch')
- residual_scale_grad: float32 [3, 512], P(None, 'batch')
The draws below stay inside these ranges and needn't reach their ends.
Inputs may be any that keep to these rules, and one draw needn't show every extreme that they name: `target_length`: at least one row has the full length 1024. `source_length`: at least one row has the full length 1024.
All inputs are finite; a program needn't handle non-finite values.
Results may differ from the reference program's by a relative error of at most 0.019.
Values may be sent and summed in bfloat16 or wider, within the bound.
No kernel may reach another device: no remote copies, remote signals or barrier semaphores. Data moves between devices by JAX's collectives and lax.ppermute only.
A program may use at most 256 MiB of HBM per device.

```python
import math
import jax
import jax.numpy as jnp
from jax import lax

D = 512
HEADS = 8
HEAD = 64
FF = 2048
L = 1024
S = 1024
BH = 16


def full_row(key, floor, top):
    first, second = jax.random.split(key)
    lengths = jax.random.randint(first, (2 * BH,), floor, top + 1)
    chosen = jax.random.randint(second, (), 0, 2 * BH)
    lengths = jnp.where(jnp.arange(2 * BH) == chosen, top, lengths)
    return lengths.reshape(2, BH).astype(jnp.int32)


def draw_target_length(key, part):
    key = jax.random.fold_in(key, 11)
    return full_row(key, L // 2, L)


def draw_source_length(key, part):
    key = jax.random.fold_in(key, 23)
    return full_row(key, S // 4, S)


def spiked(drawn, key, source, target, blocks, factor):
    def block_of(position):
        return (jnp.arange(drawn.shape[position]) // (drawn.shape[position] // blocks)).reshape((-1,) + (1,) * (drawn.ndim - 1 - position))

    near = jax.random.permutation(key, blocks)[block_of(target)]
    other_side = (block_of(target) + blocks // 2) % blocks
    return jnp.where((block_of(source) == near) | (block_of(source) == other_side), factor * drawn, drawn)


def steps_of(stream_key, dims, pieces, low, top_value):
    factor_of, own = 1.0, jax.random.fold_in(stream_key, 6)
    for dim, shards_of in pieces:
        draws = jnp.exp(jax.random.uniform(jax.random.fold_in(own, dim), (shards_of,), jnp.float32, low / len(pieces), top_value / len(pieces)))
        factor_of = factor_of * jnp.repeat(draws, dims[dim] // shards_of).reshape([-1 if axis == dim else 1 for axis in range(len(dims))])
    return factor_of


def centred(rng, extent, width, reach, cuts=(), held_as=jnp.bfloat16):
    array = width * jax.random.normal(rng, extent, jnp.float32)
    if cuts:
        array = array * steps_of(rng, extent, cuts, -0.22, 0.18)
    return jnp.clip(array, -reach, reach).astype(held_as)


def heavy_noise(key, shape, deviation, bound, cuts, heavy, kind=jnp.bfloat16):
    values = deviation * jax.random.normal(key, shape, jnp.float32)
    if cuts:
        values = values * steps_of(key, shape, cuts, -0.22, 0.18)
    return jnp.clip(spiked(values, jax.random.fold_in(key, 3), *heavy), -bound, bound).astype(kind)


def setup_inputs(seed: int = 0) -> dict:
    key_list = jax.random.split(jax.random.key(seed), 19)
    block_input = centred(key_list[0], (2, BH, L, D), 1.0, 6.0, ((0, 2), (1, 16)))
    memory = centred(key_list[1], (2, BH, S, D), 1.0, 6.0, ((1, 16), (2, 2)))
    memory_grad_rest = centred(key_list[2], (2, BH, S, D), 0.1, 0.625, ((1, 16), (2, 2)), jnp.float32)
    output_grad = heavy_noise(key_list[3], (2, BH, L, D), 1.0, 8.0, ((0, 2), (1, 16)), (1, 3, 16, 2.0))
    target_length = draw_target_length(jax.random.fold_in(key_list[18], 71), 0)
    source_length = draw_source_length(jax.random.fold_in(key_list[18], 71), 0)
    self_maps = centred(key_list[6], (3, D, D), D ** -0.5, 0.25)
    self_output = centred(key_list[7], (D, D), (D // 16) ** -0.5, 1.0)
    cross_maps = centred(key_list[8], (3, D, D), D ** -0.5, 0.25)
    cross_output = centred(key_list[9], (D, D), (D // 16) ** -0.5, 1.0)
    attention_bias = centred(key_list[10], (6, D), 0.2, 1.25, (), jnp.float32)
    expand_weight = centred(key_list[11], (D, FF), D ** -0.5, 0.25)
    expand_bias = centred(key_list[12], (FF,), 0.2, 1.25, (), jnp.float32)
    shrink_weight = centred(key_list[13], (FF, D), FF ** -0.5, 0.125)
    shrink_bias = centred(key_list[14], (D,), 0.2, 1.25, (), jnp.float32)
    norm_gain = jnp.clip(1.0 + 0.1 * jax.random.normal(key_list[15], (3, D), jnp.float32), 0.5, 1.5)
    norm_bias = centred(key_list[16], (3, D), 0.2, 1.25, (), jnp.float32)
    residual_scale = jnp.clip(jnp.exp(jax.random.uniform(key_list[17], (3, D), jnp.float32, math.log(0.8), math.log(2.0))), 0.8, 2.0)
    return dict(block_input=block_input, memory=memory, memory_grad_rest=memory_grad_rest, output_grad=output_grad, target_length=target_length, source_length=source_length, self_maps=self_maps, self_output=self_output, cross_maps=cross_maps, cross_output=cross_output, attention_bias=attention_bias, expand_weight=expand_weight, expand_bias=expand_bias, shrink_weight=shrink_weight, shrink_bias=shrink_bias, norm_gain=norm_gain, norm_bias=norm_bias, residual_scale=residual_scale)


highest = lax.Precision.HIGHEST
eps = 1e-05
masked_score = -1000000000.0

@jax.custom_vjp
def low(v):
    return lax.optimization_barrier(v.astype(jnp.bfloat16)).astype(jnp.float32)

@jax.custom_vjp
def low_back(v):
    return v

def low_keep(v):
    return (low(v), None)

def low_pass(kept, grad):
    return (grad,)

def back_keep(v):
    return (v, None)

def back_low(kept, grad):
    return (low(grad),)
low.defvjp(low_keep, low_pass)
low_back.defvjp(back_keep, back_low)

def product(left, right):
    return jnp.matmul(left, right, precision=highest)

def normalize(total, gain, shift):
    center = total - lax.optimization_barrier(jnp.mean(total, axis=-1, keepdims=True))
    spread = lax.optimization_barrier(jnp.mean(center * center, axis=-1, keepdims=True))
    return center * lax.rsqrt(spread + eps) * gain + shift

def attend(query, keys, values, valid):
    scores = low_back(jnp.einsum('qhe,khe->hqk', query, keys, precision=highest) * HEAD ** (-0.5))
    scores = jnp.where(valid[None], scores, masked_score)
    top = lax.optimization_barrier(jnp.max(scores, axis=-1, keepdims=True))
    expo = jnp.exp(scores - top)
    probs = low(expo / lax.optimization_barrier(jnp.sum(expo, axis=-1, keepdims=True)))
    mixed = jnp.einsum('hqk,khe->qhe', probs, values, precision=highest)
    return low_back(low(mixed))

def forward(inputs, source, self_maps, self_output, cross_maps, cross_output, attention_bias, expand_weight, expand_bias, shrink_weight, shrink_bias, norm_gain, norm_bias, residual_scale, target_length, source_length):
    rows = inputs.shape[0]
    target_pos = jnp.arange(L, dtype=jnp.int32)
    source_pos = jnp.arange(S, dtype=jnp.int32)
    causal = target_pos[:, None] >= target_pos[None, :]

    def self_row(items):
        query, keys, values, limit = items
        return attend(query, keys, values, causal & (target_pos[None, :] < limit))

    def cross_row(items):
        query, keys, values, limit = items
        valid = jnp.broadcast_to(source_pos[None, :] < limit, (L, S))
        return attend(query, keys, values, valid)

    def by_heads(value):
        return value.reshape(rows, value.shape[1], HEADS, HEAD)
    inputs_low = low(inputs)
    self_query = low_back(low(product(inputs_low, self_maps[0]) + attention_bias[0]))
    self_keys = low_back(low(product(inputs_low, self_maps[1])))
    self_values = low_back(low(product(inputs_low, self_maps[2]) + attention_bias[1]))
    self_mixed = lax.map(jax.checkpoint(self_row), (by_heads(self_query), by_heads(self_keys), by_heads(self_values), target_length))
    self_branch = low_back(product(self_mixed.reshape(rows, L, D), self_output) + attention_bias[2])
    first = normalize(inputs * residual_scale[0] + self_branch, norm_gain[0], norm_bias[0])
    first_low = low(first)
    cross_query = low_back(low(product(first_low, cross_maps[0]) + attention_bias[3]))
    cross_keys = low_back(low(product(source, cross_maps[1])))
    cross_values = low_back(low(product(source, cross_maps[2]) + attention_bias[4]))
    cross_mixed = lax.map(jax.checkpoint(cross_row), (by_heads(cross_query), by_heads(cross_keys), by_heads(cross_values), source_length))
    cross_branch = low_back(product(cross_mixed.reshape(rows, L, D), cross_output) + attention_bias[5])
    second = normalize(first * residual_scale[1] + cross_branch, norm_gain[1], norm_bias[1])
    hidden = low(jax.nn.gelu(low_back(product(low(second), expand_weight) + expand_bias), approximate=True))
    ffn_branch = low_back(product(hidden, shrink_weight) + shrink_bias)
    return normalize(second * residual_scale[2] + ffn_branch, norm_gain[2], norm_bias[2])

def reference(block_input, memory, memory_grad_rest, output_grad, target_length, source_length, self_maps, self_output, cross_maps, cross_output, attention_bias, expand_weight, expand_bias, shrink_weight, shrink_bias, norm_gain, norm_bias, residual_scale):
    rows = 2 * BH
    inputs = block_input.reshape(rows, L, D).astype(jnp.float32)
    source = memory.reshape(rows, S, D).astype(jnp.float32)
    targets = target_length.reshape(rows)
    sources = source_length.reshape(rows)
    weights = (self_maps, self_output, cross_maps, cross_output, attention_bias, expand_weight, expand_bias, shrink_weight, shrink_bias, norm_gain, norm_bias, residual_scale)
    weights = tuple((weight.astype(jnp.float32) for weight in weights))

    def closed(inputs, source, *weights):
        return forward(inputs, source, *weights, targets, sources)
    output, pullback = jax.vjp(closed, inputs, source, *weights)
    grads = pullback(output_grad.reshape(rows, L, D).astype(jnp.float32))
    return (output.reshape(2, BH, L, D), grads[0].reshape(2, BH, L, D), grads[1].reshape(2, BH, S, D) + memory_grad_rest, grads[2], grads[3], grads[4], grads[5], grads[6], grads[7], grads[8], grads[9], grads[10], grads[11], grads[12], grads[13])
```

```python
from functools import partial
import math

import jax
import jax.numpy as jnp
from jax import lax
from jax.experimental import pallas as pl
from jax.experimental.pallas import tpu as pltpu
from jax.sharding import PartitionSpec as P

HEADS = 8
HEAD = 64
GROUPS = 16
LANES = 128

eps = 1e-05
bfloat = jnp.bfloat16
single = jnp.float32
scale = HEAD ** (-0.5)
to_log2 = math.log2(math.e) * scale
far = -1.5e9

NN = (((1,), (0,)), ((), ()))
NT = (((1,), (1,)), ((), ()))
TN = (((0,), (0,)), ((), ()))

VM = pl.BlockSpec(memory_space=pltpu.VMEM)
SM = pl.BlockSpec(memory_space=pltpu.SMEM)
sds = jax.ShapeDtypeStruct


def dot(left, right, dims):
    return lax.dot_general(left, right, dims, preferred_element_type=single)


def low(value):
    return value.astype(bfloat)


def wide(value):
    return value.astype(single)


def split(value):
    high = low(value)
    return high, low(value - wide(high))


def split_three(value):
    high = low(value)
    rest = value - wide(high)
    middle = low(rest)
    return wide(high), wide(middle), wide(low(rest - wide(middle)))


def rows_of(rows, count=16):
    width = rows[0].shape[1]
    index = lax.broadcasted_iota(jnp.int32, (count, width), 0)
    out = jnp.zeros((count, width), single)
    for at, row in enumerate(rows):
        out = jnp.where(index == at, row, out)
    return out


def columns_of(rows):
    return rows_of(rows, -(-len(rows) // 8) * 8).T


def over_tokens(value):
    return jnp.sum(value, axis=1, keepdims=True)


def normalize(total):
    center = total - jnp.mean(total, axis=0, keepdims=True)
    spread = jnp.mean(center * center, axis=0, keepdims=True)
    scaled = lax.rsqrt(spread + eps)
    return center * scaled, scaled


def normalize_back(grad, normed, scaled, gain):
    inner = grad * gain
    back = scaled * (
        inner
        - jnp.mean(inner, axis=0, keepdims=True)
        - normed * jnp.mean(inner * normed, axis=0, keepdims=True)
    )
    return back, over_tokens(grad * normed), over_tokens(grad)


def put_columns(stats, items):
    lane = lax.broadcasted_iota(jnp.int32, stats.shape, 1)
    for at, column in items:
        stats = jnp.where(lane == at, column, stats)
    return stats


def pack(keep_ref, send_ref, held_ref, grad, at, me, pieces=1):
    held_ref[...] = low(grad)
    rows = grad.shape[0] // GROUPS // pieces
    width = grad.shape[1]
    for place in range(GROUPS):
        block = place // 8 + (place // 4 % 2) * 2 + (place % 4) * 4
        start = jnp.bitwise_xor(me, block) * (rows * pieces)
        out = send_ref if place >= 8 else keep_ref
        for piece in range(pieces):
            out[place % 8, :, at + piece * width : at + (piece + 1) * width] = held_ref[
                pl.ds(pl.multiple_of(start + piece * rows, rows), rows), :
            ]


def head_rows(head):
    return pl.ds(pl.multiple_of(head * HEAD, HEAD), HEAD)


def causal(scores, query_axis):
    key_pos = lax.broadcasted_iota(jnp.int32, scores.shape, 1 - query_axis)
    query_pos = lax.broadcasted_iota(jnp.int32, scores.shape, query_axis)
    return jnp.where(key_pos <= query_pos, scores, far)


def attend_forward(query_ref, keys_ref, values_ref, mask, block, is_causal, mixed_ref, totals_ref):
    span = query_ref.shape[1]
    keys_span = keys_ref.shape[1]

    def body(head, carry):
        rows = head_rows(head)
        query, keys, values = query_ref[rows], keys_ref[rows], values_ref[rows]
        ones = jnp.ones((1, span), single)
        high, rest = split(wide(query) * to_log2)
        query = jnp.concatenate([high, rest, low(rows_of([ones]))], axis=0)
        keys = jnp.concatenate([keys, keys, low(rows_of([mask]))], axis=0)
        values = jnp.concatenate([values, low(rows_of([jnp.ones((1, keys_span), single)]))], axis=0)
        for start in range(0, span, block):
            at = slice(start, start + block)
            end = start + block if is_causal else keys_span
            scores = dot(keys[:, :end], query[:, at], TN)
            if is_causal:
                diagonal = causal(scores[start:], 1)
                scores = jnp.concatenate([scores[:start], diagonal], axis=0) if start else diagonal
            top = jnp.max(scores, axis=0, keepdims=True)
            expo = low(jnp.exp2(scores - top))
            mixed = dot(values[:, :end], expo, NN)
            summed = mixed[HEAD : HEAD + 1]
            mixed_ref[rows, at] = low(mixed[:HEAD] / summed)
            totals_ref[pl.ds(head, 1), at] = top + jnp.log2(summed)
        return carry

    lax.fori_loop(0, HEADS, body, 0)


def attend_backward(
    query_ref, keys_ref, values_ref, mixed_ref, totals_ref, incoming_ref, mask, block, is_causal,
    query_grad_ref, keys_grad_ref, values_grad_ref,
):
    span = query_ref.shape[1]
    keys_span = keys_ref.shape[1]

    def body(head, carry):
        rows = head_rows(head)
        query, keys, values, incoming = (
            query_ref[rows], keys_ref[rows], values_ref[rows], incoming_ref[rows],
        )
        ones = jnp.ones((1, span), single)
        key_ones = jnp.ones((1, keys_span), single)
        delta = jnp.sum(wide(incoming) * wide(mixed_ref[rows]), axis=0, keepdims=True)
        high, rest = split(wide(query) * to_log2)
        totals = split_three(-totals_ref[pl.ds(head, 1), :])
        more_query = jnp.concatenate([high, rest, low(rows_of([*totals, ones]))], axis=0)
        more_keys = jnp.concatenate(
            [keys, keys, low(rows_of([key_ones, key_ones, key_ones, mask]))], axis=0
        )
        more_incoming = jnp.concatenate([incoming, low(rows_of(split_three(-delta)))], axis=0)
        more_values = jnp.concatenate(
            [values, low(rows_of([key_ones, key_ones, key_ones]))], axis=0
        )
        keys_grad = None
        values_grad = None
        for start in range(0, span, block):
            at = slice(start, start + block)
            end = start + block if is_causal else keys_span
            scores = dot(more_query[:, at], more_keys[:, :end], TN)
            if is_causal:
                diagonal = causal(scores[:, start:], 0)
                scores = (
                    jnp.concatenate([scores[:, :start], diagonal], axis=1) if start else diagonal
                )
            probs = jnp.exp2(scores)
            prob_grad = dot(more_incoming[:, at], more_values[:, :end], TN)
            score_grad = low(probs * prob_grad)
            value_part = dot(incoming[:, at], low(probs), NN)
            key_part = dot(query[:, at], score_grad, NN)
            if end < keys_span:
                blank = jnp.zeros((HEAD, keys_span - end), single)
                value_part = jnp.concatenate([value_part, blank], axis=1)
                key_part = jnp.concatenate([key_part, blank], axis=1)
            values_grad = value_part if values_grad is None else values_grad + value_part
            keys_grad = key_part if keys_grad is None else keys_grad + key_part
            query_grad_ref[rows, at] = low(dot(keys[:, :end], score_grad, NT) * scale)
        keys_grad_ref[rows] = low(keys_grad * scale)
        values_grad_ref[rows] = low(values_grad)
        return carry

    lax.fori_loop(0, HEADS, body, 0)


def gelu_parts(value):
    root = math.sqrt(2 / math.pi)
    square = value * value
    tanh = jnp.tanh(root * value * (1 + 0.044715 * square))
    half = 0.5 * (1 + tanh)
    slope = half + 0.5 * value * (1 - tanh * tanh) * (root * (1 + 3 * 0.044715 * square))
    return value * half, slope


def self_forward_kernel(
    limit_ref, input_ref, maps_ref, output_ref, bias_ref, omega_ref,
    input_t_ref, qkv_ref, mixed_ref, totals_ref, normed_ref, scaled_ref,
):
    columns = columns_of([bias_ref[0:1], bias_ref[1:2], bias_ref[2:3], omega_ref[0:1]])
    inputs = input_ref[0, 0].T
    input_t_ref[...] = inputs
    width, span = inputs.shape
    qkv_ref[0:width] = low(dot(maps_ref[0], inputs, TN) + columns[:, 0:1])
    qkv_ref[width : 2 * width] = low(dot(maps_ref[1], inputs, TN))
    qkv_ref[2 * width :] = low(dot(maps_ref[2], inputs, TN) + columns[:, 1:2])
    position = lax.broadcasted_iota(jnp.int32, (1, span), 1)
    mask = jnp.where(position < limit_ref[0, 0], 0.0, far)
    attend_forward(
        qkv_ref.at[0:width], qkv_ref.at[width : 2 * width], qkv_ref.at[2 * width :],
        mask, 512, True, mixed_ref, totals_ref,
    )
    branch = dot(output_ref[...], mixed_ref[...], TN) + columns[:, 2:3]
    normed, scaled = normalize(wide(inputs) * columns[:, 3:4] + branch)
    normed_ref[...] = normed
    scaled_ref[...] = scaled


def source_mask(limit, half, size):
    local = lax.broadcasted_iota(jnp.int32, (1, 2 * size), 1)
    own = local < size
    position = jnp.where(own, local + half * size, local - size + (1 - half) * size)
    return jnp.where(position < limit, 0.0, far)


def cross_forward_kernel(
    limit_ref, normed_ref, memory_ref, arrived_ref, maps_ref, output_ref, bias_ref,
    gain_ref, shift_ref, omega_ref,
    memory_t_ref, query_ref, keys_ref, values_ref, mixed_ref, totals_ref,
    second_normed_ref, second_scaled_ref,
):
    half = lax.axis_index("half")
    columns = columns_of(
        [bias_ref[3:4], bias_ref[4:5], bias_ref[5:6], gain_ref[0:1], shift_ref[0:1], omega_ref[1:2]]
    )
    size = memory_ref.shape[2]
    first = normed_ref[...] * columns[:, 3:4] + columns[:, 4:5]
    query_ref[...] = low(dot(maps_ref[0], low(first), TN) + columns[:, 0:1])
    memory_t_ref[:, :size] = memory_ref[half, 0].T
    memory_t_ref[:, size:] = arrived_ref[...].T
    keys_ref[...] = low(dot(maps_ref[1], memory_t_ref[...], TN))
    values_ref[...] = low(dot(maps_ref[2], memory_t_ref[...], TN) + columns[:, 1:2])
    mask = source_mask(limit_ref[0, 0], half, size)
    attend_forward(query_ref, keys_ref, values_ref, mask, 512, False, mixed_ref, totals_ref)
    branch = dot(output_ref[...], mixed_ref[...], TN) + columns[:, 2:3]
    second_normed, second_scaled = normalize(first * columns[:, 5:6] + branch)
    second_normed_ref[...] = second_normed
    second_scaled_ref[...] = second_scaled


def ffn_kernel(
    second_normed_ref, gain_ref, shift_ref, omega_ref, expand_ref, expand_bias_ref, shrink_ref,
    shrink_bias_ref, grad_ref,
    layer_ref, back_ref, stats_ref, keep_ref, send_ref,
    hidden_ref, slope_ref, held_ref, wide_held_ref,
    *, shift,
):
    me = lax.axis_index("batch") // (1 << shift)
    columns = columns_of(
        [gain_ref[1:2], gain_ref[2:3], shift_ref[1:2], shift_ref[2:3], omega_ref[2:3]]
        + [shrink_bias_ref[...]]
        + [expand_bias_ref[i : i + 1] for i in range(4)]
    )
    width, span = second_normed_ref.shape
    second = second_normed_ref[...] * columns[:, 0:1] + columns[:, 2:3]
    second_low = low(second)
    features = expand_ref.shape[1]
    chunk = 512
    ffn = None
    for at in range(0, features, chunk):
        part = slice(at, at + chunk)
        pre = dot(expand_ref[:, part], second_low, TN) + columns[:, 6 + at // chunk : 7 + at // chunk]
        value, slope = gelu_parts(pre)
        hidden_ref[part] = low(value)
        slope_ref[part] = low(slope)
        term = dot(shrink_ref[part], hidden_ref[part], TN)
        ffn = term if ffn is None else ffn + term
    third_normed, third_scaled = normalize(second * columns[:, 4:5] + (ffn + columns[:, 5:6]))
    layer_ref[0, 0] = (third_normed * columns[:, 1:2] + columns[:, 3:4]).T
    grad = wide(grad_ref[0, 0].T)
    third_grad, gain_third, shift_third = normalize_back(
        grad, third_normed, third_scaled, columns[:, 1:2]
    )
    scale_third = over_tokens(second * third_grad)
    ffn_low = low(third_grad)
    shrink_bias_grad = over_tokens(wide(ffn_low))
    second_grad = third_grad * columns[:, 4:5]
    sums = []
    for at in range(0, features, chunk):
        part = slice(at, at + chunk)
        wide_held_ref[part] = low(dot(hidden_ref[part], ffn_low, NT))
        pre_grad = low(dot(shrink_ref[part], ffn_low, NN) * wide(slope_ref[part]))
        sums.append(over_tokens(wide(pre_grad)))
        held_ref[:, part] = low(dot(second_low, pre_grad, NT))
        second_grad = second_grad + dot(expand_ref[:, part], pre_grad, NN)
    back_ref[...] = second_grad
    rows = features // GROUPS // 4
    for place in range(GROUPS):
        block = place // 8 + (place // 4 % 2) * 2 + (place % 4) * 4
        group = jnp.bitwise_xor(me, block)
        out = send_ref if place >= 8 else keep_ref
        start = pl.multiple_of(group * rows, rows)
        out[place % 8, :, :features] = held_ref[pl.ds(start, rows), :]
        for piece in range(4):
            start = pl.multiple_of(group * (4 * rows) + piece * rows, rows)
            lanes = slice(features + piece * width, features + (piece + 1) * width)
            out[place % 8, :, lanes] = wide_held_ref[pl.ds(start, rows), :]
    expand_sums = jnp.concatenate(sums, axis=0)
    pieces = [
        jnp.concatenate(
            [
                expand_sums[(4 * group + piece) * rows : (4 * group + piece + 1) * rows]
                for group in range(GROUPS)
            ],
            axis=0,
        )
        for piece in range(4)
    ]
    stats_ref[...] = put_columns(
        jnp.zeros(stats_ref.shape, single),
        [(8, gain_third), (11, shift_third), (14, scale_third), (15, shrink_bias_grad)]
        + [(16 + piece, pieces[piece]) for piece in range(4)],
    )


def cross_back_kernel(
    limit_ref, normed_ref, second_normed_ref, second_scaled_ref, back_ref, memory_t_ref,
    query_ref, keys_ref, values_ref, mixed_ref, totals_ref, maps_ref, output_ref,
    gain_ref, shift_ref, omega_ref, stats_in_ref,
    first_grad_ref, own_ref, away_ref, stats_ref, keep_ref, send_ref,
    incoming_ref, query_grad_ref, keys_grad_ref, values_grad_ref, held_ref,
    *, shift,
):
    half = lax.axis_index("half")
    me = lax.axis_index("batch") // (1 << shift)
    columns = columns_of(
        [gain_ref[0:1], shift_ref[0:1], gain_ref[1:2], omega_ref[1:2]]
    )
    size = own_ref.shape[1]
    width = normed_ref.shape[0]
    first = normed_ref[...] * columns[:, 0:1] + columns[:, 1:2]
    first_low = low(first)
    sum_grad, gain_second, shift_second = normalize_back(
        back_ref[...], second_normed_ref[...], second_scaled_ref[...], columns[:, 2:3]
    )
    scale_second = over_tokens(first * sum_grad)
    cross_low = low(sum_grad)
    out_bias = over_tokens(wide(cross_low))
    pack(keep_ref, send_ref, held_ref, dot(mixed_ref[...], cross_low, NT), 3 * width, me)
    incoming_ref[...] = low(dot(output_ref[...], cross_low, NN))
    mask = source_mask(limit_ref[0, 0], half, size)
    attend_backward(
        query_ref, keys_ref, values_ref, mixed_ref, totals_ref, incoming_ref, mask, 512, False,
        query_grad_ref, keys_grad_ref, values_grad_ref,
    )
    query_grad, keys_grad, values_grad = query_grad_ref[...], keys_grad_ref[...], values_grad_ref[...]
    first_grad_ref[...] = sum_grad * columns[:, 3:4] + dot(maps_ref[0], query_grad, NN)
    memory_grad = dot(maps_ref[1], keys_grad, NN) + dot(maps_ref[2], values_grad, NN)
    own_ref[...] = memory_grad[:, :size]
    away_ref[...] = low(memory_grad[:, size:])
    pack(keep_ref, send_ref, held_ref, dot(first_low, query_grad, NT), 0, me)
    pack(keep_ref, send_ref, held_ref, dot(memory_t_ref[...], keys_grad, NT), width, me)
    pack(keep_ref, send_ref, held_ref, dot(memory_t_ref[...], values_grad, NT), 2 * width, me)
    stats_ref[...] = put_columns(
        stats_in_ref[...],
        [
            (3, over_tokens(wide(query_grad))), (4, over_tokens(wide(values_grad))), (5, out_bias),
            (7, gain_second), (10, shift_second), (13, scale_second),
        ],
    )


def self_back_kernel(
    limit_ref, input_t_ref, normed_ref, scaled_ref, first_grad_ref, qkv_ref, mixed_ref, totals_ref,
    maps_ref, output_ref, gain_ref, omega_ref, stats_in_ref,
    input_grad_ref, keep_ref, send_ref,
    incoming_ref, query_grad_ref, keys_grad_ref, values_grad_ref, held_ref, held_stats_ref,
    *, shift,
):
    me = lax.axis_index("batch") // (1 << shift)
    columns = columns_of([gain_ref[0:1], omega_ref[0:1]])
    width, span = input_t_ref.shape
    inputs = input_t_ref[...]
    sum_grad, gain_first, shift_first = normalize_back(
        first_grad_ref[...], normed_ref[...], scaled_ref[...], columns[:, 0:1]
    )
    scale_first = over_tokens(wide(inputs) * sum_grad)
    self_low = low(sum_grad)
    out_bias = over_tokens(wide(self_low))
    pack(keep_ref, send_ref, held_ref, dot(mixed_ref[...], self_low, NT), 3 * width, me)
    incoming_ref[...] = low(dot(output_ref[...], self_low, NN))
    position = lax.broadcasted_iota(jnp.int32, (1, span), 1)
    mask = jnp.where(position < limit_ref[0, 0], 0.0, far)
    attend_backward(
        qkv_ref.at[0:width], qkv_ref.at[width : 2 * width], qkv_ref.at[2 * width :],
        mixed_ref, totals_ref, incoming_ref, mask, 512, True,
        query_grad_ref, keys_grad_ref, values_grad_ref,
    )
    query_grad, keys_grad, values_grad = query_grad_ref[...], keys_grad_ref[...], values_grad_ref[...]
    pack(keep_ref, send_ref, held_ref, dot(inputs, query_grad, NT), 0, me)
    pack(keep_ref, send_ref, held_ref, dot(inputs, keys_grad, NT), width, me)
    pack(keep_ref, send_ref, held_ref, dot(inputs, values_grad, NT), 2 * width, me)
    stats = put_columns(
        stats_in_ref[...],
        [
            (0, over_tokens(wide(query_grad))), (1, over_tokens(wide(values_grad))), (2, out_bias),
            (6, gain_first), (9, shift_first), (12, scale_first),
        ],
    )
    pack(keep_ref, send_ref, held_stats_ref, stats, 4 * width, me)
    input_grad_ref[0, 0] = (
        sum_grad * columns[:, 1:2]
        + dot(maps_ref[0], query_grad, NN)
        + dot(maps_ref[1], keys_grad, NN)
        + dot(maps_ref[2], values_grad, NN)
    ).T


def memory_kernel(own_ref, returned_ref, rest_ref, out_ref):
    half = lax.axis_index("half")
    out_ref[half, 0] = own_ref[...].T + rest_ref[half, 0]
    out_ref[1 - half, 0] = wide(returned_ref[...]).T + rest_ref[1 - half, 0]


def finish(ffn, cross, own, width):
    features = ffn.shape[1] // 2
    maps = [own[:, i * width : (i + 1) * width] for i in range(3)]
    cross_maps = [cross[:, i * width : (i + 1) * width] for i in range(3)]
    shrink = jnp.concatenate(
        [ffn[:, features + i * width : features + (i + 1) * width] for i in range(4)], axis=0
    )
    stats = own[:, 4 * width :].T
    rows = ffn.shape[0]
    return (
        maps, own[:, 3 * width : 4 * width], cross_maps, cross[:, 3 * width :],
        stats[0:6], ffn[:, :features], [stats[16 + i : 17 + i] for i in range(4)], shrink,
        stats[15:16], stats[6:9], stats[9:12], stats[12:15],
    )


def finish_kernel(ffn_ref, ffn_in_ref, cross_ref, cross_in_ref, own_ref, own_in_ref, *outs):
    def summed(ref, other):
        return wide(ref[...]) + wide(other[...])

    width = outs[1].shape[1]
    values = finish(
        summed(ffn_ref, ffn_in_ref), summed(cross_ref, cross_in_ref), summed(own_ref, own_in_ref), width
    )
    for ref, value in zip(outs, values):
        if isinstance(value, list):
            for at, item in enumerate(value):
                ref[at] = item.reshape(ref.shape[1:])
        else:
            ref[...] = value


def call(kernel, name, outs, scratch=(), specs=None, flops=0, **options):
    return lambda *args: pl.pallas_call(
        partial(kernel, **options) if options else kernel,
        name=name,
        out_shape=outs,
        in_specs=specs or [VM] * len(args),
        out_specs=jax.tree.map(lambda _: VM, outs),
        scratch_shapes=scratch,
        compiler_params=pltpu.CompilerParams(vmem_limit_bytes=56 * 1024 * 1024),
        cost_estimate=pl.CostEstimate(flops=flops, bytes_accessed=10_000_000, transcendentals=0),
    )(*args)


def shards(
    block_input, memory, memory_grad_rest, output_grad, target_length, source_length,
    self_maps, self_output, cross_maps, cross_output, attention_bias,
    expand_weight, expand_bias, shrink_weight, shrink_bias, norm_gain, norm_bias, residual_scale,
    *, devices,
):
    span, width = block_input.shape[2:]
    size = memory.shape[2]
    source = 2 * size
    features = expand_weight.shape[1]
    shift = int(math.log2(devices // GROUPS))
    assert GROUPS << shift == devices
    rows = width // GROUPS
    half = lax.axis_index("half")
    me = lax.axis_index("batch")

    def swap_half(value):
        return lax.ppermute(value, "half", [(0, 1), (1, 0)])

    def swap(value, bits):
        return lax.ppermute(value, "batch", [(i, i ^ bits) for i in range(devices)])

    def add(*values):
        return low(sum(wide(value) for value in values))

    def reduced(keep, send):
        total = add(keep, swap(send, 1 << shift))
        total = add(total[:4], swap(total[4:], 2 << shift))
        total = add(
            total[0],
            swap(total[1], 4 << shift), swap(total[2], 8 << shift), swap(total[3], 12 << shift),
        )
        for bit in reversed(range(shift)):
            part = total.shape[0] // 2
            mine = (me >> bit) & 1
            sent = lax.dynamic_slice_in_dim(total, (1 - mine) * part, part, 0)
            total = add(lax.dynamic_slice_in_dim(total, mine * part, part, 0), swap(sent, 1 << bit))
        return total, swap_half(total)

    arrived = swap_half(lax.dynamic_index_in_dim(memory, 1 - half, 0, keepdims=False)[0])
    tall = sds((width, span), bfloat)
    packet = lambda lanes: [sds((GROUPS // 2, rows, lanes), bfloat)] * 2
    input_t, qkv, mixed, totals, normed, scaled = call(
        self_forward_kernel, "self_forward",
        [tall, sds((3 * width, span), bfloat), tall, sds((HEADS, span), single),
         sds((width, span), single), sds((1, span), single)],
        specs=[SM] + [VM] * 5, flops=10_000_000_000,
    )(target_length, block_input, self_maps, self_output, attention_bias, residual_scale)
    source_tall = sds((width, source), bfloat)
    (
        memory_t, query, keys, values, cross_mixed, cross_totals, second_normed, second_scaled,
    ) = call(
        cross_forward_kernel, "cross_forward",
        [source_tall, tall, source_tall, source_tall, tall, sds((HEADS, span), single),
         sds((width, span), single), sds((1, span), single)],
        specs=[SM] + [VM] * 9, flops=10_000_000_000,
    )(
        source_length, normed, memory, arrived, cross_maps, cross_output, attention_bias,
        norm_gain, norm_bias, residual_scale,
    )
    layer_output, second_grad, stats, ffn_keep, ffn_send = call(
        ffn_kernel, "ffn",
        [sds((1, 1, span, width), single), sds((width, span), single), sds((width, LANES), single)]
        + packet(2 * features),
        scratch=[pltpu.VMEM((features, span), bfloat)] * 2
        + [pltpu.VMEM((width, features), bfloat), pltpu.VMEM((features, width), bfloat)],
        flops=20_000_000_000, shift=shift,
    )(
        second_normed, norm_gain, norm_bias, residual_scale, expand_weight,
        expand_bias.reshape(4, -1), shrink_weight, shrink_bias.reshape(1, -1), output_grad,
    )
    grads = [pltpu.VMEM((width, span), bfloat)] * 2 + [pltpu.VMEM((width, source), bfloat)] * 2
    first_grad, own, away, stats, cross_keep, cross_send = call(
        cross_back_kernel, "cross_back",
        [sds((width, span), single), sds((width, size), single), sds((width, size), bfloat),
         sds((width, LANES), single)] + packet(4 * width),
        scratch=grads + [pltpu.VMEM((width, width), bfloat)],
        specs=[SM] + [VM] * 16, flops=20_000_000_000, shift=shift,
    )(
        source_length, normed, second_normed, second_scaled, second_grad, memory_t,
        query, keys, values, cross_mixed, cross_totals, cross_maps, cross_output,
        norm_gain, norm_bias, residual_scale, stats,
    )
    returned = swap_half(away)
    input_grad, self_keep, self_send = call(
        self_back_kernel, "self_back",
        [sds((1, 1, span, width), single)] + packet(4 * width + LANES),
        scratch=grads + [pltpu.VMEM((width, width), bfloat), pltpu.VMEM((width, LANES), bfloat)],
        specs=[SM] + [VM] * 12, flops=20_000_000_000, shift=shift,
    )(
        target_length, input_t, normed, scaled, first_grad, qkv, mixed, totals,
        self_maps, self_output, norm_gain, residual_scale, stats,
    )
    memory_grad = call(memory_kernel, "memory_grad", sds(memory_grad_rest.shape, single))(
        own, returned, memory_grad_rest
    )
    if shift:
        def regroup(value, start, stop):
            lanes = (stop - start) // 4
            part = value[..., start:stop].reshape(-1, rows, 4, lanes).swapaxes(1, 2)
            part = part.reshape(-1, 1 << shift, 4, rows >> shift, lanes).swapaxes(2, 3)
            part = part.reshape(value.shape[0], rows, stop - start)
            return jnp.concatenate([value[..., :start], part, value[..., stop:]], axis=-1)

        ffn_keep, ffn_send = (regroup(v, features, 2 * features) for v in (ffn_keep, ffn_send))
        start = 4 * width + 16
        self_keep, self_send = (regroup(v, start, start + 4) for v in (self_keep, self_send))
    parts = (
        *reduced(ffn_keep, ffn_send), *reduced(cross_keep, cross_send), *reduced(self_keep, self_send),
    )
    mine = rows >> shift
    outs = [
        sds((3, mine, width), single), sds((mine, width), single), sds((3, mine, width), single),
        sds((mine, width), single), sds((6, mine), single), sds((mine, features), single),
        sds((4, mine), single), sds((4 * mine, width), single), sds((1, mine), single),
        sds((3, mine), single), sds((3, mine), single), sds((3, mine), single),
    ]
    done = list(call(finish_kernel, "finish", outs)(*parts))
    done[6] = done[6].reshape(-1)
    done[8] = done[8].reshape(-1)
    return (layer_output, input_grad, memory_grad, *done)


def solution(mesh):
    rows = P("half", "batch", None, None)
    sources = P(None, "batch", "half", None)
    placed = (rows, sources, sources, rows, P("half", "batch"), P("half", "batch")) + (P(),) * 12
    return jax.shard_map(
        partial(shards, devices=mesh.shape["batch"]),
        mesh=mesh,
        in_specs=placed,
        out_specs=(
            rows, rows, sources,
            P(None, "batch", None), P("batch", None), P(None, "batch", None), P("batch", None),
            P(None, "batch"), P("batch", None), P("batch"), P("batch", None), P("batch"),
            P(None, "batch"), P(None, "batch"), P(None, "batch"),
        ),
        check_vma=False,
    )
```

```python
from functools import partial
import math

import jax
import jax.numpy as jnp
from jax import lax
from jax.experimental import pallas as pl
from jax.experimental.pallas import tpu as pltpu
from jax.sharding import PartitionSpec as P

HEADS = 8
HEAD = 64
GROUPS = 16
LANES = 128
QUERY_BLOCK = 512
KEY_BLOCK = 256
ROW_BLOCK = 256
MICROSECOND = 1_000

eps = 1e-05
bfloat = jnp.bfloat16
single = jnp.float32
scale = HEAD ** (-0.5)
to_log2 = math.log2(math.e) * scale
far = -1.5e9

NN = (((1,), (0,)), ((), ()))
NT = (((1,), (1,)), ((), ()))
TN = (((0,), (0,)), ((), ()))

VM = pl.BlockSpec(memory_space=pltpu.VMEM)
SM = pl.BlockSpec(memory_space=pltpu.SMEM)
sds = jax.ShapeDtypeStruct


def dot(left, right, dims):
    return lax.dot_general(left, right, dims, preferred_element_type=single)


def low(value):
    return value.astype(bfloat)


def wide(value):
    return value.astype(single)


def split(value):
    high = low(value)
    return high, low(value - wide(high))


def split_three(value):
    high = low(value)
    rest = value - wide(high)
    middle = low(rest)
    return wide(high), wide(middle), wide(low(rest - wide(middle)))


def rows_of(rows, count=16):
    width = rows[0].shape[1]
    index = lax.broadcasted_iota(jnp.int32, (count, width), 0)
    out = jnp.zeros((count, width), single)
    for at, row in enumerate(rows):
        out = jnp.where(index == at, row, out)
    return out


def columns_of(rows):
    return rows_of(rows, -(-len(rows) // 8) * 8).T


def over_tokens(value):
    return jnp.sum(value, axis=1, keepdims=True)


def normalize(total):
    center = total - jnp.mean(total, axis=0, keepdims=True)
    spread = jnp.mean(center * center, axis=0, keepdims=True)
    scaled = lax.rsqrt(spread + eps)
    return center * scaled, scaled


def normalize_back(grad, normed, scaled, gain):
    inner = grad * gain
    back = scaled * (
        inner
        - jnp.mean(inner, axis=0, keepdims=True)
        - normed * jnp.mean(inner * normed, axis=0, keepdims=True)
    )
    return back, over_tokens(grad * normed), over_tokens(grad)


def put_columns(stats, items):
    lane = lax.broadcasted_iota(jnp.int32, stats.shape, 1)
    for at, column in items:
        stats = jnp.where(lane == at, column, stats)
    return stats


def places(me, half):
    for core in range(2):
        for near in range(2):
            for far_off in range(4):
                bits = core + 2 * near + 4 * (far_off // 2) + 8 * (far_off % 2)
                group = jnp.bitwise_xor(me, bits)
                if half is None:
                    yield core, (near, far_off), group, 0
                else:
                    for across in range(2):
                        yield core, (across, near, far_off), group, jnp.bitwise_xor(half, across)


def pack(keep_ref, send_ref, held_ref, grad, at, me, half):
    held_ref[:, : grad.shape[1]] = low(grad)
    rows = grad.shape[0] // GROUPS
    part = rows if half is None else rows // 2
    lanes = slice(at, at + grad.shape[1])
    for core, place, group, portion in places(me, half):
        start = pl.multiple_of(group * rows + portion * part, part)
        (send_ref if core else keep_ref)[(*place, slice(None), lanes)] = held_ref[
            pl.ds(start, part), : grad.shape[1]
        ]


def ranks(shift):
    return (0, 0) if shift else (lax.axis_index("batch"), lax.axis_index("half"))


def head_rows(head):
    return pl.ds(pl.multiple_of(head * HEAD, HEAD), HEAD)


def hide_later(scores, offset, query_axis):
    key_pos = lax.broadcasted_iota(jnp.int32, scores.shape, 1 - query_axis) + offset
    query_pos = lax.broadcasted_iota(jnp.int32, scores.shape, query_axis)
    return jnp.where(key_pos <= query_pos, scores, far)


def forward_scratch(span):
    return [
        pltpu.VMEM((2, span, QUERY_BLOCK), single),
        pltpu.VMEM((8, QUERY_BLOCK), single),
        pltpu.VMEM((2, 2 * HEAD + 16, span), bfloat),
        pltpu.VMEM((2, span, 2 * HEAD + 16), bfloat),
        pltpu.VMEM((3, HEAD + 16, span), bfloat),
    ]


def attend_forward(query_ref, keys_ref, values_ref, mask, is_causal, mixed_ref, totals_ref, scratch):
    scores_ref, top_ref, more_query_ref, more_keys_ref, more_values_ref = scratch
    span = query_ref.shape[1]
    blocks = span // QUERY_BLOCK
    ones = low(rows_of([jnp.ones((1, span), single)]))
    more_query_ref[0, 2 * HEAD :] = ones
    more_query_ref[1, 2 * HEAD :] = ones
    mask_column = low(rows_of([mask])).T
    more_keys_ref[0, :, 2 * HEAD :] = mask_column
    more_keys_ref[1, :, 2 * HEAD :] = mask_column
    for slot in range(3):
        more_values_ref[slot, HEAD:] = ones

    def key_blocks(block):
        return range(0, (block + 1) * QUERY_BLOCK if is_causal else span, KEY_BLOCK)

    def prepare(head, slot):
        rows = head_rows(head)
        high, rest = split(wide(query_ref[rows]) * to_log2)
        more_query_ref[slot, :HEAD] = high
        more_query_ref[slot, HEAD : 2 * HEAD] = rest
        keys = keys_ref[rows]
        more_keys_ref[slot, :, : 2 * HEAD] = jnp.concatenate([keys, keys], axis=0).T
        more_values_ref[lax.rem(head, 3), :HEAD] = values_ref[rows]

    def score(slot, block, key, top):
        at = slice(block * QUERY_BLOCK, (block + 1) * QUERY_BLOCK)
        scores = dot(more_keys_ref[slot, key : key + KEY_BLOCK], more_query_ref[slot, :, at], NN)
        if is_causal and key + KEY_BLOCK > block * QUERY_BLOCK:
            scores = hide_later(scores, key - block * QUERY_BLOCK, 1)
        scores_ref[block % 2, key : key + KEY_BLOCK] = scores
        part = jnp.max(scores.reshape(KEY_BLOCK // 8, 8, QUERY_BLOCK), axis=0)
        return part if top is None else jnp.maximum(top, part)

    def mix(head, block, key, top, total):
        expo = low(jnp.exp2(scores_ref[block % 2, key : key + KEY_BLOCK] - top))
        part = dot(more_values_ref[lax.rem(head, 3), :, key : key + KEY_BLOCK], expo, NN)
        return part if total is None else total + part

    def finish_block(head, block, top, total):
        at = slice(block * QUERY_BLOCK, (block + 1) * QUERY_BLOCK)
        summed = total[HEAD : HEAD + 1]
        mixed_ref[head_rows(head), at] = low(total[:HEAD] / summed)
        totals_ref[pl.ds(head, 1), at] = top + jnp.log2(summed)

    prepare(0, 0)
    last = blocks - 1

    def body(pair, carry):
        for odd in range(2):
            head = 2 * pair + odd
            for block in range(blocks):
                before, block_before = (head, block - 1) if block else (jnp.maximum(head - 1, 0), last)
                top_before = top_ref[block_before % 2 : block_before % 2 + 1]
                top = None
                total = None
                now, then = list(key_blocks(block)), list(key_blocks(block_before))
                for step in range(max(len(now), len(then))):
                    if step < len(now):
                        top = score(odd, block, now[step], top)
                    if step < len(then):
                        total = mix(before, block_before, then[step], top_before, total)
                top_ref[block % 2 : block % 2 + 1] = jnp.max(top, axis=0, keepdims=True)
                finish_block(before, block_before, top_before, total)
                if block == 0:
                    prepare(jnp.minimum(head + 1, HEADS - 1), 1 - odd)
        return carry

    lax.fori_loop(0, HEADS // 2, body, 0)
    top = top_ref[last % 2 : last % 2 + 1]
    total = None
    for key in key_blocks(last):
        total = mix(HEADS - 1, last, key, top, total)
    finish_block(HEADS - 1, last, top, total)


def backward_scratch(span):
    return (
        [pltpu.VMEM((2, span, KEY_BLOCK), bfloat)] * 2
        + [pltpu.VMEM((2, span, HEAD + 16), bfloat)] * 2
        + [pltpu.VMEM((2, HEAD + 16, span), bfloat)] * 2
        + [pltpu.VMEM((HEAD, span), single)]
    )


def attend_backward(
    query_ref, keys_ref, values_ref, mixed_ref, totals_ref, incoming_ref, mask, is_causal,
    query_grad_ref, keys_grad_ref, values_grad_ref, first_head, last_head, scratch,
):
    probs_ref, score_grads_ref, more_query_ref, more_incoming_ref, more_keys_ref, more_values_ref, held_ref = scratch
    span = query_ref.shape[1]
    blocks = span // KEY_BLOCK
    ones = jnp.ones((1, span), single)
    for slot in range(2):
        more_keys_ref[slot, HEAD:] = low(rows_of([ones, ones, ones, mask]))
        more_values_ref[slot, HEAD:] = low(rows_of([ones, ones, ones]))

    def first_query(block):
        return block * KEY_BLOCK if is_causal else 0

    def prepare(head, slot):
        rows = head_rows(head)
        query, incoming = query_ref[rows], incoming_ref[rows]
        delta = jnp.sum(wide(incoming) * wide(mixed_ref[rows]), axis=0, keepdims=True)
        totals = split_three(totals_ref[pl.ds(head, 1), :] * (-1 / to_log2))
        more_query_ref[slot] = jnp.concatenate([query, low(rows_of([*totals, ones]))], axis=0).T
        more_incoming_ref[slot] = jnp.concatenate(
            [incoming, low(rows_of(split_three(-delta)))], axis=0
        ).T
        more_keys_ref[slot, :HEAD] = keys_ref[rows]
        more_values_ref[slot, :HEAD] = values_ref[rows]

    def score(slot, block, start):
        keys, rows = slice(block * KEY_BLOCK, (block + 1) * KEY_BLOCK), slice(start, start + ROW_BLOCK)
        scores = dot(more_query_ref[slot, rows], more_keys_ref[slot, :, keys], NN)
        if is_causal and start < (block + 1) * KEY_BLOCK:
            scores = hide_later(scores, block * KEY_BLOCK - start, 0)
        probs = jnp.exp2(scores * to_log2)
        prob_grad = dot(more_incoming_ref[slot, rows], more_values_ref[slot, :, keys], NN)
        probs_ref[block % 2, rows] = low(probs)
        score_grads_ref[block % 2, rows] = low(probs * prob_grad)

    def products(head, block):
        rows, keys = head_rows(head), slice(block * KEY_BLOCK, (block + 1) * KEY_BLOCK)
        start = first_query(block)

        def values_part():
            values_grad_ref[rows, keys] = low(
                dot(incoming_ref[rows, start:], probs_ref[block % 2, start:], NN)
            )

        def keys_part():
            keys_grad_ref[rows, keys] = low(
                dot(query_ref[rows, start:], score_grads_ref[block % 2, start:], NN) * scale
            )

        def query_part(at):
            stop = min(at + 2 * ROW_BLOCK, span)
            part = dot(keys_ref[rows, keys], score_grads_ref[block % 2, at:stop], NT)
            if block:
                part = part + held_ref[:, at:stop]
            held_ref[:, at:stop] = part

        def query_whole():
            query_grad_ref[rows] = low(held_ref[...] * scale)

        steps = [values_part, keys_part]
        steps += [partial(query_part, at) for at in range(start, span, 2 * ROW_BLOCK)]
        return steps + [query_whole] * (block == blocks - 1)

    prepare(first_head, 0)

    def body(pair, carry):
        for odd in range(2):
            head = first_head + 2 * pair + odd
            for block in range(blocks):
                if block:
                    steps = products(head, block - 1)
                else:
                    steps = products(jnp.maximum(head - 1, first_head), blocks - 1)
                starts = range(first_query(block), span, ROW_BLOCK)
                for step in range(max(len(starts), len(steps))):
                    if step < len(starts):
                        score(odd, block, starts[step])
                    if step < len(steps):
                        steps[step]()
                if block == 0:
                    prepare(jnp.minimum(head + 1, last_head - 1), 1 - odd)
        return carry

    lax.fori_loop(0, (last_head - first_head) // 2, body, 0)
    for step in products(last_head - 1, blocks - 1):
        step()


def gelu_parts(value):
    root = math.sqrt(2 / math.pi)
    square = value * value
    tanh = jnp.tanh(root * value * (1 + 0.044715 * square))
    half = 0.5 * (1 + tanh)
    slope = half + 0.5 * value * (1 - tanh * tanh) * (root * (1 + 3 * 0.044715 * square))
    return value * half, slope


def projection_kernel(input_ref, maps_ref, bias_ref, input_t_ref, qkv_ref):
    columns = columns_of([bias_ref[0:1], bias_ref[1:2]])
    inputs = input_ref[0, 0].T
    input_t_ref[...] = inputs
    width = inputs.shape[0]
    qkv_ref[0:width] = low(dot(maps_ref[0], inputs, TN) + columns[:, 0:1])
    qkv_ref[width : 2 * width] = low(dot(maps_ref[1], inputs, TN))
    qkv_ref[2 * width :] = low(dot(maps_ref[2], inputs, TN) + columns[:, 1:2])


def self_forward_kernel(
    limit_ref, input_t_ref, qkv_ref, output_ref, bias_ref, omega_ref,
    mixed_ref, totals_ref, normed_ref, scaled_ref, *scratch,
):
    columns = columns_of([bias_ref[2:3], omega_ref[0:1]])
    width, span = input_t_ref.shape
    position = lax.broadcasted_iota(jnp.int32, (1, span), 1)
    mask = jnp.where(position < limit_ref[0, 0], 0.0, far)
    attend_forward(
        qkv_ref.at[0:width], qkv_ref.at[width : 2 * width], qkv_ref.at[2 * width :],
        mask, True, mixed_ref, totals_ref, scratch,
    )
    branch = dot(output_ref[...], mixed_ref[...], TN) + columns[:, 0:1]
    normed, scaled = normalize(wide(input_t_ref[...]) * columns[:, 1:2] + branch)
    normed_ref[...] = normed
    scaled_ref[...] = scaled


def source_mask(limit, half, size):
    local = lax.broadcasted_iota(jnp.int32, (1, 2 * size), 1)
    own = local < size
    position = jnp.where(own, local + half * size, local - size + (1 - half) * size)
    return jnp.where(position < limit, 0.0, far)


def cross_forward_kernel(
    limit_ref, normed_ref, memory_ref, arrived_ref, maps_ref, output_ref, bias_ref,
    gain_ref, shift_ref, omega_ref,
    memory_t_ref, query_ref, keys_ref, values_ref, mixed_ref, totals_ref,
    second_normed_ref, second_scaled_ref, *scratch,
):
    half = lax.axis_index("half")
    columns = columns_of(
        [bias_ref[3:4], bias_ref[4:5], bias_ref[5:6], gain_ref[0:1], shift_ref[0:1], omega_ref[1:2]]
    )
    size = memory_ref.shape[2]
    first = normed_ref[...] * columns[:, 3:4] + columns[:, 4:5]
    query_ref[...] = low(dot(maps_ref[0], low(first), TN) + columns[:, 0:1])
    memory_t_ref[:, :size] = memory_ref[half, 0].T
    memory_t_ref[:, size:] = arrived_ref[...].T
    keys_ref[...] = low(dot(maps_ref[1], memory_t_ref[...], TN))
    values_ref[...] = low(dot(maps_ref[2], memory_t_ref[...], TN) + columns[:, 1:2])
    mask = source_mask(limit_ref[0, 0], half, size)
    attend_forward(query_ref, keys_ref, values_ref, mask, False, mixed_ref, totals_ref, scratch)
    branch = dot(output_ref[...], mixed_ref[...], TN) + columns[:, 2:3]
    second_normed, second_scaled = normalize(first * columns[:, 5:6] + branch)
    second_normed_ref[...] = second_normed
    second_scaled_ref[...] = second_scaled


def ffn_kernel(
    second_normed_ref, gain_ref, shift_ref, omega_ref, expand_ref, expand_bias_ref, shrink_ref,
    shrink_bias_ref, grad_ref,
    layer_ref, back_ref, stats_ref, keep_ref, send_ref,
    hidden_ref, slope_ref, held_ref, wide_held_ref,
    *, shift,
):
    me, half = ranks(shift)
    columns = columns_of(
        [gain_ref[1:2], gain_ref[2:3], shift_ref[1:2], shift_ref[2:3], omega_ref[2:3]]
        + [shrink_bias_ref[...].reshape(1, -1)]
        + [expand_bias_ref[i : i + 512].reshape(1, -1) for i in range(0, expand_ref.shape[1], 512)]
    )
    width, span = second_normed_ref.shape
    second = second_normed_ref[...] * columns[:, 0:1] + columns[:, 2:3]
    second_low = low(second)
    features = expand_ref.shape[1]
    chunk = 512
    ffn = None
    for at in range(0, features, chunk):
        part = slice(at, at + chunk)
        pre = dot(expand_ref[:, part], second_low, TN) + columns[:, 6 + at // chunk : 7 + at // chunk]
        value, slope = gelu_parts(pre)
        hidden_ref[part] = low(value)
        slope_ref[part] = low(slope)
        term = dot(shrink_ref[part], hidden_ref[part], TN)
        ffn = term if ffn is None else ffn + term
    third_normed, third_scaled = normalize(second * columns[:, 4:5] + (ffn + columns[:, 5:6]))
    layer_ref[0, 0] = (third_normed * columns[:, 1:2] + columns[:, 3:4]).T
    grad = wide(grad_ref[0, 0].T)
    third_grad, gain_third, shift_third = normalize_back(
        grad, third_normed, third_scaled, columns[:, 1:2]
    )
    scale_third = over_tokens(second * third_grad)
    ffn_low = low(third_grad)
    shrink_bias_grad = over_tokens(wide(ffn_low))
    second_grad = third_grad * columns[:, 4:5]
    sums = []
    for at in range(0, features, chunk):
        part = slice(at, at + chunk)
        wide_held_ref[part] = low(dot(hidden_ref[part], ffn_low, NT))
        pre_grad = low(dot(shrink_ref[part], ffn_low, NN) * wide(slope_ref[part]))
        sums.append(over_tokens(wide(pre_grad)))
        held_ref[:, part] = low(dot(second_low, pre_grad, NT))
        second_grad = second_grad + dot(expand_ref[:, part], pre_grad, NN)
    back_ref[...] = second_grad
    rows = features // GROUPS // 4
    for core, place, group, portion in places(me, half):
        out = send_ref if core else keep_ref
        start = pl.multiple_of(group * rows + portion * (rows // 2), rows // 2)
        out[(*place, slice(None), slice(0, features))] = held_ref[pl.ds(start, rows // 2), :]
        for piece in range(4):
            start = (4 * group + piece) * rows + portion * (rows // 2)
            lanes = slice(features + piece * width, features + (piece + 1) * width)
            out[(*place, slice(None), lanes)] = wide_held_ref[
                pl.ds(pl.multiple_of(start, rows // 2), rows // 2), :
            ]
    expand_sums = jnp.concatenate(sums, axis=0)
    pieces = [
        jnp.concatenate(
            [
                expand_sums[(4 * group + piece) * rows : (4 * group + piece + 1) * rows]
                for group in range(GROUPS)
            ],
            axis=0,
        )
        for piece in range(4)
    ]
    stats_ref[...] = put_columns(
        jnp.zeros(stats_ref.shape, single),
        [(8, gain_third), (11, shift_third), (14, scale_third), (15, shrink_bias_grad)]
        + [(16 + piece, pieces[piece]) for piece in range(4)],
    )


def cross_back_kernel(
    limit_ref, normed_ref, second_normed_ref, second_scaled_ref, back_ref,
    query_ref, keys_ref, values_ref, mixed_ref, totals_ref, output_ref,
    gain_ref, shift_ref, omega_ref, stats_in_ref,
    part_grad_ref, incoming_ref, output_grad_ref, stats_ref,
    query_grad_ref, keys_grad_ref, values_grad_ref, *scratch,
):
    half = lax.axis_index("half")
    columns = columns_of([gain_ref[0:1], shift_ref[0:1], gain_ref[1:2], omega_ref[1:2]])
    size = keys_ref.shape[1] // 2
    first = normed_ref[...] * columns[:, 0:1] + columns[:, 1:2]
    sum_grad, gain_second, shift_second = normalize_back(
        back_ref[...], second_normed_ref[...], second_scaled_ref[...], columns[:, 2:3]
    )
    part_grad_ref[...] = sum_grad * columns[:, 3:4]
    cross_low = low(sum_grad)
    stats_ref[...] = put_columns(
        stats_in_ref[...],
        [
            (5, over_tokens(wide(cross_low))),
            (7, gain_second), (10, shift_second), (13, over_tokens(first * sum_grad)),
        ],
    )
    output_grad_ref[...] = low(dot(mixed_ref[...], cross_low, NT))
    incoming_ref[...] = low(dot(output_ref[...], cross_low, NN))
    mask = source_mask(limit_ref[0, 0], half, size)
    attend_backward(
        query_ref, keys_ref, values_ref, mixed_ref, totals_ref, incoming_ref, mask, False,
        query_grad_ref, keys_grad_ref, values_grad_ref, 0, HEADS // 2, scratch,
    )


def cross_rest_kernel(
    limit_ref, normed_ref, memory_t_ref, query_ref, keys_ref, values_ref, mixed_ref, totals_ref,
    maps_ref, gain_ref, shift_ref, part_grad_ref, incoming_ref, output_grad_ref, stats_in_ref,
    query_half_ref, keys_half_ref, values_half_ref,
    first_grad_ref, own_ref, away_ref, stats_ref, keep_ref, send_ref,
    query_grad_ref, keys_grad_ref, values_grad_ref, held_ref, *scratch, shift,
):
    me, across = ranks(shift)
    columns = columns_of([gain_ref[0:1], shift_ref[0:1]])
    size = own_ref.shape[1]
    width = normed_ref.shape[0]
    mask = source_mask(limit_ref[0, 0], lax.axis_index("half"), size)
    attend_backward(
        query_ref, keys_ref, values_ref, mixed_ref, totals_ref, incoming_ref, mask, False,
        query_grad_ref, keys_grad_ref, values_grad_ref, HEADS // 2, HEADS, scratch,
    )
    top = slice(0, width // 2)
    query_grad_ref[top] = query_half_ref[top]
    keys_grad_ref[top] = keys_half_ref[top]
    values_grad_ref[top] = values_half_ref[top]
    query_grad, keys_grad, values_grad = query_grad_ref[...], keys_grad_ref[...], values_grad_ref[...]
    first_low = low(normed_ref[...] * columns[:, 0:1] + columns[:, 1:2])
    pack(keep_ref, send_ref, held_ref, output_grad_ref[...], 3 * width, me, across)
    pack(keep_ref, send_ref, held_ref, dot(first_low, query_grad, NT), 0, me, across)
    pack(keep_ref, send_ref, held_ref, dot(memory_t_ref[...], keys_grad, NT), width, me, across)
    pack(keep_ref, send_ref, held_ref, dot(memory_t_ref[...], values_grad, NT), 2 * width, me, across)
    first_grad_ref[...] = part_grad_ref[...] + dot(maps_ref[0], query_grad, NN)
    memory_grad = dot(maps_ref[1], keys_grad, NN) + dot(maps_ref[2], values_grad, NN)
    own_ref[...] = memory_grad[:, :size]
    away_ref[...] = low(memory_grad[:, size:])
    stats_ref[...] = put_columns(
        stats_in_ref[...],
        [(3, over_tokens(wide(query_grad))), (4, over_tokens(wide(values_grad)))],
    )


def self_back_kernel(
    limit_ref, input_t_ref, normed_ref, scaled_ref, first_grad_ref, qkv_ref, mixed_ref, totals_ref,
    output_ref, gain_ref, omega_ref, stats_in_ref,
    part_grad_ref, incoming_ref, stats_ref, query_grad_ref, keys_grad_ref, values_grad_ref,
    keep_ref, send_ref, held_ref, *scratch, shift,
):
    me, _ = ranks(shift)
    columns = columns_of([gain_ref[0:1], omega_ref[0:1]])
    width, span = input_t_ref.shape
    sum_grad, gain_first, shift_first = normalize_back(
        first_grad_ref[...], normed_ref[...], scaled_ref[...], columns[:, 0:1]
    )
    part_grad_ref[...] = sum_grad * columns[:, 1:2]
    self_low = low(sum_grad)
    inputs = input_t_ref[...]
    stats_ref[...] = put_columns(
        stats_in_ref[...],
        [
            (2, over_tokens(wide(self_low))), (6, gain_first), (9, shift_first),
            (12, over_tokens(wide(inputs) * sum_grad)),
        ],
    )
    incoming_ref[...] = low(dot(output_ref[...], self_low, NN))
    position = lax.broadcasted_iota(jnp.int32, (1, span), 1)
    mask = jnp.where(position < limit_ref[0, 0], 0.0, far)
    attend_backward(
        qkv_ref.at[0:width], qkv_ref.at[width : 2 * width], qkv_ref.at[2 * width :],
        mixed_ref, totals_ref, incoming_ref, mask, True,
        query_grad_ref, keys_grad_ref, values_grad_ref, 0, HEADS // 2, scratch,
    )
    pack(keep_ref, send_ref, held_ref, dot(mixed_ref[...], self_low, NT), 3 * width // 2, me, None)
    pack_maps(
        keep_ref, send_ref, held_ref, inputs, (query_grad_ref, keys_grad_ref, values_grad_ref),
        slice(0, width // 2), me,
    )


def pack_maps(keep_ref, send_ref, held_ref, inputs, grads, rows, me):
    for at, ref in enumerate(grads):
        part = dot(inputs, ref[rows], NT)
        pack(keep_ref, send_ref, held_ref, part, at * part.shape[1], me, None)


def self_heads_kernel(
    limit_ref, qkv_ref, mixed_ref, totals_ref, incoming_ref,
    query_half_ref, keys_half_ref, values_half_ref,
    query_grad_ref, keys_grad_ref, values_grad_ref, *scratch,
):
    width, span = mixed_ref.shape
    position = lax.broadcasted_iota(jnp.int32, (1, span), 1)
    mask = jnp.where(position < limit_ref[0, 0], 0.0, far)
    attend_backward(
        qkv_ref.at[0:width], qkv_ref.at[width : 2 * width], qkv_ref.at[2 * width :],
        mixed_ref, totals_ref, incoming_ref, mask, True,
        query_grad_ref, keys_grad_ref, values_grad_ref, HEADS // 2, HEADS, scratch,
    )
    top = slice(0, width // 2)
    query_grad_ref[top] = query_half_ref[top]
    keys_grad_ref[top] = keys_half_ref[top]
    values_grad_ref[top] = values_half_ref[top]


def self_rest_kernel(
    input_t_ref, stats_in_ref, query_grad_ref, keys_grad_ref, values_grad_ref,
    keep_ref, send_ref, held_ref, *, shift,
):
    me, _ = ranks(shift)
    width = input_t_ref.shape[0]
    pack_maps(
        keep_ref, send_ref, held_ref, input_t_ref[...], (query_grad_ref, keys_grad_ref, values_grad_ref),
        slice(width // 2, width), me,
    )
    stats = put_columns(
        stats_in_ref[...],
        [(0, over_tokens(wide(query_grad_ref[...]))), (1, over_tokens(wide(values_grad_ref[...])))],
    )
    pack(keep_ref, send_ref, held_ref, stats, 3 * width // 2, me, None)


def input_kernel(part_grad_ref, query_grad_ref, keys_grad_ref, values_grad_ref, maps_ref, input_grad_ref):
    input_grad_ref[0, 0] = (
        part_grad_ref[...]
        + dot(maps_ref[0], query_grad_ref[...], NN)
        + dot(maps_ref[1], keys_grad_ref[...], NN)
        + dot(maps_ref[2], values_grad_ref[...], NN)
    ).T


def halve_kernel(kept_ref, arrived_ref, sent_out_ref, kept_out_ref):
    part = kept_ref.shape[0] // 2
    at = slice(part, None) if part > 1 else 1
    sent_out_ref[...] = low(wide(kept_ref[at]) + wide(arrived_ref[at]))
    at = slice(0, part) if part > 1 else 0
    kept_out_ref[...] = low(wide(kept_ref[at]) + wide(arrived_ref[at]))


def sum_kernel(kept_ref, arrived_ref, out_ref):
    out_ref[...] = low(wide(kept_ref[...]) + wide(arrived_ref[...]))


def memory_kernel(own_ref, returned_ref, rest_ref, out_ref):
    half = lax.axis_index("half")
    out_ref[half, 0] = own_ref[...].T + rest_ref[half, 0]
    out_ref[1 - half, 0] = wide(returned_ref[...]).T + rest_ref[1 - half, 0]


def finish(ffn, cross, early, late, width):
    features = ffn.shape[1] // 2
    part = width // 2
    maps = [
        jnp.concatenate([v[:, i * part : (i + 1) * part] for v in (early, late)], axis=1)
        for i in range(3)
    ]
    cross_maps = [cross[:, i * width : (i + 1) * width] for i in range(3)]
    shrink = jnp.concatenate(
        [ffn[:, features + i * width : features + (i + 1) * width] for i in range(4)], axis=0
    )
    stats = late[:, 3 * part :].T
    return (
        maps, early[:, 3 * part :], cross_maps, cross[:, 3 * width :],
        stats[0:6], ffn[:, :features], [stats[16 + i : 17 + i] for i in range(4)], shrink,
        stats[15:16], stats[6:9], stats[9:12], stats[12:15],
    )


def finish_kernel(*refs, shift):
    ins, outs, held = refs[:8], refs[8:-4], refs[-4:]
    half = lax.axis_index("half")
    width = outs[1].shape[1]
    for i in range(4):
        own, other = wide(ins[2 * i][...]), wide(ins[2 * i + 1][...])
        if shift or i >= 2:
            held[i][...] = own + other
        else:
            rows = own.shape[0]
            held[i][pl.ds(pl.multiple_of(half * rows, rows), rows)] = own
            held[i][pl.ds(pl.multiple_of((1 - half) * rows, rows), rows)] = other
    for ref, value in zip(outs, finish(*(ref[...] for ref in held), width)):
        if isinstance(value, list):
            for at, item in enumerate(value):
                ref[at] = item.reshape(ref.shape[1:])
        else:
            ref[...] = value


TIMES = {
    "projections": 2, "self_forward": 10, "cross_forward": 13, "ffn": 20, "cross_back": 12, "cross_rest": 13,
    "self_back": 11, "self_heads": 7, "self_rest": 3, "input_grad": 3, "memory_grad": 2,
}


def call(kernel, name, outs, scratch=(), specs=None, after=(), vmem=16, **options):
    def entry(*refs):
        kernel(*refs[len(after) :], **options)

    return lambda *args: pl.pallas_call(
        entry,
        name=name,
        out_shape=outs,
        in_specs=[pl.BlockSpec(memory_space=pl.ANY)] * len(after) + (specs or [VM] * len(args)),
        out_specs=jax.tree.map(lambda _: VM, outs),
        scratch_shapes=scratch,
        compiler_params=pltpu.CompilerParams(vmem_limit_bytes=vmem * 1024 * 1024),
        cost_estimate=pl.CostEstimate(
            flops=TIMES.get(name, 1) * MICROSECOND, bytes_accessed=1_000_000, transcendentals=0
        ),
    )(*after, *args)


def shards(
    block_input, memory, memory_grad_rest, output_grad, target_length, source_length,
    self_maps, self_output, cross_maps, cross_output, attention_bias,
    expand_weight, expand_bias, shrink_weight, shrink_bias, norm_gain, norm_bias, residual_scale,
    *, devices,
):
    span, width = block_input.shape[2:]
    size = memory.shape[2]
    source = 2 * size
    features = expand_weight.shape[1]
    shift = int(math.log2(devices // GROUPS))
    assert GROUPS << shift == devices
    rows = width // GROUPS
    half = lax.axis_index("half")

    def swap_half(value):
        return lax.ppermute(value, "half", [(0, 1), (1, 0)])

    def swap(value, bits):
        return lax.ppermute(value, "batch", [(i, i ^ bits) for i in range(devices)])

    def halve(kept, arrived, *after):
        part = kept.shape[0] // 2
        shape = kept.shape[1:] if part == 1 else (part, *kept.shape[1:])
        return call(halve_kernel, "halve", [sds(shape, bfloat)] * 2, after=after)(kept, arrived)

    def joined(kept, arrived, *after):
        return call(sum_kernel, "join", sds(kept.shape, bfloat), after=after)(kept, arrived)

    CORE, NEAR, NEXT, AWAY = 1, 2, 4, 8

    def scattered(keep, send, pieces=None):
        packet = jnp.stack([keep, send])
        if packet.ndim == 6:
            packet = packet.transpose(3, 2, 0, 1, 4, 5)
        else:
            packet = packet.transpose(2, 1, 0, 3, 4)
        packet = packet.reshape(2, 2, 4, rows, -1).swapaxes(0, 1)
        packet = packet.reshape(GROUPS, rows, -1)
        if pieces:
            start, stop = pieces
            part = packet[..., start:stop].reshape(GROUPS, rows, 4, -1).swapaxes(1, 2)
            part = part.reshape(GROUPS, 1 << shift, 4, rows >> shift, -1).swapaxes(2, 3)
            part = part.reshape(GROUPS, rows, stop - start)
            packet = jnp.concatenate([packet[..., :start], part, packet[..., stop:]], axis=-1)
        total = lax.psum_scatter(
            packet.reshape(width, -1), "batch", scatter_dimension=0, tiled=True
        )
        return total, swap_half(total)

    arrived = swap_half(lax.dynamic_index_in_dim(memory, 1 - half, 0, keepdims=False)[0])
    tall = sds((width, span), bfloat)
    tall_wide = sds((width, span), single)
    packet = lambda lanes: [sds((2, 2, 4, rows // 2, lanes), bfloat)] * 2
    simple = lambda lanes: [sds((2, 4, rows, lanes), bfloat)] * 2
    input_t, qkv = call(
        projection_kernel, "projections", [tall, sds((3 * width, span), bfloat)],
    )(block_input, self_maps, attention_bias)
    mixed, totals, normed, scaled = call(
        self_forward_kernel, "self_forward",
        [tall, sds((HEADS, span), single), tall_wide, sds((1, span), single)],
        specs=[SM] + [VM] * 5, scratch=forward_scratch(span),
    )(target_length, input_t, qkv, self_output, attention_bias, residual_scale)
    source_tall = sds((width, source), bfloat)
    (
        memory_t, query, keys, values, cross_mixed, cross_totals, second_normed, second_scaled,
    ) = call(
        cross_forward_kernel, "cross_forward",
        [source_tall, tall, source_tall, source_tall, tall, sds((HEADS, span), single),
         tall_wide, sds((1, span), single)],
        specs=[SM] + [VM] * 9, scratch=forward_scratch(span),
    )(
        source_length, normed, memory, arrived, cross_maps, cross_output, attention_bias,
        norm_gain, norm_bias, residual_scale,
    )
    layer_output, second_grad, stats, ffn_keep, ffn_send = call(
        ffn_kernel, "ffn",
        [sds((1, 1, span, width), single), tall_wide, sds((width, LANES), single)]
        + packet(2 * features),
        scratch=[pltpu.VMEM((features, span), bfloat)] * 2
        + [pltpu.VMEM((width, features), bfloat), pltpu.VMEM((features, width), bfloat)],
        shift=shift, vmem=32,
    )(
        second_normed, norm_gain, norm_bias, residual_scale, expand_weight,
        expand_bias, shrink_weight, shrink_bias, output_grad,
    )
    grads = [pltpu.VMEM((width, span), bfloat)] + [pltpu.VMEM((width, source), bfloat)] * 2
    held = pltpu.VMEM((width, width), bfloat)
    square = sds((width, width), bfloat)
    stats_shape = sds((width, LANES), single)
    part_grad, incoming, output_part, stats, *halves = call(
        cross_back_kernel, "cross_back",
        [tall_wide, tall, square, stats_shape, tall, source_tall, source_tall],
        specs=[SM] + [VM] * 14, scratch=backward_scratch(span),
    )(
        source_length, normed, second_normed, second_scaled, second_grad,
        query, keys, values, cross_mixed, cross_totals, cross_output,
        norm_gain, norm_bias, residual_scale, stats,
    )
    if not shift:
        ffn = halve(ffn_keep, swap(ffn_send, CORE), part_grad)
    first_grad, own, away, stats, cross_keep, cross_send = call(
        cross_rest_kernel, "cross_rest",
        [tall_wide, sds((width, size), single), sds((width, size), bfloat), stats_shape]
        + packet(4 * width),
        scratch=grads + [held] + backward_scratch(span), specs=[SM] + [VM] * 17, after=() if shift else ffn, shift=shift,
    )(
        source_length, normed, memory_t, query, keys, values, cross_mixed, cross_totals, cross_maps,
        norm_gain, norm_bias, part_grad, incoming, output_part, stats, *halves,
    )
    part_grad, incoming, stats, *rest_of = call(
        self_back_kernel, "self_back",
        [tall_wide, tall, stats_shape, tall, tall, tall] + simple(5 * width // 2),
        specs=[SM] + [VM] * 11, scratch=[held] + backward_scratch(span), shift=shift,
    )(
        target_length, input_t, normed, scaled, first_grad, qkv, mixed, totals,
        self_output, norm_gain, residual_scale, stats,
    )
    *halves, early_keep, early_send = rest_of
    before = ()
    if not shift:
        ffn = halve(ffn[1], swap_half(ffn[0]), stats)
        cross = halve(cross_keep, swap(cross_send, CORE), *ffn)
        before = (*ffn, *cross)
    grads_out = call(
        self_heads_kernel, "self_heads", [tall] * 3, specs=[SM] + [VM] * 7,
        scratch=backward_scratch(span), after=before,
    )(target_length, qkv, mixed, totals, incoming, *halves)
    before = ()
    if not shift:
        early = halve(early_keep, swap(early_send, CORE), grads_out[0])
        before = early
    late_keep, late_send = call(
        self_rest_kernel, "self_rest", simple(3 * width // 2 + LANES),
        scratch=[held], after=before, shift=shift,
    )(input_t, stats, *grads_out)
    def to_input(*after):
        return call(input_kernel, "input_grad", sds((1, 1, span, width), single), after=after)(
            part_grad, *grads_out, self_maps
        )

    if shift:
        input_grad = to_input()
        start = 3 * width // 2 + 16
        parts = (
            *scattered(ffn_keep, ffn_send, (features, 2 * features)),
            *scattered(cross_keep, cross_send),
            *scattered(early_keep, early_send),
            *scattered(late_keep, late_send, (start, start + 4)),
        )
    else:
        ffn = halve(ffn[1], swap(ffn[0], NEAR), late_keep)
        late = halve(late_keep, swap(late_send, CORE), *ffn)
        cross = halve(cross[1], swap_half(cross[0]), *late)
        input_grad = to_input(*cross)
        early = halve(early[1], swap(early[0], NEAR), input_grad)
        ffn = halve(ffn[1], swap(ffn[0], NEXT), *early)
        late = halve(late[1], swap(late[0], NEAR), *ffn)
        cross = halve(cross[1], swap(cross[0], NEAR), *late)
        early = halve(early[1], swap(early[0], NEXT), *cross)
        late = halve(late[1], swap(late[0], NEXT), *early)
        ffn = joined(ffn[1], swap(ffn[0], AWAY), *late)
        cross = halve(cross[1], swap(cross[0], NEXT), ffn)
        early = joined(early[1], swap(early[0], AWAY), *cross)
        late = joined(late[1], swap(late[0], AWAY), early)
        cross = joined(cross[1], swap(cross[0], AWAY), late)
        parts = tuple(
            part for value in (ffn, cross, early, late) for part in (value, swap_half(value))
        )
    memory_grad = call(memory_kernel, "memory_grad", sds(memory_grad_rest.shape, single))(
        own, swap_half(away), memory_grad_rest
    )
    mine = rows >> shift
    outs = [
        sds((3, mine, width), single), sds((mine, width), single), sds((3, mine, width), single),
        sds((mine, width), single), sds((6, mine), single), sds((mine, features), single),
        sds((4, mine), single), sds((4 * mine, width), single), sds((1, mine), single),
        sds((3, mine), single), sds((3, mine), single), sds((3, mine), single),
    ]
    done = list(
        call(
            finish_kernel, "finish", outs, shift=shift,
            scratch=[
                pltpu.VMEM((mine, lanes), single)
                for lanes in (2 * features, 4 * width, 5 * width // 2, 3 * width // 2 + LANES)
            ],
        )(*parts)
    )
    done[6] = done[6].reshape(-1)
    done[8] = done[8].reshape(-1)
    return (layer_output, input_grad, memory_grad, *done)


def solution(mesh):
    rows = P("half", "batch", None, None)
    sources = P(None, "batch", "half", None)
    placed = (rows, sources, sources, rows, P("half", "batch"), P("half", "batch")) + (P(),) * 12
    return jax.shard_map(
        partial(shards, devices=mesh.shape["batch"]),
        mesh=mesh,
        in_specs=placed,
        out_specs=(
            rows, rows, sources,
            P(None, "batch", None), P("batch", None), P(None, "batch", None), P("batch", None),
            P(None, "batch"), P("batch", None), P("batch"), P("batch", None), P("batch"),
            P(None, "batch"), P(None, "batch"), P(None, "batch"),
        ),
        check_vma=False,
    )
```

```python
from functools import partial
import math

import jax
import jax.numpy as jnp
from jax import lax
from jax.experimental import pallas as pl
from jax.experimental.pallas import tpu as pltpu
from jax.sharding import PartitionSpec as P

HEADS = 8
HEAD = 64
GROUPS = 16
LANES = 128
QUERY_BLOCK = 512
KEY_BLOCK = 256
ROW_BLOCK = 256

eps = 1e-05
bfloat = jnp.bfloat16
single = jnp.float32
scale = HEAD ** (-0.5)
to_log2 = math.log2(math.e) * scale
far = -1.5e9

NN = (((1,), (0,)), ((), ()))
NT = (((1,), (1,)), ((), ()))
TN = (((0,), (0,)), ((), ()))

VM = pl.BlockSpec(memory_space=pltpu.VMEM)
SM = pl.BlockSpec(memory_space=pltpu.SMEM)
sds = jax.ShapeDtypeStruct


def dot(left, right, dims):
    return lax.dot_general(left, right, dims, preferred_element_type=single)


def low(value):
    return value.astype(bfloat)


def wide(value):
    return value.astype(single)


def split(value):
    high = low(value)
    return high, low(value - wide(high))


def split_three(value):
    high = low(value)
    rest = value - wide(high)
    middle = low(rest)
    return wide(high), wide(middle), wide(low(rest - wide(middle)))


def rows_of(rows, count=16):
    width = rows[0].shape[1]
    index = lax.broadcasted_iota(jnp.int32, (count, width), 0)
    out = jnp.zeros((count, width), single)
    for at, row in enumerate(rows):
        out = jnp.where(index == at, row, out)
    return out


def columns_of(rows):
    return rows_of(rows, -(-len(rows) // 8) * 8).T


def over_tokens(value):
    return jnp.sum(value, axis=1, keepdims=True)


def normalize(total):
    center = total - jnp.mean(total, axis=0, keepdims=True)
    spread = jnp.mean(center * center, axis=0, keepdims=True)
    scaled = lax.rsqrt(spread + eps)
    return center * scaled, scaled


def normalize_back(grad, normed, scaled, gain):
    inner = grad * gain
    back = scaled * (
        inner
        - jnp.mean(inner, axis=0, keepdims=True)
        - normed * jnp.mean(inner * normed, axis=0, keepdims=True)
    )
    return back, over_tokens(grad * normed), over_tokens(grad)


def put_columns(stats, items):
    lane = lax.broadcasted_iota(jnp.int32, stats.shape, 1)
    for at, column in items:
        stats = jnp.where(lane == at, column, stats)
    return stats


def places(me, half):
    for core in range(2):
        for near in range(2):
            for far_off in range(4):
                bits = core + 2 * near + 4 * (far_off // 2) + 8 * (far_off % 2)
                group = jnp.bitwise_xor(me, bits)
                if half is None:
                    yield core, (near, far_off), group, 0
                else:
                    for across in range(2):
                        yield core, (near, across, far_off), group, jnp.bitwise_xor(half, across)


def pack(keep_ref, send_ref, held_ref, grad, at, me, half):
    held_ref[:, : grad.shape[1]] = low(grad)
    rows = grad.shape[0] // GROUPS
    part = rows if half is None else rows // 2
    lanes = slice(at, at + grad.shape[1])
    for core, place, group, portion in places(me, half):
        start = pl.multiple_of(group * rows + portion * part, part)
        (send_ref if core else keep_ref)[(*place, slice(None), lanes)] = held_ref[
            pl.ds(start, part), : grad.shape[1]
        ]


def ranks(shift):
    return (0, 0) if shift else (lax.axis_index("batch"), lax.axis_index("half"))


def head_rows(head):
    return pl.ds(pl.multiple_of(head * HEAD, HEAD), HEAD)


def hide_later(scores, offset, query_axis):
    key_pos = lax.broadcasted_iota(jnp.int32, scores.shape, 1 - query_axis) + offset
    query_pos = lax.broadcasted_iota(jnp.int32, scores.shape, query_axis)
    return jnp.where(key_pos <= query_pos, scores, far)


def forward_scratch(span):
    return [
        pltpu.VMEM((2, span, QUERY_BLOCK), single),
        pltpu.VMEM((8, QUERY_BLOCK), single),
        pltpu.VMEM((2, 2 * HEAD + 16, span), bfloat),
        pltpu.VMEM((2, span, 2 * HEAD + 16), bfloat),
        pltpu.VMEM((3, HEAD + 16, span), bfloat),
    ]


def attend_forward(query_ref, keys_ref, values_ref, mask, is_causal, mixed_ref, totals_ref, scratch):
    scores_ref, top_ref, more_query_ref, more_keys_ref, more_values_ref = scratch
    span = query_ref.shape[1]
    blocks = span // QUERY_BLOCK
    ones = low(rows_of([jnp.ones((1, span), single)]))
    more_query_ref[0, 2 * HEAD :] = ones
    more_query_ref[1, 2 * HEAD :] = ones
    mask_column = low(rows_of([mask])).T
    more_keys_ref[0, :, 2 * HEAD :] = mask_column
    more_keys_ref[1, :, 2 * HEAD :] = mask_column
    for slot in range(3):
        more_values_ref[slot, HEAD:] = ones

    def key_blocks(block):
        return range(0, (block + 1) * QUERY_BLOCK if is_causal else span, KEY_BLOCK)

    def prepare(head, slot):
        rows = head_rows(head)
        high, rest = split(wide(query_ref[rows]) * to_log2)
        more_query_ref[slot, :HEAD] = high
        more_query_ref[slot, HEAD : 2 * HEAD] = rest
        keys = keys_ref[rows]
        more_keys_ref[slot, :, : 2 * HEAD] = jnp.concatenate([keys, keys], axis=0).T
        more_values_ref[lax.rem(head, 3), :HEAD] = values_ref[rows]

    def score(slot, block, key, top):
        at = slice(block * QUERY_BLOCK, (block + 1) * QUERY_BLOCK)
        scores = dot(more_keys_ref[slot, key : key + KEY_BLOCK], more_query_ref[slot, :, at], NN)
        if is_causal and key + KEY_BLOCK > block * QUERY_BLOCK:
            scores = hide_later(scores, key - block * QUERY_BLOCK, 1)
        scores_ref[block % 2, key : key + KEY_BLOCK] = scores
        part = jnp.max(scores.reshape(KEY_BLOCK // 8, 8, QUERY_BLOCK), axis=0)
        return part if top is None else jnp.maximum(top, part)

    def mix(head, block, key, top, total):
        expo = low(jnp.exp2(scores_ref[block % 2, key : key + KEY_BLOCK] - top))
        part = dot(more_values_ref[lax.rem(head, 3), :, key : key + KEY_BLOCK], expo, NN)
        return part if total is None else total + part

    def finish_block(head, block, top, total):
        at = slice(block * QUERY_BLOCK, (block + 1) * QUERY_BLOCK)
        summed = total[HEAD : HEAD + 1]
        mixed_ref[head_rows(head), at] = low(total[:HEAD] / summed)
        totals_ref[pl.ds(head, 1), at] = top + jnp.log2(summed)

    prepare(0, 0)
    last = blocks - 1

    def body(pair, carry):
        for odd in range(2):
            head = 2 * pair + odd
            for block in range(blocks):
                before, block_before = (head, block - 1) if block else (jnp.maximum(head - 1, 0), last)
                top_before = top_ref[block_before % 2 : block_before % 2 + 1]
                top = None
                total = None
                now, then = list(key_blocks(block)), list(key_blocks(block_before))
                for step in range(max(len(now), len(then))):
                    if step < len(now):
                        top = score(odd, block, now[step], top)
                    if step < len(then):
                        total = mix(before, block_before, then[step], top_before, total)
                top_ref[block % 2 : block % 2 + 1] = jnp.max(top, axis=0, keepdims=True)
                finish_block(before, block_before, top_before, total)
                if block == 0:
                    prepare(jnp.minimum(head + 1, HEADS - 1), 1 - odd)
        return carry

    lax.fori_loop(0, HEADS // 2, body, 0)
    top = top_ref[last % 2 : last % 2 + 1]
    total = None
    for key in key_blocks(last):
        total = mix(HEADS - 1, last, key, top, total)
    finish_block(HEADS - 1, last, top, total)


def backward_scratch(span):
    return (
        [pltpu.VMEM((2, span, KEY_BLOCK), bfloat)] * 2
        + [pltpu.VMEM((2, span, HEAD + 16), bfloat)] * 2
        + [pltpu.VMEM((2, HEAD + 16, span), bfloat)] * 2
        + [pltpu.VMEM((HEAD, span), single)]
    )


def attend_backward(
    query_ref, keys_ref, values_ref, mixed_ref, totals_ref, incoming_ref, mask, is_causal,
    query_grad_ref, keys_grad_ref, values_grad_ref, first_head, last_head, scratch,
):
    probs_ref, score_grads_ref, more_query_ref, more_incoming_ref, more_keys_ref, more_values_ref, held_ref = scratch
    span = query_ref.shape[1]
    blocks = span // KEY_BLOCK
    ones = jnp.ones((1, span), single)
    for slot in range(2):
        more_keys_ref[slot, HEAD:] = low(rows_of([ones, ones, ones, mask]))
        more_values_ref[slot, HEAD:] = low(rows_of([ones, ones, ones]))

    def first_query(block):
        return block * KEY_BLOCK if is_causal else 0

    def prepare(head, slot):
        rows = head_rows(head)
        query, incoming = query_ref[rows], incoming_ref[rows]
        delta = jnp.sum(wide(incoming) * wide(mixed_ref[rows]), axis=0, keepdims=True)
        totals = split_three(totals_ref[pl.ds(head, 1), :] * (-1 / to_log2))
        more_query_ref[slot] = jnp.concatenate([query, low(rows_of([*totals, ones]))], axis=0).T
        more_incoming_ref[slot] = jnp.concatenate(
            [incoming, low(rows_of(split_three(-delta)))], axis=0
        ).T
        more_keys_ref[slot, :HEAD] = keys_ref[rows]
        more_values_ref[slot, :HEAD] = values_ref[rows]

    def score(slot, block, start):
        keys, rows = slice(block * KEY_BLOCK, (block + 1) * KEY_BLOCK), slice(start, start + ROW_BLOCK)
        scores = dot(more_query_ref[slot, rows], more_keys_ref[slot, :, keys], NN)
        if is_causal and start < (block + 1) * KEY_BLOCK:
            scores = hide_later(scores, block * KEY_BLOCK - start, 0)
        probs = jnp.exp2(scores * to_log2)
        prob_grad = dot(more_incoming_ref[slot, rows], more_values_ref[slot, :, keys], NN)
        probs_ref[block % 2, rows] = low(probs)
        score_grads_ref[block % 2, rows] = low(probs * prob_grad)

    def products(head, block):
        rows, keys = head_rows(head), slice(block * KEY_BLOCK, (block + 1) * KEY_BLOCK)
        start = first_query(block)

        def values_part():
            values_grad_ref[rows, keys] = low(
                dot(incoming_ref[rows, start:], probs_ref[block % 2, start:], NN)
            )

        def keys_part():
            keys_grad_ref[rows, keys] = low(
                dot(query_ref[rows, start:], score_grads_ref[block % 2, start:], NN) * scale
            )

        def query_part(at):
            stop = min(at + 2 * ROW_BLOCK, span)
            part = dot(keys_ref[rows, keys], score_grads_ref[block % 2, at:stop], NT)
            if block:
                part = part + held_ref[:, at:stop]
            held_ref[:, at:stop] = part

        def query_whole():
            query_grad_ref[rows] = low(held_ref[...] * scale)

        steps = [values_part, keys_part]
        steps += [partial(query_part, at) for at in range(start, span, 2 * ROW_BLOCK)]
        return steps + [query_whole] * (block == blocks - 1)

    prepare(first_head, 0)

    def body(pair, carry):
        for odd in range(2):
            head = first_head + 2 * pair + odd
            for block in range(blocks):
                if block:
                    steps = products(head, block - 1)
                else:
                    steps = products(jnp.maximum(head - 1, first_head), blocks - 1)
                starts = range(first_query(block), span, ROW_BLOCK)
                for step in range(max(len(starts), len(steps))):
                    if step < len(starts):
                        score(odd, block, starts[step])
                    if step < len(steps):
                        steps[step]()
                if block == 0:
                    prepare(jnp.minimum(head + 1, last_head - 1), 1 - odd)
        return carry

    lax.fori_loop(0, (last_head - first_head) // 2, body, 0)
    for step in products(last_head - 1, blocks - 1):
        step()


ROOT = math.sqrt(2 / math.pi)
CUBE = ROOT * 0.044715


def gelu_parts(value):
    half = 0.5 * value
    cube = CUBE * (value * value)
    tanh = jnp.tanh(value * (ROOT + cube))
    more = 1 + tanh
    return half * more, more * (0.5 + (1 - tanh) * (half * (ROOT + 3 * cube)))


def projection_kernel(input_ref, maps_ref, bias_ref, input_t_ref, qkv_ref):
    columns = columns_of([bias_ref[0:1], bias_ref[1:2]])
    inputs = input_ref[0, 0].T
    input_t_ref[...] = inputs
    width = inputs.shape[0]
    qkv_ref[0:width] = low(dot(maps_ref[0], inputs, TN) + columns[:, 0:1])
    qkv_ref[width : 2 * width] = low(dot(maps_ref[1], inputs, TN))
    qkv_ref[2 * width :] = low(dot(maps_ref[2], inputs, TN) + columns[:, 1:2])


def self_forward_kernel(
    limit_ref, input_t_ref, qkv_ref, output_ref, bias_ref, omega_ref,
    mixed_ref, totals_ref, normed_ref, scaled_ref, *scratch,
):
    columns = columns_of([bias_ref[2:3], omega_ref[0:1]])
    width, span = input_t_ref.shape
    position = lax.broadcasted_iota(jnp.int32, (1, span), 1)
    mask = jnp.where(position < limit_ref[0, 0], 0.0, far)
    attend_forward(
        qkv_ref.at[0:width], qkv_ref.at[width : 2 * width], qkv_ref.at[2 * width :],
        mask, True, mixed_ref, totals_ref, scratch,
    )
    branch = dot(output_ref[...], mixed_ref[...], TN) + columns[:, 0:1]
    normed, scaled = normalize(wide(input_t_ref[...]) * columns[:, 1:2] + branch)
    normed_ref[...] = normed
    scaled_ref[...] = scaled


def source_mask(limit, half, size):
    local = lax.broadcasted_iota(jnp.int32, (1, 2 * size), 1)
    own = local < size
    position = jnp.where(own, local + half * size, local - size + (1 - half) * size)
    return jnp.where(position < limit, 0.0, far)


def cross_forward_kernel(
    limit_ref, normed_ref, memory_ref, arrived_ref, maps_ref, output_ref, bias_ref,
    gain_ref, shift_ref, omega_ref,
    memory_t_ref, query_ref, keys_ref, values_ref, mixed_ref, totals_ref,
    second_normed_ref, second_scaled_ref, *scratch,
):
    half = lax.axis_index("half")
    columns = columns_of(
        [bias_ref[3:4], bias_ref[4:5], bias_ref[5:6], gain_ref[0:1], shift_ref[0:1], omega_ref[1:2]]
    )
    size = memory_ref.shape[2]
    first = normed_ref[...] * columns[:, 3:4] + columns[:, 4:5]
    query_ref[...] = low(dot(maps_ref[0], low(first), TN) + columns[:, 0:1])
    memory_t_ref[:, :size] = memory_ref[half, 0].T
    memory_t_ref[:, size:] = arrived_ref[...].T
    keys_ref[...] = low(dot(maps_ref[1], memory_t_ref[...], TN))
    values_ref[...] = low(dot(maps_ref[2], memory_t_ref[...], TN) + columns[:, 1:2])
    mask = source_mask(limit_ref[0, 0], half, size)
    attend_forward(query_ref, keys_ref, values_ref, mask, False, mixed_ref, totals_ref, scratch)
    branch = dot(output_ref[...], mixed_ref[...], TN) + columns[:, 2:3]
    second_normed, second_scaled = normalize(first * columns[:, 5:6] + branch)
    second_normed_ref[...] = second_normed
    second_scaled_ref[...] = second_scaled


def ffn_kernel(
    second_normed_ref, gain_ref, shift_ref, omega_ref, expand_ref, expand_bias_ref, shrink_ref,
    shrink_bias_ref, grad_ref,
    layer_ref, back_ref, stats_ref, keep_ref, send_ref,
    hidden_ref, slope_ref, held_ref, wide_held_ref,
    *, shift,
):
    me, half = ranks(shift)
    columns = columns_of(
        [gain_ref[1:2], gain_ref[2:3], shift_ref[1:2], shift_ref[2:3], omega_ref[2:3]]
        + [shrink_bias_ref[...].reshape(1, -1)]
        + [expand_bias_ref[i : i + 512].reshape(1, -1) for i in range(0, expand_ref.shape[1], 512)]
    )
    width, span = second_normed_ref.shape
    second = second_normed_ref[...] * columns[:, 0:1] + columns[:, 2:3]
    second_low = low(second)
    features = expand_ref.shape[1]
    chunk = 512
    ffn = None
    for at in range(0, features, chunk):
        part = slice(at, at + chunk)
        pre = dot(expand_ref[:, part], second_low, TN) + columns[:, 6 + at // chunk : 7 + at // chunk]
        value, slope = gelu_parts(pre)
        hidden_ref[part] = low(value)
        slope_ref[part] = low(slope)
        term = dot(shrink_ref[part], hidden_ref[part], TN)
        ffn = term if ffn is None else ffn + term
    third_normed, third_scaled = normalize(second * columns[:, 4:5] + (ffn + columns[:, 5:6]))
    layer_ref[0, 0] = (third_normed * columns[:, 1:2] + columns[:, 3:4]).T
    grad = wide(grad_ref[0, 0].T)
    third_grad, gain_third, shift_third = normalize_back(
        grad, third_normed, third_scaled, columns[:, 1:2]
    )
    scale_third = over_tokens(second * third_grad)
    ffn_low = low(third_grad)
    shrink_bias_grad = over_tokens(wide(ffn_low))
    second_grad = third_grad * columns[:, 4:5]
    sums = []
    for at in range(0, features, chunk):
        part = slice(at, at + chunk)
        wide_held_ref[part] = low(dot(hidden_ref[part], ffn_low, NT))
        pre_grad = low(dot(shrink_ref[part], ffn_low, NN) * wide(slope_ref[part]))
        sums.append(over_tokens(wide(pre_grad)))
        held_ref[:, part] = low(dot(second_low, pre_grad, NT))
        second_grad = second_grad + dot(expand_ref[:, part], pre_grad, NN)
    back_ref[...] = second_grad
    rows = features // GROUPS // 4
    for core, place, group, portion in places(me, half):
        out = send_ref if core else keep_ref
        start = pl.multiple_of(group * rows + portion * (rows // 2), rows // 2)
        out[(*place, slice(None), slice(0, features))] = held_ref[pl.ds(start, rows // 2), :]
        for piece in range(4):
            start = (4 * group + piece) * rows + portion * (rows // 2)
            lanes = slice(features + piece * width, features + (piece + 1) * width)
            out[(*place, slice(None), lanes)] = wide_held_ref[
                pl.ds(pl.multiple_of(start, rows // 2), rows // 2), :
            ]
    expand_sums = jnp.concatenate(sums, axis=0)
    pieces = [
        jnp.concatenate(
            [
                expand_sums[(4 * group + piece) * rows : (4 * group + piece + 1) * rows]
                for group in range(GROUPS)
            ],
            axis=0,
        )
        for piece in range(4)
    ]
    stats_ref[...] = put_columns(
        jnp.zeros(stats_ref.shape, single),
        [(8, gain_third), (11, shift_third), (14, scale_third), (15, shrink_bias_grad)]
        + [(16 + piece, pieces[piece]) for piece in range(4)],
    )


def cross_back_kernel(
    limit_ref, normed_ref, second_normed_ref, second_scaled_ref, back_ref,
    query_ref, keys_ref, values_ref, mixed_ref, totals_ref, output_ref,
    gain_ref, shift_ref, omega_ref, stats_in_ref,
    part_grad_ref, incoming_ref, output_grad_ref, stats_ref,
    query_grad_ref, keys_grad_ref, values_grad_ref, *scratch,
):
    half = lax.axis_index("half")
    columns = columns_of([gain_ref[0:1], shift_ref[0:1], gain_ref[1:2], omega_ref[1:2]])
    size = keys_ref.shape[1] // 2
    first = normed_ref[...] * columns[:, 0:1] + columns[:, 1:2]
    sum_grad, gain_second, shift_second = normalize_back(
        back_ref[...], second_normed_ref[...], second_scaled_ref[...], columns[:, 2:3]
    )
    part_grad_ref[...] = sum_grad * columns[:, 3:4]
    cross_low = low(sum_grad)
    stats_ref[...] = put_columns(
        stats_in_ref[...],
        [
            (5, over_tokens(wide(cross_low))),
            (7, gain_second), (10, shift_second), (13, over_tokens(first * sum_grad)),
        ],
    )
    output_grad_ref[...] = low(dot(mixed_ref[...], cross_low, NT))
    incoming_ref[...] = low(dot(output_ref[...], cross_low, NN))
    mask = source_mask(limit_ref[0, 0], half, size)
    attend_backward(
        query_ref, keys_ref, values_ref, mixed_ref, totals_ref, incoming_ref, mask, False,
        query_grad_ref, keys_grad_ref, values_grad_ref, 0, HEADS // 2, scratch,
    )


def cross_rest_kernel(
    limit_ref, normed_ref, memory_t_ref, query_ref, keys_ref, values_ref, mixed_ref, totals_ref,
    maps_ref, gain_ref, shift_ref, part_grad_ref, incoming_ref, output_grad_ref, stats_in_ref,
    query_half_ref, keys_half_ref, values_half_ref,
    first_grad_ref, own_ref, away_ref, stats_ref, keep_ref, send_ref,
    query_grad_ref, keys_grad_ref, values_grad_ref, held_ref, *scratch, shift,
):
    me, across = ranks(shift)
    columns = columns_of([gain_ref[0:1], shift_ref[0:1]])
    size = own_ref.shape[1]
    width = normed_ref.shape[0]
    mask = source_mask(limit_ref[0, 0], lax.axis_index("half"), size)
    attend_backward(
        query_ref, keys_ref, values_ref, mixed_ref, totals_ref, incoming_ref, mask, False,
        query_grad_ref, keys_grad_ref, values_grad_ref, HEADS // 2, HEADS, scratch,
    )
    top = slice(0, width // 2)
    query_grad_ref[top] = query_half_ref[top]
    keys_grad_ref[top] = keys_half_ref[top]
    values_grad_ref[top] = values_half_ref[top]
    query_grad, keys_grad, values_grad = query_grad_ref[...], keys_grad_ref[...], values_grad_ref[...]
    first_low = low(normed_ref[...] * columns[:, 0:1] + columns[:, 1:2])
    pack(keep_ref, send_ref, held_ref, output_grad_ref[...], 3 * width, me, across)
    pack(keep_ref, send_ref, held_ref, dot(first_low, query_grad, NT), 0, me, across)
    pack(keep_ref, send_ref, held_ref, dot(memory_t_ref[...], keys_grad, NT), width, me, across)
    pack(keep_ref, send_ref, held_ref, dot(memory_t_ref[...], values_grad, NT), 2 * width, me, across)
    first_grad_ref[...] = part_grad_ref[...] + dot(maps_ref[0], query_grad, NN)
    memory_grad = dot(maps_ref[1], keys_grad, NN) + dot(maps_ref[2], values_grad, NN)
    own_ref[...] = memory_grad[:, :size]
    away_ref[...] = low(memory_grad[:, size:])
    stats_ref[...] = put_columns(
        stats_in_ref[...],
        [(3, over_tokens(wide(query_grad))), (4, over_tokens(wide(values_grad)))],
    )


def self_back_kernel(
    limit_ref, input_t_ref, normed_ref, scaled_ref, first_grad_ref, qkv_ref, mixed_ref, totals_ref,
    output_ref, gain_ref, omega_ref, stats_in_ref,
    part_grad_ref, incoming_ref, stats_ref, query_grad_ref, keys_grad_ref, values_grad_ref,
    keep_ref, send_ref, held_ref, *scratch, shift,
):
    me, _ = ranks(shift)
    columns = columns_of([gain_ref[0:1], omega_ref[0:1]])
    width, span = input_t_ref.shape
    sum_grad, gain_first, shift_first = normalize_back(
        first_grad_ref[...], normed_ref[...], scaled_ref[...], columns[:, 0:1]
    )
    part_grad_ref[...] = sum_grad * columns[:, 1:2]
    self_low = low(sum_grad)
    inputs = input_t_ref[...]
    stats_ref[...] = put_columns(
        stats_in_ref[...],
        [
            (2, over_tokens(wide(self_low))), (6, gain_first), (9, shift_first),
            (12, over_tokens(wide(inputs) * sum_grad)),
        ],
    )
    incoming_ref[...] = low(dot(output_ref[...], self_low, NN))
    position = lax.broadcasted_iota(jnp.int32, (1, span), 1)
    mask = jnp.where(position < limit_ref[0, 0], 0.0, far)
    attend_backward(
        qkv_ref.at[0:width], qkv_ref.at[width : 2 * width], qkv_ref.at[2 * width :],
        mixed_ref, totals_ref, incoming_ref, mask, True,
        query_grad_ref, keys_grad_ref, values_grad_ref, 0, HEADS // 2, scratch,
    )
    pack(keep_ref, send_ref, held_ref, dot(mixed_ref[...], self_low, NT), 3 * width // 2, me, None)
    pack_maps(
        keep_ref, send_ref, held_ref, inputs, (query_grad_ref, keys_grad_ref, values_grad_ref),
        slice(0, width // 2), me,
    )


def pack_maps(keep_ref, send_ref, held_ref, inputs, grads, rows, me):
    for at, ref in enumerate(grads):
        part = dot(inputs, ref[rows], NT)
        pack(keep_ref, send_ref, held_ref, part, at * part.shape[1], me, None)


def self_heads_kernel(
    limit_ref, qkv_ref, mixed_ref, totals_ref, incoming_ref,
    query_half_ref, keys_half_ref, values_half_ref,
    query_grad_ref, keys_grad_ref, values_grad_ref, *scratch,
):
    width, span = mixed_ref.shape
    position = lax.broadcasted_iota(jnp.int32, (1, span), 1)
    mask = jnp.where(position < limit_ref[0, 0], 0.0, far)
    attend_backward(
        qkv_ref.at[0:width], qkv_ref.at[width : 2 * width], qkv_ref.at[2 * width :],
        mixed_ref, totals_ref, incoming_ref, mask, True,
        query_grad_ref, keys_grad_ref, values_grad_ref, HEADS // 2, HEADS, scratch,
    )
    top = slice(0, width // 2)
    query_grad_ref[top] = query_half_ref[top]
    keys_grad_ref[top] = keys_half_ref[top]
    values_grad_ref[top] = values_half_ref[top]


def self_rest_kernel(
    input_t_ref, stats_in_ref, query_grad_ref, keys_grad_ref, values_grad_ref,
    keep_ref, send_ref, held_ref, *, shift,
):
    me, _ = ranks(shift)
    width = input_t_ref.shape[0]
    pack_maps(
        keep_ref, send_ref, held_ref, input_t_ref[...], (query_grad_ref, keys_grad_ref, values_grad_ref),
        slice(width // 2, width), me,
    )
    stats = put_columns(
        stats_in_ref[...],
        [(0, over_tokens(wide(query_grad_ref[...]))), (1, over_tokens(wide(values_grad_ref[...])))],
    )
    pack(keep_ref, send_ref, held_ref, stats, 3 * width // 2, me, None)


def input_kernel(
    part_grad_ref, query_grad_ref, keys_grad_ref, values_grad_ref, maps_ref, input_grad_ref, token_ref
):
    token_ref[...] = jnp.zeros(token_ref.shape, single)
    input_grad_ref[0, 0] = (
        part_grad_ref[...]
        + dot(maps_ref[0], query_grad_ref[...], NN)
        + dot(maps_ref[1], keys_grad_ref[...], NN)
        + dot(maps_ref[2], values_grad_ref[...], NN)
    ).T


def halve_kernel(kept_ref, arrived_ref, sent_out_ref, kept_out_ref):
    part = kept_ref.shape[0] // 2
    at = slice(part, None) if part > 1 else 1
    sent_out_ref[...] = low(wide(kept_ref[at]) + wide(arrived_ref[at]))
    at = slice(0, part) if part > 1 else 0
    kept_out_ref[...] = low(wide(kept_ref[at]) + wide(arrived_ref[at]))


def sum_kernel(kept_ref, arrived_ref, out_ref):
    out_ref[...] = low(wide(kept_ref[...]) + wide(arrived_ref[...]))


def memory_kernel(own_ref, returned_ref, rest_ref, out_ref, token_ref):
    token_ref[...] = jnp.zeros(token_ref.shape, single)
    half = lax.axis_index("half")
    out_ref[half, 0] = own_ref[...].T + rest_ref[half, 0]
    out_ref[1 - half, 0] = wide(returned_ref[...]).T + rest_ref[1 - half, 0]


def finish(ffn, cross, early, late, width):
    features = ffn.shape[1] // 2
    part = width // 2
    maps = [
        jnp.concatenate([v[:, i * part : (i + 1) * part] for v in (early, late)], axis=1)
        for i in range(3)
    ]
    cross_maps = [cross[:, i * width : (i + 1) * width] for i in range(3)]
    shrink = jnp.concatenate(
        [ffn[:, features + i * width : features + (i + 1) * width] for i in range(4)], axis=0
    )
    stats = late[:, 3 * part :].T
    return (
        maps, early[:, 3 * part :], cross_maps, cross[:, 3 * width :],
        stats[0:6], ffn[:, :features],
        jnp.concatenate([stats[16 + i : 17 + i] for i in range(4)], axis=1).reshape(-1), shrink,
        stats[15:16].reshape(-1), stats[6:9], stats[9:12], stats[12:15],
    )


def finish_kernel(*refs, shift):
    ins, outs, held = refs[:8], refs[8:-4], refs[-4:]
    half = lax.axis_index("half")
    width = outs[1].shape[1]
    for i in range(4):
        own, other = wide(ins[2 * i][...]), wide(ins[2 * i + 1][...])
        if shift or i >= 2:
            held[i][...] = own + other
        else:
            rows = own.shape[0]
            held[i][pl.ds(pl.multiple_of(half * rows, rows), rows)] = own
            held[i][pl.ds(pl.multiple_of((1 - half) * rows, rows), rows)] = other
    for ref, value in zip(outs, finish(*(ref[...] for ref in held), width)):
        if isinstance(value, list):
            for at, item in enumerate(value):
                ref[at] = item.reshape(ref.shape[1:])
        else:
            ref[...] = value


TIMES = {
    "self_forward": 9, "cross_forward": 13, "ffn": 20, "cross_back": 12, "cross_rest": 13,
    "self_back": 10, "self_heads": 7, "self_rest": 1, "input_grad": 3, "memory_grad": 2,
}
MICROSECOND = 1_000_000_000


def call(kernel, name, outs, scratch=(), specs=None, after=(), vmem=13, **options):
    def entry(*refs):
        kernel(*refs[len(after) :], **options)

    return lambda *args: pl.pallas_call(
        entry,
        name=name,
        out_shape=outs,
        in_specs=[pl.BlockSpec(memory_space=pl.ANY)] * len(after) + (specs or [VM] * len(args)),
        out_specs=jax.tree.map(lambda _: VM, outs),
        scratch_shapes=scratch,
        compiler_params=pltpu.CompilerParams(vmem_limit_bytes=vmem * 1024 * 1024),
        cost_estimate=pl.CostEstimate(
            flops=TIMES.get(name, 0) * MICROSECOND, bytes_accessed=1, transcendentals=0
        ),
    )(*after, *args)


def shards(
    block_input, memory, memory_grad_rest, output_grad, target_length, source_length,
    self_maps, self_output, cross_maps, cross_output, attention_bias,
    expand_weight, expand_bias, shrink_weight, shrink_bias, norm_gain, norm_bias, residual_scale,
    *, devices,
):
    span, width = block_input.shape[2:]
    size = memory.shape[2]
    source = 2 * size
    features = expand_weight.shape[1]
    shift = int(math.log2(devices // GROUPS))
    assert GROUPS << shift == devices
    rows = width // GROUPS
    half = lax.axis_index("half")

    def swap_half(value):
        return lax.ppermute(value, "half", [(0, 1), (1, 0)])

    def swap(value, bits):
        return lax.ppermute(value, "batch", [(i, i ^ bits) for i in range(devices)])

    def halve(kept, arrived, *after):
        part = kept.shape[0] // 2
        shape = kept.shape[1:] if part == 1 else (part, *kept.shape[1:])
        return call(halve_kernel, "halve", [sds(shape, bfloat)] * 2, after=after)(kept, arrived)

    def joined(kept, arrived, *after):
        return call(sum_kernel, "join", sds(kept.shape, bfloat), after=after)(kept, arrived)

    CORE, NEAR, NEXT, AWAY = 1, 2, 4, 8

    def scattered(keep, send, pieces=None):
        packet = jnp.stack([keep, send])
        if packet.ndim == 6:
            packet = packet.transpose(3, 1, 0, 2, 4, 5)
        else:
            packet = packet.transpose(2, 1, 0, 3, 4)
        packet = packet.reshape(2, 2, 4, rows, -1).swapaxes(0, 1)
        packet = packet.reshape(GROUPS, rows, -1)
        if pieces:
            start, stop = pieces
            part = packet[..., start:stop].reshape(GROUPS, rows, 4, -1).swapaxes(1, 2)
            part = part.reshape(GROUPS, 1 << shift, 4, rows >> shift, -1).swapaxes(2, 3)
            part = part.reshape(GROUPS, rows, stop - start)
            packet = jnp.concatenate([packet[..., :start], part, packet[..., stop:]], axis=-1)
        total = lax.psum_scatter(
            packet.reshape(width, -1), "batch", scatter_dimension=0, tiled=True
        )
        return total, swap_half(total)

    arrived = swap_half(lax.dynamic_index_in_dim(memory, 1 - half, 0, keepdims=False)[0])
    tall = sds((width, span), bfloat)
    tall_wide = sds((width, span), single)
    packet = lambda lanes: [sds((2, 2, 4, rows // 2, lanes), bfloat)] * 2
    simple = lambda lanes: [sds((2, 4, rows, lanes), bfloat)] * 2
    input_t, qkv = call(
        projection_kernel, "projections", [tall, sds((3 * width, span), bfloat)],
    )(block_input, self_maps, attention_bias)
    mixed, totals, normed, scaled = call(
        self_forward_kernel, "self_forward",
        [tall, sds((HEADS, span), single), tall_wide, sds((1, span), single)],
        specs=[SM] + [VM] * 5, scratch=forward_scratch(span),
    )(target_length, input_t, qkv, self_output, attention_bias, residual_scale)
    source_tall = sds((width, source), bfloat)
    (
        memory_t, query, keys, values, cross_mixed, cross_totals, second_normed, second_scaled,
    ) = call(
        cross_forward_kernel, "cross_forward",
        [source_tall, tall, source_tall, source_tall, tall, sds((HEADS, span), single),
         tall_wide, sds((1, span), single)],
        specs=[SM] + [VM] * 9, scratch=forward_scratch(span),
    )(
        source_length, normed, memory, arrived, cross_maps, cross_output, attention_bias,
        norm_gain, norm_bias, residual_scale,
    )
    layer_output, second_grad, stats, ffn_keep, ffn_send = call(
        ffn_kernel, "ffn",
        [sds((1, 1, span, width), single), tall_wide, sds((width, LANES), single)]
        + packet(2 * features),
        scratch=[pltpu.VMEM((features, span), bfloat)] * 2
        + [pltpu.VMEM((width, features), bfloat), pltpu.VMEM((features, width), bfloat)],
        shift=shift, vmem=31,
    )(
        second_normed, norm_gain, norm_bias, residual_scale, expand_weight,
        expand_bias, shrink_weight, shrink_bias, output_grad,
    )
    grads = [pltpu.VMEM((width, span), bfloat)] + [pltpu.VMEM((width, source), bfloat)] * 2
    held = pltpu.VMEM((width, width), bfloat)
    square = sds((width, width), bfloat)
    stats_shape = sds((width, LANES), single)
    part_grad, incoming, output_part, stats, *halves = call(
        cross_back_kernel, "cross_back",
        [tall_wide, tall, square, stats_shape, tall, source_tall, source_tall],
        specs=[SM] + [VM] * 14, scratch=backward_scratch(span),
    )(
        source_length, normed, second_normed, second_scaled, second_grad,
        query, keys, values, cross_mixed, cross_totals, cross_output,
        norm_gain, norm_bias, residual_scale, stats,
    )
    if not shift:
        ffn = halve(ffn_keep, swap(ffn_send, CORE), part_grad)
    first_grad, own, away, stats, cross_keep, cross_send = call(
        cross_rest_kernel, "cross_rest",
        [tall_wide, sds((width, size), single), sds((width, size), bfloat), stats_shape]
        + packet(4 * width),
        scratch=grads + [held] + backward_scratch(span), specs=[SM] + [VM] * 17, after=() if shift else ffn, shift=shift,
    )(
        source_length, normed, memory_t, query, keys, values, cross_mixed, cross_totals, cross_maps,
        norm_gain, norm_bias, part_grad, incoming, output_part, stats, *halves,
    )
    returned = swap_half(away)
    part_grad, incoming, stats, *rest_of = call(
        self_back_kernel, "self_back",
        [tall_wide, tall, stats_shape, tall, tall, tall] + simple(5 * width // 2),
        specs=[SM] + [VM] * 11, scratch=[held] + backward_scratch(span), shift=shift,
    )(
        target_length, input_t, normed, scaled, first_grad, qkv, mixed, totals,
        self_output, norm_gain, residual_scale, stats,
    )
    *halves, early_keep, early_send = rest_of
    before = ()
    if not shift:
        ffn = halve(ffn[1], swap(ffn[0], NEAR), stats, returned)
        cross = halve(cross_keep, swap(cross_send, CORE), *ffn)
        before = (*ffn, *cross)
    grads_out = call(
        self_heads_kernel, "self_heads", [tall] * 3, specs=[SM] + [VM] * 7,
        scratch=backward_scratch(span), after=before,
    )(target_length, qkv, mixed, totals, incoming, *halves)
    before = ()
    if not shift:
        early = halve(early_keep, swap(early_send, CORE), grads_out[0])
        before = early
    late_keep, late_send = call(
        self_rest_kernel, "self_rest", simple(3 * width // 2 + LANES),
        scratch=[held], after=before, shift=shift,
    )(input_t, stats, *grads_out)
    def to_memory(*after):
        return call(
            memory_kernel, "memory_grad",
            [sds(memory_grad_rest.shape, single), sds((8, LANES), single)], after=after,
        )(own, returned, memory_grad_rest)

    def to_input(*after):
        return call(
            input_kernel, "input_grad", [sds((1, 1, span, width), single), sds((8, LANES), single)],
            after=after,
        )(part_grad, *grads_out, self_maps)

    if shift:
        input_grad, _ = to_input()
        memory_grad, _ = to_memory()
        start = 3 * width // 2 + 16
        parts = (
            *scattered(ffn_keep, ffn_send, (features, 2 * features)),
            *scattered(cross_keep, cross_send),
            *scattered(early_keep, early_send),
            *scattered(late_keep, late_send, (start, start + 4)),
        )
    else:
        ffn = halve(ffn[1], swap_half(ffn[0]), late_keep)
        cross = halve(cross[1], swap(cross[0], NEAR), *ffn)
        late = halve(late_keep, swap(late_send, CORE), *cross)
        input_grad, token = to_input(*late)
        memory_grad, token = to_memory(token)
        early = halve(early[1], swap(early[0], NEAR), token)
        ffn = halve(ffn[1], swap(ffn[0], NEXT), *early)
        cross = halve(cross[1], swap_half(cross[0]), *ffn)
        late = halve(late[1], swap(late[0], NEAR), *cross)
        early = halve(early[1], swap(early[0], NEXT), *late)
        ffn = joined(ffn[1], swap(ffn[0], AWAY), *early)
        cross = halve(cross[1], swap(cross[0], NEXT), ffn)
        late = halve(late[1], swap(late[0], NEXT), *cross)
        early = joined(early[1], swap(early[0], AWAY), *late)
        cross = joined(cross[1], swap(cross[0], AWAY), early)
        late = joined(late[1], swap(late[0], AWAY), cross)
        parts = tuple(
            part for value in (ffn, cross, early, late) for part in (value, swap_half(value))
        )
    mine = rows >> shift
    outs = [
        sds((3, mine, width), single), sds((mine, width), single), sds((3, mine, width), single),
        sds((mine, width), single), sds((6, mine), single), sds((mine, features), single),
        sds((4 * mine,), single), sds((4 * mine, width), single), sds((mine,), single),
        sds((3, mine), single), sds((3, mine), single), sds((3, mine), single),
    ]
    done = list(
        call(
            finish_kernel, "finish", outs, shift=shift,
            scratch=[
                pltpu.VMEM((mine, lanes), single)
                for lanes in (2 * features, 4 * width, 5 * width // 2, 3 * width // 2 + LANES)
            ],
        )(*parts)
    )
    return (layer_output, input_grad, memory_grad, *done)


def solution(mesh):
    rows = P("half", "batch", None, None)
    sources = P(None, "batch", "half", None)
    placed = (rows, sources, sources, rows, P("half", "batch"), P("half", "batch")) + (P(),) * 12
    return jax.shard_map(
        partial(shards, devices=mesh.shape["batch"]),
        mesh=mesh,
        in_specs=placed,
        out_specs=(
            rows, rows, sources,
            P(None, "batch", None), P("batch", None), P(None, "batch", None), P("batch", None),
            P(None, "batch"), P("batch", None), P("batch"), P("batch", None), P("batch"),
            P(None, "batch"), P(None, "batch"), P(None, "batch"),
        ),
        check_vma=False,
    )
```

```python
from functools import partial
import math

import jax
import jax.numpy as jnp
from jax import lax
from jax.experimental import pallas as pl
from jax.experimental.pallas import tpu as pltpu
from jax.sharding import PartitionSpec as P

HEADS = 8
HEAD = 64
GROUPS = 16
LANES = 128
QUERY_BLOCK = 512
KEY_BLOCK = 256
ROW_BLOCK = 256

eps = 1e-05
bfloat = jnp.bfloat16
single = jnp.float32
scale = HEAD ** (-0.5)
to_log2 = math.log2(math.e) * scale
far = -1.5e9

NN = (((1,), (0,)), ((), ()))
NT = (((1,), (1,)), ((), ()))
TN = (((0,), (0,)), ((), ()))

VM = pl.BlockSpec(memory_space=pltpu.VMEM)
sds = jax.ShapeDtypeStruct


def dot(left, right, dims):
    return lax.dot_general(left, right, dims, preferred_element_type=single)


def low(value):
    return value.astype(bfloat)


def wide(value):
    return value.astype(single)


def split(value):
    high = low(value)
    return high, low(value - wide(high))


def split_three(value):
    high = low(value)
    rest = value - wide(high)
    middle = low(rest)
    return wide(high), wide(middle), wide(low(rest - wide(middle)))


def rows_of(rows, count=16):
    width = rows[0].shape[1]
    index = lax.broadcasted_iota(jnp.int32, (count, width), 0)
    out = jnp.zeros((count, width), single)
    for at, row in enumerate(rows):
        out = jnp.where(index == at, row, out)
    return out


def columns_of(rows):
    return rows_of(rows, -(-len(rows) // 8) * 8).T


def over_tokens(value):
    return jnp.sum(value, axis=1, keepdims=True)


def normalize(total):
    center = total - jnp.mean(total, axis=0, keepdims=True)
    spread = jnp.mean(center * center, axis=0, keepdims=True)
    scaled = lax.rsqrt(spread + eps)
    return center * scaled, scaled


def normalize_back(grad, normed, scaled, gain):
    inner = grad * gain
    back = scaled * (
        inner
        - jnp.mean(inner, axis=0, keepdims=True)
        - normed * jnp.mean(inner * normed, axis=0, keepdims=True)
    )
    return back, over_tokens(grad * normed), over_tokens(grad)


def put_columns(stats, items):
    lane = lax.broadcasted_iota(jnp.int32, stats.shape, 1)
    for at, column in items:
        stats = jnp.where(lane == at, column, stats)
    return stats


def places(me, half):
    for core in range(2):
        for near in range(2):
            for far_off in range(4):
                bits = core + 2 * near + 4 * (far_off // 2) + 8 * (far_off % 2)
                group = jnp.bitwise_xor(me, bits)
                if half is None:
                    yield core, (near, far_off), group, 0
                else:
                    for across in range(2):
                        yield core, (near, across, far_off), group, jnp.bitwise_xor(half, across)


def pack(keep_ref, send_ref, held_ref, grad, at, me, half):
    held_ref[:, : grad.shape[1]] = low(grad)
    rows = grad.shape[0] // GROUPS
    part = rows if half is None else rows // 2
    lanes = slice(at, at + grad.shape[1])
    for core, place, group, portion in places(me, half):
        start = pl.multiple_of(group * rows + portion * part, part)
        (send_ref if core else keep_ref)[(*place, slice(None), lanes)] = held_ref[
            pl.ds(start, part), : grad.shape[1]
        ]


def ranks(shift):
    return (0, 0) if shift else (lax.axis_index("batch"), lax.axis_index("half"))


def head_rows(head):
    return pl.ds(pl.multiple_of(head * HEAD, HEAD), HEAD)


def hide_later(scores, offset, query_axis):
    key_pos = lax.broadcasted_iota(jnp.int32, scores.shape, 1 - query_axis) + offset
    query_pos = lax.broadcasted_iota(jnp.int32, scores.shape, query_axis)
    return jnp.where(key_pos <= query_pos, scores, far)


def forward_scratch(span):
    return [
        pltpu.VMEM((2, span, QUERY_BLOCK), single),
        pltpu.VMEM((8, QUERY_BLOCK), single),
        pltpu.VMEM((2, 2 * HEAD + 16, span), bfloat),
        pltpu.VMEM((2, span, 2 * HEAD + 16), bfloat),
        pltpu.VMEM((3, HEAD + 16, span), bfloat),
    ]


def attend_forward(query_ref, keys_ref, values_ref, mask, is_causal, mixed_ref, totals_ref, scratch):
    scores_ref, top_ref, more_query_ref, more_keys_ref, more_values_ref = scratch
    span = query_ref.shape[1]
    blocks = span // QUERY_BLOCK
    ones = low(rows_of([jnp.ones((1, span), single)]))
    more_query_ref[0, 2 * HEAD :] = ones
    more_query_ref[1, 2 * HEAD :] = ones
    mask_column = low(rows_of([mask])).T
    more_keys_ref[0, :, 2 * HEAD :] = mask_column
    more_keys_ref[1, :, 2 * HEAD :] = mask_column
    for slot in range(3):
        more_values_ref[slot, HEAD:] = ones

    def key_blocks(block):
        return range(0, (block + 1) * QUERY_BLOCK if is_causal else span, KEY_BLOCK)

    def prepare(head, slot):
        rows = head_rows(head)
        high, rest = split(wide(query_ref[rows]) * to_log2)
        more_query_ref[slot, :HEAD] = high
        more_query_ref[slot, HEAD : 2 * HEAD] = rest
        keys = keys_ref[rows]
        more_keys_ref[slot, :, : 2 * HEAD] = jnp.concatenate([keys, keys], axis=0).T
        more_values_ref[lax.rem(head, 3), :HEAD] = values_ref[rows]

    def score(slot, block, key, top):
        at = slice(block * QUERY_BLOCK, (block + 1) * QUERY_BLOCK)
        scores = dot(more_keys_ref[slot, key : key + KEY_BLOCK], more_query_ref[slot, :, at], NN)
        if is_causal and key + KEY_BLOCK > block * QUERY_BLOCK:
            scores = hide_later(scores, key - block * QUERY_BLOCK, 1)
        scores_ref[block % 2, key : key + KEY_BLOCK] = scores
        part = jnp.max(scores.reshape(KEY_BLOCK // 8, 8, QUERY_BLOCK), axis=0)
        return part if top is None else jnp.maximum(top, part)

    def mix(head, block, key, top, total):
        expo = low(jnp.exp2(scores_ref[block % 2, key : key + KEY_BLOCK] - top))
        part = dot(more_values_ref[lax.rem(head, 3), :, key : key + KEY_BLOCK], expo, NN)
        return part if total is None else total + part

    def finish_block(head, block, top, total):
        at = slice(block * QUERY_BLOCK, (block + 1) * QUERY_BLOCK)
        summed = total[HEAD : HEAD + 1]
        mixed_ref[head_rows(head), at] = low(total[:HEAD] / summed)
        totals_ref[pl.ds(head, 1), at] = top + jnp.log2(summed)

    prepare(0, 0)
    last = blocks - 1

    def body(pair, carry):
        for odd in range(2):
            head = 2 * pair + odd
            for block in range(blocks):
                before, block_before = (head, block - 1) if block else (jnp.maximum(head - 1, 0), last)
                top_before = top_ref[block_before % 2 : block_before % 2 + 1]
                top = None
                total = None
                now, then = list(key_blocks(block)), list(key_blocks(block_before))
                for step in range(max(len(now), len(then))):
                    if step < len(now):
                        top = score(odd, block, now[step], top)
                    if step < len(then):
                        total = mix(before, block_before, then[step], top_before, total)
                top_ref[block % 2 : block % 2 + 1] = jnp.max(top, axis=0, keepdims=True)
                finish_block(before, block_before, top_before, total)
                if block == 0:
                    prepare(jnp.minimum(head + 1, HEADS - 1), 1 - odd)
        return carry

    lax.fori_loop(0, HEADS // 2, body, 0)
    top = top_ref[last % 2 : last % 2 + 1]
    total = None
    for key in key_blocks(last):
        total = mix(HEADS - 1, last, key, top, total)
    finish_block(HEADS - 1, last, top, total)


def backward_scratch(span):
    return (
        [pltpu.VMEM((2, span, KEY_BLOCK), bfloat)] * 2
        + [pltpu.VMEM((2, span, HEAD + 16), bfloat)] * 2
        + [pltpu.VMEM((2, HEAD + 16, span), bfloat)] * 2
        + [pltpu.VMEM((HEAD, span), single)]
    )


def attend_backward(
    query_ref, keys_ref, values_ref, mixed_ref, totals_ref, incoming_ref, mask, is_causal,
    query_grad_ref, keys_grad_ref, values_grad_ref, first_head, last_head, scratch, beside=None,
):
    probs_ref, score_grads_ref, more_query_ref, more_incoming_ref, more_keys_ref, more_values_ref, held_ref = scratch
    span = query_ref.shape[1]
    blocks = span // KEY_BLOCK
    ones = jnp.ones((1, span), single)
    for slot in range(2):
        more_keys_ref[slot, HEAD:] = low(rows_of([ones, ones, ones, mask]))
        more_values_ref[slot, HEAD:] = low(rows_of([ones, ones, ones]))

    def first_query(block):
        return block * KEY_BLOCK if is_causal else 0

    def prepare(head, slot):
        rows = head_rows(head)
        query, incoming = query_ref[rows], incoming_ref[rows]
        delta = jnp.sum(wide(incoming) * wide(mixed_ref[rows]), axis=0, keepdims=True)
        totals = split_three(totals_ref[pl.ds(head, 1), :] * (-1 / to_log2))
        more_query_ref[slot] = jnp.concatenate([query, low(rows_of([*totals, ones]))], axis=0).T
        more_incoming_ref[slot] = jnp.concatenate(
            [incoming, low(rows_of(split_three(-delta)))], axis=0
        ).T
        more_keys_ref[slot, :HEAD] = keys_ref[rows]
        more_values_ref[slot, :HEAD] = values_ref[rows]

    def score(slot, block, start):
        keys, rows = slice(block * KEY_BLOCK, (block + 1) * KEY_BLOCK), slice(start, start + ROW_BLOCK)
        scores = dot(more_query_ref[slot, rows], more_keys_ref[slot, :, keys], NN)
        if is_causal and start < (block + 1) * KEY_BLOCK:
            scores = hide_later(scores, block * KEY_BLOCK - start, 0)
        probs = jnp.exp2(scores * to_log2)
        prob_grad = dot(more_incoming_ref[slot, rows], more_values_ref[slot, :, keys], NN)
        probs_ref[block % 2, rows] = low(probs)
        score_grads_ref[block % 2, rows] = low(probs * prob_grad)

    def products(head, block):
        rows, keys = head_rows(head), slice(block * KEY_BLOCK, (block + 1) * KEY_BLOCK)
        start = first_query(block)

        def values_part():
            values_grad_ref[rows, keys] = low(
                dot(incoming_ref[rows, start:], probs_ref[block % 2, start:], NN)
            )

        def keys_part():
            keys_grad_ref[rows, keys] = low(
                dot(query_ref[rows, start:], score_grads_ref[block % 2, start:], NN) * scale
            )

        def query_part(at):
            stop = min(at + 2 * ROW_BLOCK, span)
            part = dot(keys_ref[rows, keys], score_grads_ref[block % 2, at:stop], NT)
            if block:
                part = part + held_ref[:, at:stop]
            held_ref[:, at:stop] = part

        def query_whole():
            query_grad_ref[rows] = low(held_ref[...] * scale)

        steps = [values_part, keys_part]
        steps += [partial(query_part, at) for at in range(start, span, 2 * ROW_BLOCK)]
        return steps + [query_whole] * (block == blocks - 1)

    prepare(first_head, 0)

    def body(pair, carry):
        for odd in range(2):
            head = first_head + 2 * pair + odd
            for block in range(blocks):
                if block:
                    steps = products(head, block - 1)
                else:
                    steps = products(jnp.maximum(head - 1, first_head), blocks - 1)
                starts = range(first_query(block), span, ROW_BLOCK)
                for step in range(max(len(starts), len(steps))):
                    if step < len(starts):
                        score(odd, block, starts[step])
                    if step < len(steps):
                        steps[step]()
                if block == 0:
                    prepare(jnp.minimum(head + 1, last_head - 1), 1 - odd)
                if beside:
                    beside((2 * pair + odd) * blocks + block, (last_head - first_head) * blocks)
        return carry

    lax.fori_loop(0, (last_head - first_head) // 2, body, 0)
    for step in products(last_head - 1, blocks - 1):
        step()


ROOT = math.sqrt(2 / math.pi)
CUBE = ROOT * 0.044715


def gelu_parts(value):
    half = 0.5 * value
    cube = CUBE * (value * value)
    tanh = jnp.tanh(value * (ROOT + cube))
    more = 1 + tanh
    return half * more, more * (0.5 + (1 - tanh) * (half * (ROOT + 3 * cube)))


def opening_kernel(token_ref):
    token_ref[...] = jnp.zeros(token_ref.shape, single)


def projection_kernel(input_ref, maps_ref, bias_ref, input_t_ref, qkv_ref):
    columns = columns_of([bias_ref[0:1], bias_ref[1:2]])
    inputs = input_ref[0, 0].T
    input_t_ref[...] = inputs
    width = inputs.shape[0]
    qkv_ref[0:width] = low(dot(maps_ref[0], inputs, TN) + columns[:, 0:1])
    qkv_ref[width : 2 * width] = low(dot(maps_ref[1], inputs, TN))
    qkv_ref[2 * width :] = low(dot(maps_ref[2], inputs, TN) + columns[:, 1:2])


def self_forward_kernel(
    limit_ref, input_t_ref, qkv_ref, output_ref, bias_ref, omega_ref,
    mixed_ref, totals_ref, normed_ref, scaled_ref, *scratch,
):
    columns = columns_of([bias_ref[2:3], omega_ref[0:1]])
    width, span = input_t_ref.shape
    position = lax.broadcasted_iota(jnp.int32, (1, span), 1)
    mask = jnp.where(wide(position) < limit_ref[0:1, 0:1], 0.0, far)
    attend_forward(
        qkv_ref.at[0:width], qkv_ref.at[width : 2 * width], qkv_ref.at[2 * width :],
        mask, True, mixed_ref, totals_ref, scratch,
    )
    branch = dot(output_ref[...], mixed_ref[...], TN) + columns[:, 0:1]
    normed, scaled = normalize(wide(input_t_ref[...]) * columns[:, 1:2] + branch)
    normed_ref[...] = normed
    scaled_ref[...] = scaled


def source_mask(limit, half, size):
    local = lax.broadcasted_iota(jnp.int32, (1, 2 * size), 1)
    own = local < size
    position = jnp.where(own, local + half * size, local - size + (1 - half) * size)
    return jnp.where(wide(position) < limit, 0.0, far)


def cross_forward_kernel(
    limit_ref, normed_ref, memory_ref, arrived_ref, maps_ref, output_ref, bias_ref,
    gain_ref, shift_ref, omega_ref,
    memory_t_ref, query_ref, keys_ref, values_ref, mixed_ref, totals_ref,
    second_normed_ref, second_scaled_ref, *scratch,
):
    half = lax.axis_index("half")
    columns = columns_of(
        [bias_ref[3:4], bias_ref[4:5], bias_ref[5:6], gain_ref[0:1], shift_ref[0:1], omega_ref[1:2]]
    )
    size = memory_ref.shape[2]
    first = normed_ref[...] * columns[:, 3:4] + columns[:, 4:5]
    query_ref[...] = low(dot(maps_ref[0], low(first), TN) + columns[:, 0:1])
    memory_t_ref[:, :size] = memory_ref[half, 0].T
    memory_t_ref[:, size:] = arrived_ref[...].T
    keys_ref[...] = low(dot(maps_ref[1], memory_t_ref[...], TN))
    values_ref[...] = low(dot(maps_ref[2], memory_t_ref[...], TN) + columns[:, 1:2])
    mask = source_mask(limit_ref[1:2, 0:1], half, size)
    attend_forward(query_ref, keys_ref, values_ref, mask, False, mixed_ref, totals_ref, scratch)
    branch = dot(output_ref[...], mixed_ref[...], TN) + columns[:, 2:3]
    second_normed, second_scaled = normalize(first * columns[:, 5:6] + branch)
    second_normed_ref[...] = second_normed
    second_scaled_ref[...] = second_scaled


def ffn_kernel(
    second_normed_ref, gain_ref, shift_ref, omega_ref, expand_ref, expand_bias_ref, shrink_ref,
    shrink_bias_ref, grad_ref,
    layer_ref, back_ref, stats_ref, keep_ref, send_ref,
    hidden_ref, slope_ref, held_ref, wide_held_ref,
    *, shift,
):
    me, half = ranks(shift)
    columns = columns_of(
        [gain_ref[1:2], gain_ref[2:3], shift_ref[1:2], shift_ref[2:3], omega_ref[2:3]]
        + [shrink_bias_ref[...].reshape(1, -1)]
        + [expand_bias_ref[i : i + 512].reshape(1, -1) for i in range(0, expand_ref.shape[1], 512)]
    )
    width, span = second_normed_ref.shape
    second = second_normed_ref[...] * columns[:, 0:1] + columns[:, 2:3]
    second_low = low(second)
    features = expand_ref.shape[1]
    chunk = 512
    ffn = None
    for at in range(0, features, chunk):
        part = slice(at, at + chunk)
        pre = dot(expand_ref[:, part], second_low, TN) + columns[:, 6 + at // chunk : 7 + at // chunk]
        value, slope = gelu_parts(pre)
        hidden_ref[part] = low(value)
        slope_ref[part] = low(slope)
        term = dot(shrink_ref[part], hidden_ref[part], TN)
        ffn = term if ffn is None else ffn + term
    third_normed, third_scaled = normalize(second * columns[:, 4:5] + (ffn + columns[:, 5:6]))
    layer_ref[0, 0] = (third_normed * columns[:, 1:2] + columns[:, 3:4]).T
    grad = wide(grad_ref[0, 0].T)
    third_grad, gain_third, shift_third = normalize_back(
        grad, third_normed, third_scaled, columns[:, 1:2]
    )
    scale_third = over_tokens(second * third_grad)
    ffn_low = low(third_grad)
    shrink_bias_grad = over_tokens(wide(ffn_low))
    second_grad = third_grad * columns[:, 4:5]
    sums = []
    for at in range(0, features, chunk):
        part = slice(at, at + chunk)
        wide_held_ref[part] = low(dot(hidden_ref[part], ffn_low, NT))
        pre_grad = low(dot(shrink_ref[part], ffn_low, NN) * wide(slope_ref[part]))
        sums.append(over_tokens(wide(pre_grad)))
        held_ref[:, part] = low(dot(second_low, pre_grad, NT))
        second_grad = second_grad + dot(expand_ref[:, part], pre_grad, NN)
    back_ref[...] = second_grad
    rows = features // GROUPS // 4
    for core, place, group, portion in places(me, half):
        out = send_ref if core else keep_ref
        start = pl.multiple_of(group * rows + portion * (rows // 2), rows // 2)
        out[(*place, slice(None), slice(0, features))] = held_ref[pl.ds(start, rows // 2), :]
        for piece in range(4):
            start = (4 * group + piece) * rows + portion * (rows // 2)
            lanes = slice(features + piece * width, features + (piece + 1) * width)
            out[(*place, slice(None), lanes)] = wide_held_ref[
                pl.ds(pl.multiple_of(start, rows // 2), rows // 2), :
            ]
    expand_sums = jnp.concatenate(sums, axis=0)
    pieces = [
        jnp.concatenate(
            [
                expand_sums[(4 * group + piece) * rows : (4 * group + piece + 1) * rows]
                for group in range(GROUPS)
            ],
            axis=0,
        )
        for piece in range(4)
    ]
    stats_ref[...] = put_columns(
        jnp.zeros(stats_ref.shape, single),
        [(8, gain_third), (11, shift_third), (14, scale_third), (15, shrink_bias_grad)]
        + [(16 + piece, pieces[piece]) for piece in range(4)],
    )


def norm_grad(grad, normed, scaled, gain):
    inner = grad * gain
    return scaled * (
        inner
        - jnp.mean(inner, axis=0, keepdims=True)
        - normed * jnp.mean(inner * normed, axis=0, keepdims=True)
    )


def sums_scratch(width):
    return [pltpu.VMEM((width, 8), single), pltpu.VMEM((4, width, 1), single)]


def norm_sums(grad_ref, normed_ref, back_ref, input_of, columns_ref, omega, sums_ref):
    def some(step, steps):
        size = back_ref.shape[0] // steps
        rows = pl.ds(pl.multiple_of(step * size, size), size)
        grad, back = grad_ref[rows], back_ref[rows]
        sums_ref[0, rows] = over_tokens(grad * normed_ref[rows])
        sums_ref[1, rows] = over_tokens(grad)
        sums_ref[2, rows] = over_tokens(input_of(rows) * back)
        sums_ref[3, rows] = over_tokens(wide(low(back)))
        back_ref[rows] = back * columns_ref[rows, omega : omega + 1]

    return some


def cross_back_kernel(
    limit_ref, normed_ref, second_normed_ref, second_scaled_ref, back_ref,
    query_ref, keys_ref, values_ref, mixed_ref, totals_ref, output_ref,
    gain_ref, shift_ref, omega_ref, stats_in_ref,
    part_grad_ref, incoming_ref, output_grad_ref, stats_ref,
    query_grad_ref, keys_grad_ref, values_grad_ref, *scratch,
):
    half = lax.axis_index("half")
    columns = columns_of([gain_ref[0:1], shift_ref[0:1], gain_ref[1:2], omega_ref[1:2]])
    size = keys_ref.shape[1] // 2
    *scratch, columns_ref, sums_ref = scratch
    columns_ref[...] = columns
    sum_grad = norm_grad(
        back_ref[...], second_normed_ref[...], second_scaled_ref[...], columns[:, 2:3]
    )
    part_grad_ref[...] = sum_grad
    cross_low = low(sum_grad)
    incoming_ref[...] = low(dot(output_ref[...], cross_low, NN))
    output_grad_ref[...] = low(dot(mixed_ref[...], cross_low, NT))
    mask = source_mask(limit_ref[1:2, 0:1], half, size)

    def first_of(rows):
        return normed_ref[rows] * columns_ref[rows, 0:1] + columns_ref[rows, 1:2]

    attend_backward(
        query_ref, keys_ref, values_ref, mixed_ref, totals_ref, incoming_ref, mask, False,
        query_grad_ref, keys_grad_ref, values_grad_ref, 0, HEADS // 2, scratch,
        norm_sums(back_ref, second_normed_ref, part_grad_ref, first_of, columns_ref, 3, sums_ref),
    )
    stats_ref[...] = put_columns(
        stats_in_ref[...], [(7, sums_ref[0]), (10, sums_ref[1]), (13, sums_ref[2]), (5, sums_ref[3])]
    )


def cross_rest_kernel(
    limit_ref, normed_ref, memory_t_ref, query_ref, keys_ref, values_ref, mixed_ref, totals_ref,
    maps_ref, gain_ref, shift_ref, part_grad_ref, incoming_ref, output_grad_ref, stats_in_ref,
    query_half_ref, keys_half_ref, values_half_ref,
    first_grad_ref, own_ref, away_ref, stats_ref, keep_ref, send_ref,
    query_grad_ref, keys_grad_ref, values_grad_ref, held_ref, *scratch, shift,
):
    me, across = ranks(shift)
    columns = columns_of([gain_ref[0:1], shift_ref[0:1]])
    size = own_ref.shape[1]
    width = normed_ref.shape[0]
    mask = source_mask(limit_ref[1:2, 0:1], lax.axis_index("half"), size)
    attend_backward(
        query_ref, keys_ref, values_ref, mixed_ref, totals_ref, incoming_ref, mask, False,
        query_grad_ref, keys_grad_ref, values_grad_ref, HEADS // 2, HEADS, scratch,
    )
    top = slice(0, width // 2)
    query_grad_ref[top] = query_half_ref[top]
    keys_grad_ref[top] = keys_half_ref[top]
    values_grad_ref[top] = values_half_ref[top]
    query_grad, keys_grad, values_grad = query_grad_ref[...], keys_grad_ref[...], values_grad_ref[...]
    first_low = low(normed_ref[...] * columns[:, 0:1] + columns[:, 1:2])
    pack(keep_ref, send_ref, held_ref, output_grad_ref[...], 3 * width, me, across)
    pack(keep_ref, send_ref, held_ref, dot(first_low, query_grad, NT), 0, me, across)
    pack(keep_ref, send_ref, held_ref, dot(memory_t_ref[...], keys_grad, NT), width, me, across)
    pack(keep_ref, send_ref, held_ref, dot(memory_t_ref[...], values_grad, NT), 2 * width, me, across)
    first_grad_ref[...] = part_grad_ref[...] + dot(maps_ref[0], query_grad, NN)
    memory_grad = dot(maps_ref[1], keys_grad, NN) + dot(maps_ref[2], values_grad, NN)
    own_ref[...] = memory_grad[:, :size]
    away_ref[...] = low(memory_grad[:, size:])
    stats_ref[...] = put_columns(
        stats_in_ref[...],
        [(3, over_tokens(wide(query_grad))), (4, over_tokens(wide(values_grad)))],
    )


def self_back_kernel(
    limit_ref, input_t_ref, normed_ref, scaled_ref, first_grad_ref, qkv_ref, mixed_ref, totals_ref,
    output_ref, gain_ref, omega_ref, stats_in_ref,
    part_grad_ref, incoming_ref, stats_ref, query_grad_ref, keys_grad_ref, values_grad_ref,
    keep_ref, send_ref, held_ref, *scratch, shift,
):
    me, _ = ranks(shift)
    columns = columns_of([gain_ref[0:1], omega_ref[0:1]])
    *scratch, columns_ref, sums_ref = scratch
    columns_ref[...] = columns
    width, span = input_t_ref.shape
    sum_grad = norm_grad(first_grad_ref[...], normed_ref[...], scaled_ref[...], columns[:, 0:1])
    part_grad_ref[...] = sum_grad
    self_low = low(sum_grad)
    inputs = input_t_ref[...]
    incoming_ref[...] = low(dot(output_ref[...], self_low, NN))
    output_grad = dot(mixed_ref[...], self_low, NT)
    position = lax.broadcasted_iota(jnp.int32, (1, span), 1)
    mask = jnp.where(wide(position) < limit_ref[0:1, 0:1], 0.0, far)
    attend_backward(
        qkv_ref.at[0:width], qkv_ref.at[width : 2 * width], qkv_ref.at[2 * width :],
        mixed_ref, totals_ref, incoming_ref, mask, True,
        query_grad_ref, keys_grad_ref, values_grad_ref, 0, HEADS // 2, scratch,
        norm_sums(
            first_grad_ref, normed_ref, part_grad_ref, lambda rows: wide(input_t_ref[rows]),
            columns_ref, 1, sums_ref,
        ),
    )
    stats_ref[...] = put_columns(
        stats_in_ref[...], [(6, sums_ref[0]), (9, sums_ref[1]), (12, sums_ref[2]), (2, sums_ref[3])]
    )
    pack(keep_ref, send_ref, held_ref, output_grad, 3 * width // 2, me, None)
    pack_maps(
        keep_ref, send_ref, held_ref, inputs, (query_grad_ref, keys_grad_ref, values_grad_ref),
        slice(0, width // 2), me,
    )


def pack_maps(keep_ref, send_ref, held_ref, inputs, grads, rows, me):
    for at, ref in enumerate(grads):
        part = dot(inputs, ref[rows], NT)
        pack(keep_ref, send_ref, held_ref, part, at * part.shape[1], me, None)


def self_heads_kernel(
    limit_ref, qkv_ref, mixed_ref, totals_ref, incoming_ref,
    query_half_ref, keys_half_ref, values_half_ref,
    query_grad_ref, keys_grad_ref, values_grad_ref, *scratch,
):
    width, span = mixed_ref.shape
    position = lax.broadcasted_iota(jnp.int32, (1, span), 1)
    mask = jnp.where(wide(position) < limit_ref[0:1, 0:1], 0.0, far)
    attend_backward(
        qkv_ref.at[0:width], qkv_ref.at[width : 2 * width], qkv_ref.at[2 * width :],
        mixed_ref, totals_ref, incoming_ref, mask, True,
        query_grad_ref, keys_grad_ref, values_grad_ref, HEADS // 2, HEADS, scratch,
    )
    top = slice(0, width // 2)
    query_grad_ref[top] = query_half_ref[top]
    keys_grad_ref[top] = keys_half_ref[top]
    values_grad_ref[top] = values_half_ref[top]


def self_rest_kernel(
    input_t_ref, stats_in_ref, query_grad_ref, keys_grad_ref, values_grad_ref,
    keep_ref, send_ref, held_ref, *, shift,
):
    me, _ = ranks(shift)
    width = input_t_ref.shape[0]
    pack_maps(
        keep_ref, send_ref, held_ref, input_t_ref[...], (query_grad_ref, keys_grad_ref, values_grad_ref),
        slice(width // 2, width), me,
    )
    stats = put_columns(
        stats_in_ref[...],
        [(0, over_tokens(wide(query_grad_ref[...]))), (1, over_tokens(wide(values_grad_ref[...])))],
    )
    pack(keep_ref, send_ref, held_ref, stats, 3 * width // 2, me, None)


def input_kernel(
    part_grad_ref, query_grad_ref, keys_grad_ref, values_grad_ref, maps_ref, input_grad_ref, token_ref
):
    token_ref[...] = jnp.zeros(token_ref.shape, single)
    input_grad_ref[0, 0] = (
        part_grad_ref[...]
        + dot(maps_ref[0], query_grad_ref[...], NN)
        + dot(maps_ref[1], keys_grad_ref[...], NN)
        + dot(maps_ref[2], values_grad_ref[...], NN)
    ).T


def halve_kernel(kept_ref, arrived_ref, sent_out_ref, kept_out_ref):
    part = kept_ref.shape[0] // 2
    at = slice(part, None) if part > 1 else 1
    sent_out_ref[...] = low(wide(kept_ref[at]) + wide(arrived_ref[at]))
    at = slice(0, part) if part > 1 else 0
    kept_out_ref[...] = low(wide(kept_ref[at]) + wide(arrived_ref[at]))


def sum_kernel(kept_ref, arrived_ref, out_ref):
    out_ref[...] = low(wide(kept_ref[...]) + wide(arrived_ref[...]))


def memory_kernel(own_ref, returned_ref, rest_ref, out_ref, token_ref):
    token_ref[...] = jnp.zeros(token_ref.shape, single)
    half = lax.axis_index("half")
    out_ref[half, 0] = own_ref[...].T + rest_ref[half, 0]
    out_ref[1 - half, 0] = wide(returned_ref[...]).T + rest_ref[1 - half, 0]


def finish(ffn, cross, early, late, width):
    features = ffn.shape[1] // 2
    part = width // 2
    maps = [
        jnp.concatenate([v[:, i * part : (i + 1) * part] for v in (early, late)], axis=1)
        for i in range(3)
    ]
    cross_maps = [cross[:, i * width : (i + 1) * width] for i in range(3)]
    shrink = jnp.concatenate(
        [ffn[:, features + i * width : features + (i + 1) * width] for i in range(4)], axis=0
    )
    stats = late[:, 3 * part :].T
    return (
        maps, early[:, 3 * part :], cross_maps, cross[:, 3 * width :],
        stats[0:6], ffn[:, :features],
        jnp.concatenate([stats[16 + i : 17 + i] for i in range(4)], axis=1).reshape(-1), shrink,
        stats[15:16].reshape(-1), stats[6:9], stats[9:12], stats[12:15],
    )


def finish_kernel(*refs, shift):
    ins, outs, held = refs[:8], refs[8:-4], refs[-4:]
    half = lax.axis_index("half")
    width = outs[1].shape[1]
    for i in range(4):
        own, other = wide(ins[2 * i][...]), wide(ins[2 * i + 1][...])
        if shift or i >= 2:
            held[i][...] = own + other
        else:
            rows = own.shape[0]
            held[i][pl.ds(pl.multiple_of(half * rows, rows), rows)] = own
            held[i][pl.ds(pl.multiple_of((1 - half) * rows, rows), rows)] = other
    for ref, value in zip(outs, finish(*(ref[...] for ref in held), width)):
        if isinstance(value, list):
            for at, item in enumerate(value):
                ref[at] = item.reshape(ref.shape[1:])
        else:
            ref[...] = value


TIMES = {
    "opening": 6, "self_forward": 9, "cross_forward": 13, "ffn": 20, "cross_back": 12, "cross_rest": 13,
    "self_back": 10, "self_heads": 7, "self_rest": 1, "input_grad": 3, "memory_grad": 2,
}
MICROSECOND = 1_000_000_000


def call(kernel, name, outs, scratch=(), after=(), vmem=13, **options):
    def entry(*refs):
        kernel(*refs[len(after) :], **options)

    return lambda *args: pl.pallas_call(
        entry,
        name=name,
        out_shape=outs,
        in_specs=[pl.BlockSpec(memory_space=pl.ANY)] * len(after) + [VM] * len(args),
        out_specs=jax.tree.map(lambda _: VM, outs),
        scratch_shapes=scratch,
        compiler_params=pltpu.CompilerParams(vmem_limit_bytes=vmem * 1024 * 1024),
        cost_estimate=pl.CostEstimate(
            flops=TIMES.get(name, 0) * MICROSECOND, bytes_accessed=1, transcendentals=0
        ),
    )(*after, *args)


def shards(
    block_input, memory, memory_grad_rest, output_grad, target_length, source_length,
    self_maps, self_output, cross_maps, cross_output, attention_bias,
    expand_weight, expand_bias, shrink_weight, shrink_bias, norm_gain, norm_bias, residual_scale,
    *, devices,
):
    span, width = block_input.shape[2:]
    size = memory.shape[2]
    source = 2 * size
    features = expand_weight.shape[1]
    shift = int(math.log2(devices // GROUPS))
    assert GROUPS << shift == devices
    rows = width // GROUPS
    half = lax.axis_index("half")

    def swap_half(value):
        return lax.ppermute(value, "half", [(0, 1), (1, 0)])

    def swap(value, bits):
        return lax.ppermute(value, "batch", [(i, i ^ bits) for i in range(devices)])

    def halve(kept, arrived, *after):
        part = kept.shape[0] // 2
        shape = kept.shape[1:] if part == 1 else (part, *kept.shape[1:])
        return call(halve_kernel, "halve", [sds(shape, bfloat)] * 2, after=after)(kept, arrived)

    def joined(kept, arrived, *after):
        return call(sum_kernel, "join", sds(kept.shape, bfloat), after=after)(kept, arrived)

    CORE, NEAR, NEXT, AWAY = 1, 2, 4, 8

    def scattered(keep, send, pieces=None):
        packet = jnp.stack([keep, send])
        if packet.ndim == 6:
            packet = packet.transpose(3, 1, 0, 2, 4, 5)
        else:
            packet = packet.transpose(2, 1, 0, 3, 4)
        packet = packet.reshape(2, 2, 4, rows, -1).swapaxes(0, 1)
        packet = packet.reshape(GROUPS, rows, -1)
        if pieces:
            start, stop = pieces
            part = packet[..., start:stop].reshape(GROUPS, rows, 4, -1).swapaxes(1, 2)
            part = part.reshape(GROUPS, 1 << shift, 4, rows >> shift, -1).swapaxes(2, 3)
            part = part.reshape(GROUPS, rows, stop - start)
            packet = jnp.concatenate([packet[..., :start], part, packet[..., stop:]], axis=-1)
        total = lax.psum_scatter(
            packet.reshape(width, -1), "batch", scatter_dimension=0, tiled=True
        )
        return total, swap_half(total)

    arrived = swap_half(lax.dynamic_index_in_dim(memory, 1 - half, 0, keepdims=False)[0])
    tall = sds((width, span), bfloat)
    tall_wide = sds((width, span), single)
    packet = lambda lanes: [sds((2, 2, 4, rows // 2, lanes), bfloat)] * 2
    simple = lambda lanes: [sds((2, 4, rows, lanes), bfloat)] * 2
    limits = jnp.broadcast_to(
        jnp.concatenate([target_length, source_length]).astype(single), (2, LANES)
    )
    opening = call(opening_kernel, "opening", sds((8, LANES), single))()
    input_t, qkv = call(
        projection_kernel, "projections", [tall, sds((3 * width, span), bfloat)], after=(opening,),
    )(block_input, self_maps, attention_bias)
    mixed, totals, normed, scaled = call(
        self_forward_kernel, "self_forward",
        [tall, sds((HEADS, span), single), tall_wide, sds((1, span), single)],
        scratch=forward_scratch(span),
    )(limits, input_t, qkv, self_output, attention_bias, residual_scale)
    source_tall = sds((width, source), bfloat)
    (
        memory_t, query, keys, values, cross_mixed, cross_totals, second_normed, second_scaled,
    ) = call(
        cross_forward_kernel, "cross_forward",
        [source_tall, tall, source_tall, source_tall, tall, sds((HEADS, span), single),
         tall_wide, sds((1, span), single)],
        scratch=forward_scratch(span),
    )(
        limits, normed, memory, arrived, cross_maps, cross_output, attention_bias,
        norm_gain, norm_bias, residual_scale,
    )
    layer_output, second_grad, stats, ffn_keep, ffn_send = call(
        ffn_kernel, "ffn",
        [sds((1, 1, span, width), single), tall_wide, sds((width, LANES), single)]
        + packet(2 * features),
        scratch=[pltpu.VMEM((features, span), bfloat)] * 2
        + [pltpu.VMEM((width, features), bfloat), pltpu.VMEM((features, width), bfloat)],
        shift=shift, vmem=31,
    )(
        second_normed, norm_gain, norm_bias, residual_scale, expand_weight,
        expand_bias, shrink_weight, shrink_bias, output_grad,
    )
    grads = [pltpu.VMEM((width, span), bfloat)] + [pltpu.VMEM((width, source), bfloat)] * 2
    held = pltpu.VMEM((width, width), bfloat)
    square = sds((width, width), bfloat)
    stats_shape = sds((width, LANES), single)
    part_grad, incoming, output_part, stats, *halves = call(
        cross_back_kernel, "cross_back",
        [tall_wide, tall, square, stats_shape, tall, source_tall, source_tall],
        scratch=backward_scratch(span) + sums_scratch(width),
    )(
        limits, normed, second_normed, second_scaled, second_grad,
        query, keys, values, cross_mixed, cross_totals, cross_output,
        norm_gain, norm_bias, residual_scale, stats,
    )
    if not shift:
        ffn = halve(ffn_keep, swap(ffn_send, CORE), part_grad)
    first_grad, own, away, stats, cross_keep, cross_send = call(
        cross_rest_kernel, "cross_rest",
        [tall_wide, sds((width, size), single), sds((width, size), bfloat), stats_shape]
        + packet(4 * width),
        scratch=grads + [held] + backward_scratch(span), after=() if shift else ffn, shift=shift,
    )(
        limits, normed, memory_t, query, keys, values, cross_mixed, cross_totals, cross_maps,
        norm_gain, norm_bias, part_grad, incoming, output_part, stats, *halves,
    )
    returned = swap_half(away)
    part_grad, incoming, stats, *rest_of = call(
        self_back_kernel, "self_back",
        [tall_wide, tall, stats_shape, tall, tall, tall] + simple(5 * width // 2),
        scratch=[held] + backward_scratch(span) + sums_scratch(width),
        shift=shift,
    )(
        limits, input_t, normed, scaled, first_grad, qkv, mixed, totals,
        self_output, norm_gain, residual_scale, stats,
    )
    *halves, early_keep, early_send = rest_of
    before = ()
    if not shift:
        ffn = halve(ffn[1], swap(ffn[0], NEAR), stats, returned)
        cross = halve(cross_keep, swap(cross_send, CORE), *ffn)
        before = (*ffn, *cross)
    grads_out = call(
        self_heads_kernel, "self_heads", [tall] * 3,
        scratch=backward_scratch(span), after=before,
    )(limits, qkv, mixed, totals, incoming, *halves)
    before = ()
    if not shift:
        early = halve(early_keep, swap(early_send, CORE), grads_out[0])
        before = early
    late_keep, late_send = call(
        self_rest_kernel, "self_rest", simple(3 * width // 2 + LANES),
        scratch=[held], after=before, shift=shift,
    )(input_t, stats, *grads_out)
    def to_memory(*after):
        return call(
            memory_kernel, "memory_grad",
            [sds(memory_grad_rest.shape, single), sds((8, LANES), single)], after=after,
        )(own, returned, memory_grad_rest)

    def to_input(*after):
        return call(
            input_kernel, "input_grad", [sds((1, 1, span, width), single), sds((8, LANES), single)],
            after=after,
        )(part_grad, *grads_out, self_maps)

    if shift:
        input_grad, _ = to_input()
        memory_grad, _ = to_memory()
        start = 3 * width // 2 + 16
        parts = (
            *scattered(ffn_keep, ffn_send, (features, 2 * features)),
            *scattered(cross_keep, cross_send),
            *scattered(early_keep, early_send),
            *scattered(late_keep, late_send, (start, start + 4)),
        )
    else:
        ffn = halve(ffn[1], swap_half(ffn[0]), late_keep)
        cross = halve(cross[1], swap(cross[0], NEAR), *ffn)
        late = halve(late_keep, swap(late_send, CORE), *cross)
        input_grad, token = to_input(*late)
        memory_grad, token = to_memory(token)
        early = halve(early[1], swap(early[0], NEAR), token)
        ffn = halve(ffn[1], swap(ffn[0], NEXT), *early)
        cross = halve(cross[1], swap_half(cross[0]), *ffn)
        late = halve(late[1], swap(late[0], NEAR), *cross)
        early = halve(early[1], swap(early[0], NEXT), *late)
        ffn = joined(ffn[1], swap(ffn[0], AWAY), *early)
        cross = halve(cross[1], swap(cross[0], NEXT), ffn)
        late = halve(late[1], swap(late[0], NEXT), *cross)
        early = joined(early[1], swap(early[0], AWAY), *late)
        cross = joined(cross[1], swap(cross[0], AWAY), early)
        late = joined(late[1], swap(late[0], AWAY), cross)
        parts = tuple(
            part for value in (ffn, cross, early, late) for part in (value, swap_half(value))
        )
    mine = rows >> shift
    outs = [
        sds((3, mine, width), single), sds((mine, width), single), sds((3, mine, width), single),
        sds((mine, width), single), sds((6, mine), single), sds((mine, features), single),
        sds((4 * mine,), single), sds((4 * mine, width), single), sds((mine,), single),
        sds((3, mine), single), sds((3, mine), single), sds((3, mine), single),
    ]
    done = list(
        call(
            finish_kernel, "finish", outs, shift=shift,
            scratch=[
                pltpu.VMEM((mine, lanes), single)
                for lanes in (2 * features, 4 * width, 5 * width // 2, 3 * width // 2 + LANES)
            ],
        )(*parts)
    )
    return (layer_output, input_grad, memory_grad, *done)


def solution(mesh):
    rows = P("half", "batch", None, None)
    sources = P(None, "batch", "half", None)
    placed = (rows, sources, sources, rows, P("half", "batch"), P("half", "batch")) + (P(),) * 12
    return jax.shard_map(
        partial(shards, devices=mesh.shape["batch"]),
        mesh=mesh,
        in_specs=placed,
        out_specs=(
            rows, rows, sources,
            P(None, "batch", None), P("batch", None), P(None, "batch", None), P("batch", None),
            P(None, "batch"), P("batch", None), P("batch"), P("batch", None), P("batch"),
            P(None, "batch"), P(None, "batch"), P(None, "batch"),
        ),
        check_vma=False,
    )
```

```python
from functools import partial
import math

import jax
import jax.numpy as jnp
from jax import lax
from jax.experimental import pallas as pl
from jax.experimental.pallas import tpu as pltpu
from jax.sharding import PartitionSpec as P

HEADS = 8
HEAD = 64
GROUPS = 16
LANES = 128
QUERY_BLOCK = 512
KEY_BLOCK = 256
ROW_BLOCK = 256
CROSS_FIRST = 2

eps = 1e-05
bfloat = jnp.bfloat16
single = jnp.float32
scale = HEAD ** (-0.5)
to_log2 = math.log2(math.e) * scale
far = -1.5e9

NN = (((1,), (0,)), ((), ()))
NT = (((1,), (1,)), ((), ()))
TN = (((0,), (0,)), ((), ()))

VM = pl.BlockSpec(memory_space=pltpu.VMEM)
sds = jax.ShapeDtypeStruct


def dot(left, right, dims):
    return lax.dot_general(left, right, dims, preferred_element_type=single)


def low(value):
    return value.astype(bfloat)


def wide(value):
    return value.astype(single)


def split(value):
    high = low(value)
    return high, low(value - wide(high))


def split_three(value):
    high = low(value)
    rest = value - wide(high)
    middle = low(rest)
    return wide(high), wide(middle), wide(low(rest - wide(middle)))


def rows_of(rows, count=16):
    width = rows[0].shape[1]
    index = lax.broadcasted_iota(jnp.int32, (count, width), 0)
    out = jnp.zeros((count, width), single)
    for at, row in enumerate(rows):
        out = jnp.where(index == at, row, out)
    return out


def columns_of(rows):
    return rows_of(rows, -(-len(rows) // 8) * 8).T


def over_tokens(value):
    return jnp.sum(value, axis=1, keepdims=True)


def normalize(total):
    center = total - jnp.mean(total, axis=0, keepdims=True)
    spread = jnp.mean(center * center, axis=0, keepdims=True)
    scaled = lax.rsqrt(spread + eps)
    return center * scaled, scaled


def normalize_back(grad, normed, scaled, gain):
    inner = grad * gain
    back = scaled * (
        inner
        - jnp.mean(inner, axis=0, keepdims=True)
        - normed * jnp.mean(inner * normed, axis=0, keepdims=True)
    )
    return back, over_tokens(grad * normed), over_tokens(grad)


def put_columns(stats, items):
    lane = lax.broadcasted_iota(jnp.int32, stats.shape, 1)
    for at, column in items:
        stats = jnp.where(lane == at, column, stats)
    return stats


def places(me, half):
    for core in range(2):
        for near in range(2):
            for far_off in range(4):
                bits = core + 2 * near + 4 * (far_off // 2) + 8 * (far_off % 2)
                group = jnp.bitwise_xor(me, bits)
                if half is None:
                    yield core, (near, far_off), group, 0
                else:
                    for across in range(2):
                        yield core, (near, across, far_off), group, jnp.bitwise_xor(half, across)


def pack(keep_ref, send_ref, held_ref, grad, at, me, half):
    held_ref[:, : grad.shape[1]] = low(grad)
    rows = grad.shape[0] // GROUPS
    part = rows if half is None else rows // 2
    lanes = slice(at, at + grad.shape[1])
    for core, place, group, portion in places(me, half):
        start = pl.multiple_of(group * rows + portion * part, part)
        (send_ref if core else keep_ref)[(*place, slice(None), lanes)] = held_ref[
            pl.ds(start, part), : grad.shape[1]
        ]


def ranks(shift):
    return (0, 0) if shift else (lax.axis_index("batch"), lax.axis_index("half"))


def head_rows(head):
    return pl.ds(pl.multiple_of(head * HEAD, HEAD), HEAD)


def hide_later(scores, offset, query_axis):
    key_pos = lax.broadcasted_iota(jnp.int32, scores.shape, 1 - query_axis) + offset
    query_pos = lax.broadcasted_iota(jnp.int32, scores.shape, query_axis)
    return jnp.where(key_pos <= query_pos, scores, far)


def forward_scratch(span):
    return [
        pltpu.VMEM((2, span, QUERY_BLOCK), single),
        pltpu.VMEM((8, QUERY_BLOCK), single),
        pltpu.VMEM((2, 2 * HEAD + 16, span), bfloat),
        pltpu.VMEM((2, span, 2 * HEAD + 16), bfloat),
        pltpu.VMEM((3, HEAD + 16, span), bfloat),
    ]


def attend_forward(query_ref, keys_ref, values_ref, mask, is_causal, mixed_ref, totals_ref, scratch):
    scores_ref, top_ref, more_query_ref, more_keys_ref, more_values_ref = scratch
    span = query_ref.shape[1]
    blocks = span // QUERY_BLOCK
    ones = low(rows_of([jnp.ones((1, span), single)]))
    more_query_ref[0, 2 * HEAD :] = ones
    more_query_ref[1, 2 * HEAD :] = ones
    mask_column = low(rows_of([mask])).T
    more_keys_ref[0, :, 2 * HEAD :] = mask_column
    more_keys_ref[1, :, 2 * HEAD :] = mask_column
    for slot in range(3):
        more_values_ref[slot, HEAD:] = ones

    def key_blocks(block):
        return range(0, (block + 1) * QUERY_BLOCK if is_causal else span, KEY_BLOCK)

    def prepare(head, slot):
        rows = head_rows(head)
        high, rest = split(wide(query_ref[rows]) * to_log2)
        more_query_ref[slot, :HEAD] = high
        more_query_ref[slot, HEAD : 2 * HEAD] = rest
        keys = keys_ref[rows]
        more_keys_ref[slot, :, : 2 * HEAD] = jnp.concatenate([keys, keys], axis=0).T
        more_values_ref[lax.rem(head, 3), :HEAD] = values_ref[rows]

    def score(slot, block, key, top):
        at = slice(block * QUERY_BLOCK, (block + 1) * QUERY_BLOCK)
        scores = dot(more_keys_ref[slot, key : key + KEY_BLOCK], more_query_ref[slot, :, at], NN)
        if is_causal and key + KEY_BLOCK > block * QUERY_BLOCK:
            scores = hide_later(scores, key - block * QUERY_BLOCK, 1)
        scores_ref[block % 2, key : key + KEY_BLOCK] = scores
        part = jnp.max(scores.reshape(KEY_BLOCK // 8, 8, QUERY_BLOCK), axis=0)
        return part if top is None else jnp.maximum(top, part)

    def mix(head, block, key, top, total):
        expo = low(jnp.exp2(scores_ref[block % 2, key : key + KEY_BLOCK] - top))
        part = dot(more_values_ref[lax.rem(head, 3), :, key : key + KEY_BLOCK], expo, NN)
        return part if total is None else total + part

    def finish_block(head, block, top, total):
        at = slice(block * QUERY_BLOCK, (block + 1) * QUERY_BLOCK)
        summed = total[HEAD : HEAD + 1]
        mixed_ref[head_rows(head), at] = low(total[:HEAD] / summed)
        totals_ref[pl.ds(head, 1), at] = top + jnp.log2(summed)

    prepare(0, 0)
    last = blocks - 1

    def body(pair, carry):
        for odd in range(2):
            head = 2 * pair + odd
            for block in range(blocks):
                before, block_before = (head, block - 1) if block else (jnp.maximum(head - 1, 0), last)
                top_before = top_ref[block_before % 2 : block_before % 2 + 1]
                top = None
                total = None
                now, then = list(key_blocks(block)), list(key_blocks(block_before))
                for step in range(max(len(now), len(then))):
                    if step < len(now):
                        top = score(odd, block, now[step], top)
                    if step < len(then):
                        total = mix(before, block_before, then[step], top_before, total)
                top_ref[block % 2 : block % 2 + 1] = jnp.max(top, axis=0, keepdims=True)
                finish_block(before, block_before, top_before, total)
                if block == 0:
                    prepare(jnp.minimum(head + 1, HEADS - 1), 1 - odd)
        return carry

    lax.fori_loop(0, HEADS // 2, body, 0)
    top = top_ref[last % 2 : last % 2 + 1]
    total = None
    for key in key_blocks(last):
        total = mix(HEADS - 1, last, key, top, total)
    finish_block(HEADS - 1, last, top, total)


def backward_scratch(span):
    return (
        [pltpu.VMEM((2, span, KEY_BLOCK), bfloat)] * 2
        + [pltpu.VMEM((2, span, HEAD + 16), bfloat)] * 2
        + [pltpu.VMEM((2, HEAD + 16, span), bfloat)] * 2
        + [pltpu.VMEM((HEAD, span), single)]
    )


def attend_backward(
    query_ref, keys_ref, values_ref, mixed_ref, totals_ref, incoming_ref, mask, is_causal,
    query_grad_ref, keys_grad_ref, values_grad_ref, first_head, last_head, scratch, beside=None,
):
    probs_ref, score_grads_ref, more_query_ref, more_incoming_ref, more_keys_ref, more_values_ref, held_ref = scratch
    span = query_ref.shape[1]
    blocks = span // KEY_BLOCK
    ones = jnp.ones((1, span), single)
    for slot in range(2):
        more_keys_ref[slot, HEAD:] = low(rows_of([ones, ones, ones, mask]))
        more_values_ref[slot, HEAD:] = low(rows_of([ones, ones, ones]))

    def first_query(block):
        return block * KEY_BLOCK if is_causal else 0

    def prepare(head, slot):
        rows = head_rows(head)
        query, incoming = query_ref[rows], incoming_ref[rows]
        delta = jnp.sum(wide(incoming) * wide(mixed_ref[rows]), axis=0, keepdims=True)
        totals = split_three(totals_ref[pl.ds(head, 1), :] * (-1 / to_log2))
        more_query_ref[slot] = jnp.concatenate([query, low(rows_of([*totals, ones]))], axis=0).T
        more_incoming_ref[slot] = jnp.concatenate(
            [incoming, low(rows_of(split_three(-delta)))], axis=0
        ).T
        more_keys_ref[slot, :HEAD] = keys_ref[rows]
        more_values_ref[slot, :HEAD] = values_ref[rows]

    def score(slot, block, start):
        keys, rows = slice(block * KEY_BLOCK, (block + 1) * KEY_BLOCK), slice(start, start + ROW_BLOCK)
        scores = dot(more_query_ref[slot, rows], more_keys_ref[slot, :, keys], NN)
        if is_causal and start < (block + 1) * KEY_BLOCK:
            scores = hide_later(scores, block * KEY_BLOCK - start, 0)
        probs = jnp.exp2(scores * to_log2)
        prob_grad = dot(more_incoming_ref[slot, rows], more_values_ref[slot, :, keys], NN)
        probs_ref[block % 2, rows] = low(probs)
        score_grads_ref[block % 2, rows] = low(probs * prob_grad)

    def products(head, block):
        rows, keys = head_rows(head), slice(block * KEY_BLOCK, (block + 1) * KEY_BLOCK)
        start = first_query(block)

        def values_part():
            values_grad_ref[rows, keys] = low(
                dot(incoming_ref[rows, start:], probs_ref[block % 2, start:], NN)
            )

        def keys_part():
            keys_grad_ref[rows, keys] = low(
                dot(query_ref[rows, start:], score_grads_ref[block % 2, start:], NN) * scale
            )

        def query_part(at):
            stop = min(at + 2 * ROW_BLOCK, span)
            part = dot(keys_ref[rows, keys], score_grads_ref[block % 2, at:stop], NT)
            if block:
                part = part + held_ref[:, at:stop]
            held_ref[:, at:stop] = part

        def query_whole():
            query_grad_ref[rows] = low(held_ref[...] * scale)

        steps = [values_part, keys_part]
        steps += [partial(query_part, at) for at in range(start, span, 2 * ROW_BLOCK)]
        return steps + [query_whole] * (block == blocks - 1)

    prepare(first_head, 0)

    def body(pair, carry):
        for odd in range(2):
            head = first_head + 2 * pair + odd
            for block in range(blocks):
                if block:
                    steps = products(head, block - 1)
                else:
                    steps = products(jnp.maximum(head - 1, first_head), blocks - 1)
                starts = range(first_query(block), span, ROW_BLOCK)
                for step in range(max(len(starts), len(steps))):
                    if step < len(starts):
                        score(odd, block, starts[step])
                    if step < len(steps):
                        steps[step]()
                if block == 0:
                    prepare(jnp.minimum(head + 1, last_head - 1), 1 - odd)
                if beside:
                    beside((2 * pair + odd) * blocks + block, (last_head - first_head) * blocks)
        return carry

    lax.fori_loop(0, (last_head - first_head) // 2, body, 0)
    for step in products(last_head - 1, blocks - 1):
        step()


ROOT = math.sqrt(2 / math.pi)
CUBE = ROOT * 0.044715


def gelu_parts(value):
    half = 0.5 * value
    cube = CUBE * (value * value)
    tanh = jnp.tanh(value * (ROOT + cube))
    more = 1 + tanh
    return half * more, more * (0.5 + (1 - tanh) * (half * (ROOT + 3 * cube)))


def opening_kernel(token_ref):
    token_ref[...] = jnp.zeros(token_ref.shape, single)


def projection_kernel(input_ref, maps_ref, bias_ref, input_t_ref, qkv_ref):
    columns = columns_of([bias_ref[0:1], bias_ref[1:2]])
    inputs = input_ref[0, 0].T
    input_t_ref[...] = inputs
    width = inputs.shape[0]
    qkv_ref[0:width] = low(dot(maps_ref[0], inputs, TN) + columns[:, 0:1])
    qkv_ref[width : 2 * width] = low(dot(maps_ref[1], inputs, TN))
    qkv_ref[2 * width :] = low(dot(maps_ref[2], inputs, TN) + columns[:, 1:2])


def self_forward_kernel(
    limit_ref, input_t_ref, qkv_ref, output_ref, bias_ref, omega_ref,
    mixed_ref, totals_ref, normed_ref, scaled_ref, *scratch,
):
    columns = columns_of([bias_ref[2:3], omega_ref[0:1]])
    width, span = input_t_ref.shape
    position = lax.broadcasted_iota(jnp.int32, (1, span), 1)
    mask = jnp.where(wide(position) < limit_ref[0:1, 0:1], 0.0, far)
    attend_forward(
        qkv_ref.at[0:width], qkv_ref.at[width : 2 * width], qkv_ref.at[2 * width :],
        mask, True, mixed_ref, totals_ref, scratch,
    )
    branch = dot(output_ref[...], mixed_ref[...], TN) + columns[:, 0:1]
    normed, scaled = normalize(wide(input_t_ref[...]) * columns[:, 1:2] + branch)
    normed_ref[...] = normed
    scaled_ref[...] = scaled


def source_mask(limit, half, size):
    local = lax.broadcasted_iota(jnp.int32, (1, 2 * size), 1)
    own = local < size
    position = jnp.where(own, local + half * size, local - size + (1 - half) * size)
    return jnp.where(wide(position) < limit, 0.0, far)


def cross_forward_kernel(
    limit_ref, normed_ref, memory_ref, arrived_ref, maps_ref, output_ref, bias_ref,
    gain_ref, shift_ref, omega_ref,
    memory_t_ref, query_ref, keys_ref, values_ref, mixed_ref, totals_ref,
    second_normed_ref, second_scaled_ref, *scratch,
):
    half = lax.axis_index("half")
    columns = columns_of(
        [bias_ref[3:4], bias_ref[4:5], bias_ref[5:6], gain_ref[0:1], shift_ref[0:1], omega_ref[1:2]]
    )
    size = memory_ref.shape[2]
    first = normed_ref[...] * columns[:, 3:4] + columns[:, 4:5]
    query_ref[...] = low(dot(maps_ref[0], low(first), TN) + columns[:, 0:1])
    memory_t_ref[:, :size] = memory_ref[half, 0].T
    memory_t_ref[:, size:] = arrived_ref[...].T
    keys_ref[...] = low(dot(maps_ref[1], memory_t_ref[...], TN))
    values_ref[...] = low(dot(maps_ref[2], memory_t_ref[...], TN) + columns[:, 1:2])
    mask = source_mask(limit_ref[1:2, 0:1], half, size)
    attend_forward(query_ref, keys_ref, values_ref, mask, False, mixed_ref, totals_ref, scratch)
    branch = dot(output_ref[...], mixed_ref[...], TN) + columns[:, 2:3]
    second_normed, second_scaled = normalize(first * columns[:, 5:6] + branch)
    second_normed_ref[...] = second_normed
    second_scaled_ref[...] = second_scaled


def ffn_kernel(
    second_normed_ref, gain_ref, shift_ref, omega_ref, expand_ref, expand_bias_ref, shrink_ref,
    shrink_bias_ref, grad_ref,
    layer_ref, back_ref, stats_ref, keep_ref, send_ref,
    hidden_ref, slope_ref, held_ref, wide_held_ref,
    *, shift,
):
    me, half = ranks(shift)
    columns = columns_of(
        [gain_ref[1:2], gain_ref[2:3], shift_ref[1:2], shift_ref[2:3], omega_ref[2:3]]
        + [shrink_bias_ref[...].reshape(1, -1)]
        + [expand_bias_ref[i : i + 512].reshape(1, -1) for i in range(0, expand_ref.shape[1], 512)]
    )
    width, span = second_normed_ref.shape
    second = second_normed_ref[...] * columns[:, 0:1] + columns[:, 2:3]
    second_low = low(second)
    features = expand_ref.shape[1]
    chunk = 512
    ffn = None
    for at in range(0, features, chunk):
        part = slice(at, at + chunk)
        pre = dot(expand_ref[:, part], second_low, TN) + columns[:, 6 + at // chunk : 7 + at // chunk]
        value, slope = gelu_parts(pre)
        hidden_ref[part] = low(value)
        slope_ref[part] = low(slope)
        term = dot(shrink_ref[part], hidden_ref[part], TN)
        ffn = term if ffn is None else ffn + term
    third_normed, third_scaled = normalize(second * columns[:, 4:5] + (ffn + columns[:, 5:6]))
    layer_ref[0, 0] = (third_normed * columns[:, 1:2] + columns[:, 3:4]).T
    grad = wide(grad_ref[0, 0].T)
    third_grad, gain_third, shift_third = normalize_back(
        grad, third_normed, third_scaled, columns[:, 1:2]
    )
    scale_third = over_tokens(second * third_grad)
    ffn_low = low(third_grad)
    shrink_bias_grad = over_tokens(wide(ffn_low))
    second_grad = third_grad * columns[:, 4:5]
    sums = []
    for at in range(0, features, chunk):
        part = slice(at, at + chunk)
        wide_held_ref[part] = low(dot(hidden_ref[part], ffn_low, NT))
        pre_grad = low(dot(shrink_ref[part], ffn_low, NN) * wide(slope_ref[part]))
        sums.append(over_tokens(wide(pre_grad)))
        held_ref[:, part] = low(dot(second_low, pre_grad, NT))
        second_grad = second_grad + dot(expand_ref[:, part], pre_grad, NN)
    back_ref[...] = second_grad
    rows = features // GROUPS // 4
    for core, place, group, portion in places(me, half):
        out = send_ref if core else keep_ref
        start = pl.multiple_of(group * rows + portion * (rows // 2), rows // 2)
        out[(*place, slice(None), slice(0, features))] = held_ref[pl.ds(start, rows // 2), :]
        for piece in range(4):
            start = (4 * group + piece) * rows + portion * (rows // 2)
            lanes = slice(features + piece * width, features + (piece + 1) * width)
            out[(*place, slice(None), lanes)] = wide_held_ref[
                pl.ds(pl.multiple_of(start, rows // 2), rows // 2), :
            ]
    expand_sums = jnp.concatenate(sums, axis=0)
    pieces = [
        jnp.concatenate(
            [
                expand_sums[(4 * group + piece) * rows : (4 * group + piece + 1) * rows]
                for group in range(GROUPS)
            ],
            axis=0,
        )
        for piece in range(4)
    ]
    stats_ref[...] = put_columns(
        jnp.zeros(stats_ref.shape, single),
        [(8, gain_third), (11, shift_third), (14, scale_third), (15, shrink_bias_grad)]
        + [(16 + piece, pieces[piece]) for piece in range(4)],
    )


def norm_grad(grad, normed, scaled, gain):
    inner = grad * gain
    return scaled * (
        inner
        - jnp.mean(inner, axis=0, keepdims=True)
        - normed * jnp.mean(inner * normed, axis=0, keepdims=True)
    )


def sums_scratch(width):
    return [pltpu.VMEM((width, 8), single), pltpu.VMEM((4, width, 1), single)]


def norm_sums(grad_ref, normed_ref, back_ref, input_of, columns_ref, omega, sums_ref):
    def some(step, steps):
        size = back_ref.shape[0] // steps
        rows = pl.ds(pl.multiple_of(step * size, size), size)
        grad, back = grad_ref[rows], back_ref[rows]
        sums_ref[0, rows] = over_tokens(grad * normed_ref[rows])
        sums_ref[1, rows] = over_tokens(grad)
        sums_ref[2, rows] = over_tokens(input_of(rows) * back)
        sums_ref[3, rows] = over_tokens(wide(low(back)))
        back_ref[rows] = back * columns_ref[rows, omega : omega + 1]

    return some


def cross_back_kernel(
    limit_ref, normed_ref, second_normed_ref, second_scaled_ref, back_ref,
    query_ref, keys_ref, values_ref, mixed_ref, totals_ref, output_ref,
    gain_ref, shift_ref, omega_ref, stats_in_ref,
    part_grad_ref, incoming_ref, output_grad_ref, stats_ref,
    query_grad_ref, keys_grad_ref, values_grad_ref, *scratch,
):
    half = lax.axis_index("half")
    columns = columns_of([gain_ref[0:1], shift_ref[0:1], gain_ref[1:2], omega_ref[1:2]])
    size = keys_ref.shape[1] // 2
    *scratch, columns_ref, sums_ref = scratch
    columns_ref[...] = columns
    sum_grad = norm_grad(
        back_ref[...], second_normed_ref[...], second_scaled_ref[...], columns[:, 2:3]
    )
    part_grad_ref[...] = sum_grad
    cross_low = low(sum_grad)
    incoming_ref[...] = low(dot(output_ref[...], cross_low, NN))
    output_grad_ref[...] = low(dot(mixed_ref[...], cross_low, NT))
    mask = source_mask(limit_ref[1:2, 0:1], half, size)

    def first_of(rows):
        return normed_ref[rows] * columns_ref[rows, 0:1] + columns_ref[rows, 1:2]

    attend_backward(
        query_ref, keys_ref, values_ref, mixed_ref, totals_ref, incoming_ref, mask, False,
        query_grad_ref, keys_grad_ref, values_grad_ref, 0, CROSS_FIRST, scratch,
        norm_sums(back_ref, second_normed_ref, part_grad_ref, first_of, columns_ref, 3, sums_ref),
    )
    stats_ref[...] = put_columns(
        stats_in_ref[...], [(7, sums_ref[0]), (10, sums_ref[1]), (13, sums_ref[2]), (5, sums_ref[3])]
    )


def cross_rest_kernel(
    limit_ref, normed_ref, memory_t_ref, query_ref, keys_ref, values_ref, mixed_ref, totals_ref,
    maps_ref, gain_ref, shift_ref, part_grad_ref, incoming_ref, output_grad_ref, stats_in_ref,
    query_half_ref, keys_half_ref, values_half_ref,
    first_grad_ref, own_ref, away_ref, stats_ref, keep_ref, send_ref,
    query_grad_ref, keys_grad_ref, values_grad_ref, held_ref, *scratch, shift,
):
    me, across = ranks(shift)
    columns = columns_of([gain_ref[0:1], shift_ref[0:1]])
    size = own_ref.shape[1]
    width = normed_ref.shape[0]
    mask = source_mask(limit_ref[1:2, 0:1], lax.axis_index("half"), size)
    attend_backward(
        query_ref, keys_ref, values_ref, mixed_ref, totals_ref, incoming_ref, mask, False,
        query_grad_ref, keys_grad_ref, values_grad_ref, CROSS_FIRST, HEADS, scratch,
    )
    top = slice(0, CROSS_FIRST * HEAD)
    query_grad_ref[top] = query_half_ref[top]
    keys_grad_ref[top] = keys_half_ref[top]
    values_grad_ref[top] = values_half_ref[top]
    query_grad, keys_grad, values_grad = query_grad_ref[...], keys_grad_ref[...], values_grad_ref[...]
    first_low = low(normed_ref[...] * columns[:, 0:1] + columns[:, 1:2])
    pack(keep_ref, send_ref, held_ref, output_grad_ref[...], 3 * width, me, across)
    pack(keep_ref, send_ref, held_ref, dot(first_low, query_grad, NT), 0, me, across)
    pack(keep_ref, send_ref, held_ref, dot(memory_t_ref[...], keys_grad, NT), width, me, across)
    pack(keep_ref, send_ref, held_ref, dot(memory_t_ref[...], values_grad, NT), 2 * width, me, across)
    first_grad_ref[...] = part_grad_ref[...] + dot(maps_ref[0], query_grad, NN)
    memory_grad = dot(maps_ref[1], keys_grad, NN) + dot(maps_ref[2], values_grad, NN)
    own_ref[...] = memory_grad[:, :size]
    away_ref[...] = low(memory_grad[:, size:])
    stats_ref[...] = put_columns(
        stats_in_ref[...],
        [(3, over_tokens(wide(query_grad))), (4, over_tokens(wide(values_grad)))],
    )


def self_back_kernel(
    limit_ref, input_t_ref, normed_ref, scaled_ref, first_grad_ref, qkv_ref, mixed_ref, totals_ref,
    output_ref, gain_ref, omega_ref, stats_in_ref,
    part_grad_ref, incoming_ref, stats_ref, query_grad_ref, keys_grad_ref, values_grad_ref,
    keep_ref, send_ref, held_ref, *scratch, shift,
):
    me, _ = ranks(shift)
    columns = columns_of([gain_ref[0:1], omega_ref[0:1]])
    *scratch, columns_ref, sums_ref = scratch
    columns_ref[...] = columns
    width, span = input_t_ref.shape
    sum_grad = norm_grad(first_grad_ref[...], normed_ref[...], scaled_ref[...], columns[:, 0:1])
    part_grad_ref[...] = sum_grad
    self_low = low(sum_grad)
    inputs = input_t_ref[...]
    incoming_ref[...] = low(dot(output_ref[...], self_low, NN))
    output_grad = dot(mixed_ref[...], self_low, NT)
    position = lax.broadcasted_iota(jnp.int32, (1, span), 1)
    mask = jnp.where(wide(position) < limit_ref[0:1, 0:1], 0.0, far)
    attend_backward(
        qkv_ref.at[0:width], qkv_ref.at[width : 2 * width], qkv_ref.at[2 * width :],
        mixed_ref, totals_ref, incoming_ref, mask, True,
        query_grad_ref, keys_grad_ref, values_grad_ref, 0, HEADS // 2, scratch,
        norm_sums(
            first_grad_ref, normed_ref, part_grad_ref, lambda rows: wide(input_t_ref[rows]),
            columns_ref, 1, sums_ref,
        ),
    )
    stats_ref[...] = put_columns(
        stats_in_ref[...], [(6, sums_ref[0]), (9, sums_ref[1]), (12, sums_ref[2]), (2, sums_ref[3])]
    )
    pack(keep_ref, send_ref, held_ref, output_grad, 3 * width // 2, me, None)
    pack_maps(
        keep_ref, send_ref, held_ref, inputs, (query_grad_ref, keys_grad_ref, values_grad_ref),
        slice(0, width // 2), me,
    )


def pack_maps(keep_ref, send_ref, held_ref, inputs, grads, rows, me):
    for at, ref in enumerate(grads):
        part = dot(inputs, ref[rows], NT)
        pack(keep_ref, send_ref, held_ref, part, at * part.shape[1], me, None)


def self_heads_kernel(
    limit_ref, qkv_ref, mixed_ref, totals_ref, incoming_ref,
    query_half_ref, keys_half_ref, values_half_ref,
    query_grad_ref, keys_grad_ref, values_grad_ref, *scratch,
):
    width, span = mixed_ref.shape
    position = lax.broadcasted_iota(jnp.int32, (1, span), 1)
    mask = jnp.where(wide(position) < limit_ref[0:1, 0:1], 0.0, far)
    attend_backward(
        qkv_ref.at[0:width], qkv_ref.at[width : 2 * width], qkv_ref.at[2 * width :],
        mixed_ref, totals_ref, incoming_ref, mask, True,
        query_grad_ref, keys_grad_ref, values_grad_ref, HEADS // 2, HEADS, scratch,
    )
    top = slice(0, width // 2)
    query_grad_ref[top] = query_half_ref[top]
    keys_grad_ref[top] = keys_half_ref[top]
    values_grad_ref[top] = values_half_ref[top]


def self_rest_kernel(
    input_t_ref, stats_in_ref, query_grad_ref, keys_grad_ref, values_grad_ref,
    keep_ref, send_ref, held_ref, *, shift,
):
    me, _ = ranks(shift)
    width = input_t_ref.shape[0]
    pack_maps(
        keep_ref, send_ref, held_ref, input_t_ref[...], (query_grad_ref, keys_grad_ref, values_grad_ref),
        slice(width // 2, width), me,
    )
    stats = put_columns(
        stats_in_ref[...],
        [(0, over_tokens(wide(query_grad_ref[...]))), (1, over_tokens(wide(values_grad_ref[...])))],
    )
    pack(keep_ref, send_ref, held_ref, stats, 3 * width // 2, me, None)


def input_kernel(
    part_grad_ref, query_grad_ref, keys_grad_ref, values_grad_ref, maps_ref, input_grad_ref, token_ref
):
    token_ref[...] = jnp.zeros(token_ref.shape, single)
    input_grad_ref[0, 0] = (
        part_grad_ref[...]
        + dot(maps_ref[0], query_grad_ref[...], NN)
        + dot(maps_ref[1], keys_grad_ref[...], NN)
        + dot(maps_ref[2], values_grad_ref[...], NN)
    ).T


def halve_kernel(kept_ref, arrived_ref, sent_out_ref, kept_out_ref):
    part = kept_ref.shape[0] // 2
    at = slice(part, None) if part > 1 else 1
    sent_out_ref[...] = low(wide(kept_ref[at]) + wide(arrived_ref[at]))
    at = slice(0, part) if part > 1 else 0
    kept_out_ref[...] = low(wide(kept_ref[at]) + wide(arrived_ref[at]))


def sum_kernel(kept_ref, arrived_ref, out_ref):
    out_ref[...] = low(wide(kept_ref[...]) + wide(arrived_ref[...]))


def memory_kernel(own_ref, returned_ref, rest_ref, out_ref, token_ref):
    token_ref[...] = jnp.zeros(token_ref.shape, single)
    half = lax.axis_index("half")
    out_ref[half, 0] = own_ref[...].T + rest_ref[half, 0]
    out_ref[1 - half, 0] = wide(returned_ref[...]).T + rest_ref[1 - half, 0]


def finish(ffn, cross, early, late, width):
    features = ffn.shape[1] // 2
    part = width // 2
    maps = [
        jnp.concatenate([v[:, i * part : (i + 1) * part] for v in (early, late)], axis=1)
        for i in range(3)
    ]
    cross_maps = [cross[:, i * width : (i + 1) * width] for i in range(3)]
    shrink = jnp.concatenate(
        [ffn[:, features + i * width : features + (i + 1) * width] for i in range(4)], axis=0
    )
    stats = late[:, 3 * part :].T
    return (
        maps, early[:, 3 * part :], cross_maps, cross[:, 3 * width :],
        stats[0:6], ffn[:, :features],
        jnp.concatenate([stats[16 + i : 17 + i] for i in range(4)], axis=1).reshape(-1), shrink,
        stats[15:16].reshape(-1), stats[6:9], stats[9:12], stats[12:15],
    )


def finish_kernel(*refs, shift):
    ins, outs, held = refs[:8], refs[8:-4], refs[-4:]
    half = lax.axis_index("half")
    width = outs[1].shape[1]
    for i in range(4):
        own, other = wide(ins[2 * i][...]), wide(ins[2 * i + 1][...])
        if shift or i >= 2:
            held[i][...] = own + other
        else:
            rows = own.shape[0]
            held[i][pl.ds(pl.multiple_of(half * rows, rows), rows)] = own
            held[i][pl.ds(pl.multiple_of((1 - half) * rows, rows), rows)] = other
    for ref, value in zip(outs, finish(*(ref[...] for ref in held), width)):
        if isinstance(value, list):
            for at, item in enumerate(value):
                ref[at] = item.reshape(ref.shape[1:])
        else:
            ref[...] = value


TIMES = {
    "opening": 6, "self_forward": 9, "cross_forward": 13, "ffn": 20, "cross_back": 7, "cross_rest": 18,
    "self_back": 10, "self_heads": 7, "self_rest": 1, "input_grad": 3, "memory_grad": 2,
}
MICROSECOND = 1_000_000_000


def call(kernel, name, outs, scratch=(), after=(), vmem=13, **options):
    def entry(*refs):
        kernel(*refs[len(after) :], **options)

    return lambda *args: pl.pallas_call(
        entry,
        name=name,
        out_shape=outs,
        in_specs=[pl.BlockSpec(memory_space=pl.ANY)] * len(after) + [VM] * len(args),
        out_specs=jax.tree.map(lambda _: VM, outs),
        scratch_shapes=scratch,
        compiler_params=pltpu.CompilerParams(vmem_limit_bytes=vmem * 1024 * 1024),
        cost_estimate=pl.CostEstimate(
            flops=TIMES.get(name, 0) * MICROSECOND, bytes_accessed=1, transcendentals=0
        ),
    )(*after, *args)


def shards(
    block_input, memory, memory_grad_rest, output_grad, target_length, source_length,
    self_maps, self_output, cross_maps, cross_output, attention_bias,
    expand_weight, expand_bias, shrink_weight, shrink_bias, norm_gain, norm_bias, residual_scale,
    *, devices,
):
    span, width = block_input.shape[2:]
    size = memory.shape[2]
    source = 2 * size
    features = expand_weight.shape[1]
    shift = int(math.log2(devices // GROUPS))
    assert GROUPS << shift == devices
    rows = width // GROUPS
    half = lax.axis_index("half")

    def swap_half(value):
        return lax.ppermute(value, "half", [(0, 1), (1, 0)])

    def swap(value, bits):
        return lax.ppermute(value, "batch", [(i, i ^ bits) for i in range(devices)])

    def halve(kept, arrived, *after):
        part = kept.shape[0] // 2
        shape = kept.shape[1:] if part == 1 else (part, *kept.shape[1:])
        return call(halve_kernel, "halve", [sds(shape, bfloat)] * 2, after=after)(kept, arrived)

    def joined(kept, arrived, *after):
        return call(sum_kernel, "join", sds(kept.shape, bfloat), after=after)(kept, arrived)

    CORE, NEAR, NEXT, AWAY = 1, 2, 4, 8

    def scattered(keep, send, pieces=None):
        packet = jnp.stack([keep, send])
        if packet.ndim == 6:
            packet = packet.transpose(3, 1, 0, 2, 4, 5)
        else:
            packet = packet.transpose(2, 1, 0, 3, 4)
        packet = packet.reshape(2, 2, 4, rows, -1).swapaxes(0, 1)
        packet = packet.reshape(GROUPS, rows, -1)
        if pieces:
            start, stop = pieces
            part = packet[..., start:stop].reshape(GROUPS, rows, 4, -1).swapaxes(1, 2)
            part = part.reshape(GROUPS, 1 << shift, 4, rows >> shift, -1).swapaxes(2, 3)
            part = part.reshape(GROUPS, rows, stop - start)
            packet = jnp.concatenate([packet[..., :start], part, packet[..., stop:]], axis=-1)
        total = lax.psum_scatter(
            packet.reshape(width, -1), "batch", scatter_dimension=0, tiled=True
        )
        return total, swap_half(total)

    arrived = swap_half(lax.dynamic_index_in_dim(memory, 1 - half, 0, keepdims=False)[0])
    tall = sds((width, span), bfloat)
    tall_wide = sds((width, span), single)
    packet = lambda lanes: [sds((2, 2, 4, rows // 2, lanes), bfloat)] * 2
    simple = lambda lanes: [sds((2, 4, rows, lanes), bfloat)] * 2
    limits = jnp.broadcast_to(
        jnp.concatenate([target_length, source_length]).astype(single), (2, LANES)
    )
    opening = call(opening_kernel, "opening", sds((8, LANES), single))()
    input_t, qkv = call(
        projection_kernel, "projections", [tall, sds((3 * width, span), bfloat)], after=(opening,),
    )(block_input, self_maps, attention_bias)
    mixed, totals, normed, scaled = call(
        self_forward_kernel, "self_forward",
        [tall, sds((HEADS, span), single), tall_wide, sds((1, span), single)],
        scratch=forward_scratch(span),
    )(limits, input_t, qkv, self_output, attention_bias, residual_scale)
    source_tall = sds((width, source), bfloat)
    (
        memory_t, query, keys, values, cross_mixed, cross_totals, second_normed, second_scaled,
    ) = call(
        cross_forward_kernel, "cross_forward",
        [source_tall, tall, source_tall, source_tall, tall, sds((HEADS, span), single),
         tall_wide, sds((1, span), single)],
        scratch=forward_scratch(span),
    )(
        limits, normed, memory, arrived, cross_maps, cross_output, attention_bias,
        norm_gain, norm_bias, residual_scale,
    )
    layer_output, second_grad, stats, ffn_keep, ffn_send = call(
        ffn_kernel, "ffn",
        [sds((1, 1, span, width), single), tall_wide, sds((width, LANES), single)]
        + packet(2 * features),
        scratch=[pltpu.VMEM((features, span), bfloat)] * 2
        + [pltpu.VMEM((width, features), bfloat), pltpu.VMEM((features, width), bfloat)],
        shift=shift, vmem=31,
    )(
        second_normed, norm_gain, norm_bias, residual_scale, expand_weight,
        expand_bias, shrink_weight, shrink_bias, output_grad,
    )
    grads = [pltpu.VMEM((width, span), bfloat)] + [pltpu.VMEM((width, source), bfloat)] * 2
    held = pltpu.VMEM((width, width), bfloat)
    square = sds((width, width), bfloat)
    stats_shape = sds((width, LANES), single)
    part_grad, incoming, output_part, stats, *halves = call(
        cross_back_kernel, "cross_back",
        [tall_wide, tall, square, stats_shape, tall, source_tall, source_tall],
        scratch=backward_scratch(span) + sums_scratch(width),
    )(
        limits, normed, second_normed, second_scaled, second_grad,
        query, keys, values, cross_mixed, cross_totals, cross_output,
        norm_gain, norm_bias, residual_scale, stats,
    )
    if not shift:
        ffn = halve(ffn_keep, swap(ffn_send, CORE), part_grad)
    first_grad, own, away, stats, cross_keep, cross_send = call(
        cross_rest_kernel, "cross_rest",
        [tall_wide, sds((width, size), single), sds((width, size), bfloat), stats_shape]
        + packet(4 * width),
        scratch=grads + [held] + backward_scratch(span), after=() if shift else ffn, shift=shift,
    )(
        limits, normed, memory_t, query, keys, values, cross_mixed, cross_totals, cross_maps,
        norm_gain, norm_bias, part_grad, incoming, output_part, stats, *halves,
    )
    returned = swap_half(away)
    part_grad, incoming, stats, *rest_of = call(
        self_back_kernel, "self_back",
        [tall_wide, tall, stats_shape, tall, tall, tall] + simple(5 * width // 2),
        scratch=[held] + backward_scratch(span) + sums_scratch(width),
        shift=shift,
    )(
        limits, input_t, normed, scaled, first_grad, qkv, mixed, totals,
        self_output, norm_gain, residual_scale, stats,
    )
    *halves, early_keep, early_send = rest_of
    before = ()
    if not shift:
        ffn = halve(ffn[1], swap(ffn[0], NEAR), stats)
        cross = halve(cross_keep, swap(cross_send, CORE), *ffn)
        before = (*ffn, *cross, returned)
    grads_out = call(
        self_heads_kernel, "self_heads", [tall] * 3,
        scratch=backward_scratch(span), after=before,
    )(limits, qkv, mixed, totals, incoming, *halves)
    before = ()
    if not shift:
        early = halve(early_keep, swap(early_send, CORE), grads_out[0])
        before = early
    late_keep, late_send = call(
        self_rest_kernel, "self_rest", simple(3 * width // 2 + LANES),
        scratch=[held], after=before, shift=shift,
    )(input_t, stats, *grads_out)
    def to_memory(*after):
        return call(
            memory_kernel, "memory_grad",
            [sds(memory_grad_rest.shape, single), sds((8, LANES), single)], after=after,
        )(own, returned, memory_grad_rest)

    def to_input(*after):
        return call(
            input_kernel, "input_grad", [sds((1, 1, span, width), single), sds((8, LANES), single)],
            after=after,
        )(part_grad, *grads_out, self_maps)

    if shift:
        input_grad, _ = to_input()
        memory_grad, token = to_memory()
        start = 3 * width // 2 + 16
        parts = (
            *scattered(ffn_keep, ffn_send, (features, 2 * features)),
            *scattered(cross_keep, cross_send),
            *scattered(early_keep, early_send),
            *scattered(late_keep, late_send, (start, start + 4)),
        )
    else:
        ffn = halve(ffn[1], swap_half(ffn[0]), late_keep)
        cross = halve(cross[1], swap(cross[0], NEAR), *ffn)
        late = halve(late_keep, swap(late_send, CORE), *cross)
        input_grad, token = to_input(*late)
        early = halve(early[1], swap(early[0], NEAR), token)
        ffn = halve(ffn[1], swap(ffn[0], NEXT), *early)
        cross = halve(cross[1], swap_half(cross[0]), *ffn)
        late = halve(late[1], swap(late[0], NEAR), *cross)
        early = halve(early[1], swap(early[0], NEXT), *late)
        ffn = joined(ffn[1], swap(ffn[0], AWAY), *early)
        cross = halve(cross[1], swap(cross[0], NEXT), ffn)
        late = halve(late[1], swap(late[0], NEXT), *cross)
        early = joined(early[1], swap(early[0], AWAY), *late)
        cross = joined(cross[1], swap(cross[0], AWAY), early)
        late = joined(late[1], swap(late[0], AWAY), cross)
        memory_grad, token = to_memory(late)
        parts = tuple(
            part for value in (ffn, cross, early, late) for part in (value, swap_half(value))
        )
    mine = rows >> shift
    outs = [
        sds((3, mine, width), single), sds((mine, width), single), sds((3, mine, width), single),
        sds((mine, width), single), sds((6, mine), single), sds((mine, features), single),
        sds((4 * mine,), single), sds((4 * mine, width), single), sds((mine,), single),
        sds((3, mine), single), sds((3, mine), single), sds((3, mine), single),
    ]
    done = list(
        call(
            finish_kernel, "finish", outs, shift=shift, after=(token,),
            scratch=[
                pltpu.VMEM((mine, lanes), single)
                for lanes in (2 * features, 4 * width, 5 * width // 2, 3 * width // 2 + LANES)
            ],
        )(*parts)
    )
    return (layer_output, input_grad, memory_grad, *done)


def solution(mesh):
    rows = P("half", "batch", None, None)
    sources = P(None, "batch", "half", None)
    placed = (rows, sources, sources, rows, P("half", "batch"), P("half", "batch")) + (P(),) * 12
    return jax.shard_map(
        partial(shards, devices=mesh.shape["batch"]),
        mesh=mesh,
        in_specs=placed,
        out_specs=(
            rows, rows, sources,
            P(None, "batch", None), P("batch", None), P(None, "batch", None), P("batch", None),
            P(None, "batch"), P("batch", None), P("batch"), P("batch", None), P("batch"),
            P(None, "batch"), P(None, "batch"), P(None, "batch"),
        ),
        check_vma=False,
    )
```

```python
from functools import partial
import math

import jax
import jax.numpy as jnp
from jax import lax
from jax.experimental import pallas as pl
from jax.experimental.pallas import tpu as pltpu
from jax.sharding import PartitionSpec as P

HEADS = 8
HEAD = 64
GROUPS = 16
LANES = 128
QUERY_BLOCK = 512
KEY_BLOCK = 256
ROW_BLOCK = 256
CROSS_FIRST = 2

eps = 1e-05
bfloat = jnp.bfloat16
single = jnp.float32
scale = HEAD ** (-0.5)
to_log2 = math.log2(math.e) * scale
far = -1.5e9

NN = (((1,), (0,)), ((), ()))
NT = (((1,), (1,)), ((), ()))
TN = (((0,), (0,)), ((), ()))

VM = pl.BlockSpec(memory_space=pltpu.VMEM)
sds = jax.ShapeDtypeStruct


def dot(left, right, dims):
    return lax.dot_general(left, right, dims, preferred_element_type=single)


def low(value):
    return value.astype(bfloat)


def wide(value):
    return value.astype(single)


def split(value):
    high = low(value)
    return high, low(value - wide(high))


def split_three(value):
    high = low(value)
    rest = value - wide(high)
    middle = low(rest)
    return wide(high), wide(middle), wide(low(rest - wide(middle)))


def rows_of(rows, count=16):
    width = rows[0].shape[1]
    index = lax.broadcasted_iota(jnp.int32, (count, width), 0)
    out = jnp.zeros((count, width), single)
    for at, row in enumerate(rows):
        out = jnp.where(index == at, row, out)
    return out


def columns_of(rows):
    return rows_of(rows, -(-len(rows) // 8) * 8).T


def over_tokens(value):
    return jnp.sum(value, axis=1, keepdims=True)


def normalize(total):
    center = total - jnp.mean(total, axis=0, keepdims=True)
    spread = jnp.mean(center * center, axis=0, keepdims=True)
    scaled = lax.rsqrt(spread + eps)
    return center * scaled, scaled


def normalize_back(grad, normed, scaled, gain):
    inner = grad * gain
    back = scaled * (
        inner
        - jnp.mean(inner, axis=0, keepdims=True)
        - normed * jnp.mean(inner * normed, axis=0, keepdims=True)
    )
    return back, over_tokens(grad * normed), over_tokens(grad)


def put_columns(stats, items):
    lane = lax.broadcasted_iota(jnp.int32, stats.shape, 1)
    for at, column in items:
        stats = jnp.where(lane == at, column, stats)
    return stats


def places(me, half):
    for core in range(2):
        for near in range(2):
            for far_off in range(4):
                bits = core + 2 * near + 4 * (far_off // 2) + 8 * (far_off % 2)
                group = jnp.bitwise_xor(me, bits)
                if half is None:
                    yield core, (near, far_off), group, 0
                else:
                    for across in range(2):
                        yield core, (near, across, far_off), group, jnp.bitwise_xor(half, across)


def pack(keep_ref, send_ref, held_ref, grad, at, me, half):
    held_ref[:, : grad.shape[1]] = low(grad)
    rows = grad.shape[0] // GROUPS
    part = rows if half is None else rows // 2
    lanes = slice(at, at + grad.shape[1])
    for core, place, group, portion in places(me, half):
        start = pl.multiple_of(group * rows + portion * part, part)
        (send_ref if core else keep_ref)[(*place, slice(None), lanes)] = held_ref[
            pl.ds(start, part), : grad.shape[1]
        ]


def ranks(shift):
    return (0, 0) if shift else (lax.axis_index("batch"), lax.axis_index("half"))


def head_rows(head):
    return pl.ds(pl.multiple_of(head * HEAD, HEAD), HEAD)


def hide_later(scores, offset, query_axis):
    key_pos = lax.broadcasted_iota(jnp.int32, scores.shape, 1 - query_axis) + offset
    query_pos = lax.broadcasted_iota(jnp.int32, scores.shape, query_axis)
    return jnp.where(key_pos <= query_pos, scores, far)


def forward_scratch(span):
    return [
        pltpu.VMEM((2, span, QUERY_BLOCK), single),
        pltpu.VMEM((8, QUERY_BLOCK), single),
        pltpu.VMEM((2, 2 * HEAD + 16, span), bfloat),
        pltpu.VMEM((2, span, 2 * HEAD + 16), bfloat),
        pltpu.VMEM((3, HEAD + 16, span), bfloat),
    ]


def attend_forward(query_ref, keys_ref, values_ref, mask, is_causal, mixed_ref, totals_ref, scratch):
    scores_ref, top_ref, more_query_ref, more_keys_ref, more_values_ref = scratch
    span = query_ref.shape[1]
    blocks = span // QUERY_BLOCK
    ones = low(rows_of([jnp.ones((1, span), single)]))
    more_query_ref[0, 2 * HEAD :] = ones
    more_query_ref[1, 2 * HEAD :] = ones
    mask_column = low(rows_of([mask])).T
    more_keys_ref[0, :, 2 * HEAD :] = mask_column
    more_keys_ref[1, :, 2 * HEAD :] = mask_column
    for slot in range(3):
        more_values_ref[slot, HEAD:] = ones

    def key_blocks(block):
        return range(0, (block + 1) * QUERY_BLOCK if is_causal else span, KEY_BLOCK)

    def prepare(head, slot):
        rows = head_rows(head)
        high, rest = split(wide(query_ref[rows]) * to_log2)
        more_query_ref[slot, :HEAD] = high
        more_query_ref[slot, HEAD : 2 * HEAD] = rest
        keys = keys_ref[rows]
        more_keys_ref[slot, :, : 2 * HEAD] = jnp.concatenate([keys, keys], axis=0).T
        more_values_ref[lax.rem(head, 3), :HEAD] = values_ref[rows]

    def score(slot, block, key, top):
        at = slice(block * QUERY_BLOCK, (block + 1) * QUERY_BLOCK)
        scores = dot(more_keys_ref[slot, key : key + KEY_BLOCK], more_query_ref[slot, :, at], NN)
        if is_causal and key + KEY_BLOCK > block * QUERY_BLOCK:
            scores = hide_later(scores, key - block * QUERY_BLOCK, 1)
        scores_ref[block % 2, key : key + KEY_BLOCK] = scores
        part = jnp.max(scores.reshape(KEY_BLOCK // 8, 8, QUERY_BLOCK), axis=0)
        return part if top is None else jnp.maximum(top, part)

    def mix(head, block, key, top, total):
        expo = low(jnp.exp2(scores_ref[block % 2, key : key + KEY_BLOCK] - top))
        part = dot(more_values_ref[lax.rem(head, 3), :, key : key + KEY_BLOCK], expo, NN)
        return part if total is None else total + part

    def finish_block(head, block, top, total):
        at = slice(block * QUERY_BLOCK, (block + 1) * QUERY_BLOCK)
        summed = total[HEAD : HEAD + 1]
        mixed_ref[head_rows(head), at] = low(total[:HEAD] / summed)
        totals_ref[pl.ds(head, 1), at] = top + jnp.log2(summed)

    prepare(0, 0)
    last = blocks - 1

    def body(pair, carry):
        for odd in range(2):
            head = 2 * pair + odd
            for block in range(blocks):
                before, block_before = (head, block - 1) if block else (jnp.maximum(head - 1, 0), last)
                top_before = top_ref[block_before % 2 : block_before % 2 + 1]
                top = None
                total = None
                now, then = list(key_blocks(block)), list(key_blocks(block_before))
                for step in range(max(len(now), len(then))):
                    if step < len(now):
                        top = score(odd, block, now[step], top)
                    if step < len(then):
                        total = mix(before, block_before, then[step], top_before, total)
                top_ref[block % 2 : block % 2 + 1] = jnp.max(top, axis=0, keepdims=True)
                finish_block(before, block_before, top_before, total)
                if block == 0:
                    prepare(jnp.minimum(head + 1, HEADS - 1), 1 - odd)
        return carry

    lax.fori_loop(0, HEADS // 2, body, 0)
    top = top_ref[last % 2 : last % 2 + 1]
    total = None
    for key in key_blocks(last):
        total = mix(HEADS - 1, last, key, top, total)
    finish_block(HEADS - 1, last, top, total)


def backward_scratch(span):
    return (
        [pltpu.VMEM((2, span, KEY_BLOCK), bfloat)] * 2
        + [pltpu.VMEM((2, span, HEAD + 16), bfloat)] * 2
        + [pltpu.VMEM((2, HEAD + 16, span), bfloat)] * 2
        + [pltpu.VMEM((HEAD, span), single)]
    )


def attend_backward(
    query_ref, keys_ref, values_ref, mixed_ref, totals_ref, incoming_ref, mask, is_causal,
    query_grad_ref, keys_grad_ref, values_grad_ref, first_head, last_head, scratch, beside=None,
):
    probs_ref, score_grads_ref, more_query_ref, more_incoming_ref, more_keys_ref, more_values_ref, held_ref = scratch
    span = query_ref.shape[1]
    blocks = span // KEY_BLOCK
    ones = jnp.ones((1, span), single)
    for slot in range(2):
        more_keys_ref[slot, HEAD:] = low(rows_of([ones, ones, ones, mask]))
        more_values_ref[slot, HEAD:] = low(rows_of([ones, ones, ones]))

    def first_query(block):
        return block * KEY_BLOCK if is_causal else 0

    def prepare(head, slot):
        rows = head_rows(head)
        query, incoming = query_ref[rows], incoming_ref[rows]
        delta = jnp.sum(wide(incoming) * wide(mixed_ref[rows]), axis=0, keepdims=True)
        totals = split_three(totals_ref[pl.ds(head, 1), :] * (-1 / to_log2))
        more_query_ref[slot] = jnp.concatenate([query, low(rows_of([*totals, ones]))], axis=0).T
        more_incoming_ref[slot] = jnp.concatenate(
            [incoming, low(rows_of(split_three(-delta)))], axis=0
        ).T
        more_keys_ref[slot, :HEAD] = keys_ref[rows]
        more_values_ref[slot, :HEAD] = values_ref[rows]

    def score(slot, block, start):
        keys, rows = slice(block * KEY_BLOCK, (block + 1) * KEY_BLOCK), slice(start, start + ROW_BLOCK)
        scores = dot(more_query_ref[slot, rows], more_keys_ref[slot, :, keys], NN)
        if is_causal and start < (block + 1) * KEY_BLOCK:
            scores = hide_later(scores, block * KEY_BLOCK - start, 0)
        probs = jnp.exp2(scores * to_log2)
        prob_grad = dot(more_incoming_ref[slot, rows], more_values_ref[slot, :, keys], NN)
        probs_ref[block % 2, rows] = low(probs)
        score_grads_ref[block % 2, rows] = low(probs * prob_grad)

    def products(head, block):
        rows, keys = head_rows(head), slice(block * KEY_BLOCK, (block + 1) * KEY_BLOCK)
        start = first_query(block)

        def values_part():
            values_grad_ref[rows, keys] = low(
                dot(incoming_ref[rows, start:], probs_ref[block % 2, start:], NN)
            )

        def keys_part():
            keys_grad_ref[rows, keys] = low(
                dot(query_ref[rows, start:], score_grads_ref[block % 2, start:], NN) * scale
            )

        def query_part(at):
            stop = min(at + 2 * ROW_BLOCK, span)
            part = dot(keys_ref[rows, keys], score_grads_ref[block % 2, at:stop], NT)
            if block:
                part = part + held_ref[:, at:stop]
            held_ref[:, at:stop] = part

        def query_whole():
            query_grad_ref[rows] = low(held_ref[...] * scale)

        steps = [values_part, keys_part]
        steps += [partial(query_part, at) for at in range(start, span, 2 * ROW_BLOCK)]
        return steps + [query_whole] * (block == blocks - 1)

    prepare(first_head, 0)

    def body(pair, carry):
        for odd in range(2):
            head = first_head + 2 * pair + odd
            for block in range(blocks):
                if block:
                    steps = products(head, block - 1)
                else:
                    steps = products(jnp.maximum(head - 1, first_head), blocks - 1)
                starts = range(first_query(block), span, ROW_BLOCK)
                for step in range(max(len(starts), len(steps))):
                    if step < len(starts):
                        score(odd, block, starts[step])
                    if step < len(steps):
                        steps[step]()
                if block == 0:
                    prepare(jnp.minimum(head + 1, last_head - 1), 1 - odd)
                if beside:
                    beside((2 * pair + odd) * blocks + block, (last_head - first_head) * blocks)
        return carry

    lax.fori_loop(0, (last_head - first_head) // 2, body, 0)
    for step in products(last_head - 1, blocks - 1):
        step()


ROOT = math.sqrt(2 / math.pi)
CUBE = ROOT * 0.044715


def gelu_parts(value):
    half = 0.5 * value
    cube = CUBE * (value * value)
    tanh = jnp.tanh(value * (ROOT + cube))
    more = 1 + tanh
    return half * more, more * (0.5 + (1 - tanh) * (half * (ROOT + 3 * cube)))


def opening_kernel(token_ref):
    token_ref[...] = jnp.zeros(token_ref.shape, single)


def projection_kernel(input_ref, maps_ref, bias_ref, input_t_ref, qkv_ref):
    columns = columns_of([bias_ref[0:1], bias_ref[1:2]])
    inputs = input_ref[0, 0].T
    input_t_ref[...] = inputs
    width = inputs.shape[0]
    qkv_ref[0:width] = low(dot(maps_ref[0], inputs, TN) + columns[:, 0:1])
    qkv_ref[width : 2 * width] = low(dot(maps_ref[1], inputs, TN))
    qkv_ref[2 * width :] = low(dot(maps_ref[2], inputs, TN) + columns[:, 1:2])


def self_forward_kernel(
    limit_ref, input_t_ref, qkv_ref, output_ref, bias_ref, omega_ref,
    mixed_ref, totals_ref, normed_ref, scaled_ref, *scratch,
):
    columns = columns_of([bias_ref[2:3], omega_ref[0:1]])
    width, span = input_t_ref.shape
    position = lax.broadcasted_iota(jnp.int32, (1, span), 1)
    mask = jnp.where(wide(position) < limit_ref[0:1, 0:1], 0.0, far)
    attend_forward(
        qkv_ref.at[0:width], qkv_ref.at[width : 2 * width], qkv_ref.at[2 * width :],
        mask, True, mixed_ref, totals_ref, scratch,
    )
    branch = dot(output_ref[...], mixed_ref[...], TN) + columns[:, 0:1]
    normed, scaled = normalize(wide(input_t_ref[...]) * columns[:, 1:2] + branch)
    normed_ref[...] = normed
    scaled_ref[...] = scaled


def source_mask(limit, half, size):
    local = lax.broadcasted_iota(jnp.int32, (1, 2 * size), 1)
    own = local < size
    position = jnp.where(own, local + half * size, local - size + (1 - half) * size)
    return jnp.where(wide(position) < limit, 0.0, far)


def cross_forward_kernel(
    limit_ref, normed_ref, memory_ref, arrived_ref, maps_ref, output_ref, bias_ref,
    gain_ref, shift_ref, omega_ref,
    memory_t_ref, query_ref, keys_ref, values_ref, mixed_ref, totals_ref,
    second_normed_ref, second_scaled_ref, *scratch,
):
    half = lax.axis_index("half")
    columns = columns_of(
        [bias_ref[3:4], bias_ref[4:5], bias_ref[5:6], gain_ref[0:1], shift_ref[0:1], omega_ref[1:2]]
    )
    size = memory_ref.shape[2]
    first = normed_ref[...] * columns[:, 3:4] + columns[:, 4:5]
    query_ref[...] = low(dot(maps_ref[0], low(first), TN) + columns[:, 0:1])
    memory_t_ref[:, :size] = memory_ref[half, 0].T
    memory_t_ref[:, size:] = arrived_ref[...].T
    keys_ref[...] = low(dot(maps_ref[1], memory_t_ref[...], TN))
    values_ref[...] = low(dot(maps_ref[2], memory_t_ref[...], TN) + columns[:, 1:2])
    mask = source_mask(limit_ref[1:2, 0:1], half, size)
    attend_forward(query_ref, keys_ref, values_ref, mask, False, mixed_ref, totals_ref, scratch)
    branch = dot(output_ref[...], mixed_ref[...], TN) + columns[:, 2:3]
    second_normed, second_scaled = normalize(first * columns[:, 5:6] + branch)
    second_normed_ref[...] = second_normed
    second_scaled_ref[...] = second_scaled


def ffn_kernel(
    second_normed_ref, gain_ref, shift_ref, omega_ref, expand_ref, expand_bias_ref, shrink_ref,
    shrink_bias_ref, grad_ref,
    layer_ref, back_ref, stats_ref, keep_ref, send_ref,
    hidden_ref, slope_ref, held_ref, wide_held_ref,
    *, shift,
):
    me, half = ranks(shift)
    columns = columns_of(
        [gain_ref[1:2], gain_ref[2:3], shift_ref[1:2], shift_ref[2:3], omega_ref[2:3]]
        + [shrink_bias_ref[...].reshape(1, -1)]
        + [expand_bias_ref[i : i + 512].reshape(1, -1) for i in range(0, expand_ref.shape[1], 512)]
    )
    width, span = second_normed_ref.shape
    second = second_normed_ref[...] * columns[:, 0:1] + columns[:, 2:3]
    second_low = low(second)
    features = expand_ref.shape[1]
    chunk = 512
    ffn = None
    for at in range(0, features, chunk):
        part = slice(at, at + chunk)
        pre = dot(expand_ref[:, part], second_low, TN) + columns[:, 6 + at // chunk : 7 + at // chunk]
        value, slope = gelu_parts(pre)
        hidden_ref[part] = low(value)
        slope_ref[part] = low(slope)
        term = dot(shrink_ref[part], hidden_ref[part], TN)
        ffn = term if ffn is None else ffn + term
    third_normed, third_scaled = normalize(second * columns[:, 4:5] + (ffn + columns[:, 5:6]))
    layer_ref[0, 0] = (third_normed * columns[:, 1:2] + columns[:, 3:4]).T
    grad = wide(grad_ref[0, 0].T)
    third_grad, gain_third, shift_third = normalize_back(
        grad, third_normed, third_scaled, columns[:, 1:2]
    )
    scale_third = over_tokens(second * third_grad)
    ffn_low = low(third_grad)
    shrink_bias_grad = over_tokens(wide(ffn_low))
    second_grad = third_grad * columns[:, 4:5]
    sums = []
    chunk = 2048
    for at in range(0, features, chunk):
        part = slice(at, at + chunk)
        wide_held_ref[part] = low(dot(hidden_ref[part], ffn_low, NT))
        pre_grad = low(dot(shrink_ref[part], ffn_low, NN) * wide(slope_ref[part]))
        sums.append(over_tokens(wide(pre_grad)))
        held_ref[:, part] = low(dot(second_low, pre_grad, NT))
        second_grad = second_grad + dot(expand_ref[:, part], pre_grad, NN)
    back_ref[...] = second_grad
    rows = features // GROUPS // 4
    for core, place, group, portion in places(me, half):
        out = send_ref if core else keep_ref
        start = pl.multiple_of(group * rows + portion * (rows // 2), rows // 2)
        out[(*place, slice(None), slice(0, features))] = held_ref[pl.ds(start, rows // 2), :]
        for piece in range(4):
            start = (4 * group + piece) * rows + portion * (rows // 2)
            lanes = slice(features + piece * width, features + (piece + 1) * width)
            out[(*place, slice(None), lanes)] = wide_held_ref[
                pl.ds(pl.multiple_of(start, rows // 2), rows // 2), :
            ]
    expand_sums = jnp.concatenate(sums, axis=0)
    pieces = [
        jnp.concatenate(
            [
                expand_sums[(4 * group + piece) * rows : (4 * group + piece + 1) * rows]
                for group in range(GROUPS)
            ],
            axis=0,
        )
        for piece in range(4)
    ]
    stats_ref[...] = put_columns(
        jnp.zeros(stats_ref.shape, single),
        [(8, gain_third), (11, shift_third), (14, scale_third), (15, shrink_bias_grad)]
        + [(16 + piece, pieces[piece]) for piece in range(4)],
    )


def norm_grad(grad, normed, scaled, gain):
    inner = grad * gain
    return scaled * (
        inner
        - jnp.mean(inner, axis=0, keepdims=True)
        - normed * jnp.mean(inner * normed, axis=0, keepdims=True)
    )


def sums_scratch(width):
    return [pltpu.VMEM((width, 8), single), pltpu.VMEM((4, width, 1), single)]


def norm_sums(grad_ref, normed_ref, back_ref, input_of, columns_ref, omega, sums_ref):
    def some(step, steps):
        size = back_ref.shape[0] // steps
        rows = pl.ds(pl.multiple_of(step * size, size), size)
        grad, back = grad_ref[rows], back_ref[rows]
        sums_ref[0, rows] = over_tokens(grad * normed_ref[rows])
        sums_ref[1, rows] = over_tokens(grad)
        sums_ref[2, rows] = over_tokens(input_of(rows) * back)
        sums_ref[3, rows] = over_tokens(wide(low(back)))
        back_ref[rows] = back * columns_ref[rows, omega : omega + 1]

    return some


def cross_back_kernel(
    limit_ref, normed_ref, second_normed_ref, second_scaled_ref, back_ref,
    query_ref, keys_ref, values_ref, mixed_ref, totals_ref, output_ref,
    gain_ref, shift_ref, omega_ref, stats_in_ref,
    part_grad_ref, incoming_ref, output_grad_ref, stats_ref,
    query_grad_ref, keys_grad_ref, values_grad_ref, *scratch,
):
    half = lax.axis_index("half")
    columns = columns_of([gain_ref[0:1], shift_ref[0:1], gain_ref[1:2], omega_ref[1:2]])
    size = keys_ref.shape[1] // 2
    *scratch, columns_ref, sums_ref = scratch
    columns_ref[...] = columns
    sum_grad = norm_grad(
        back_ref[...], second_normed_ref[...], second_scaled_ref[...], columns[:, 2:3]
    )
    part_grad_ref[...] = sum_grad
    cross_low = low(sum_grad)
    incoming_ref[...] = low(dot(output_ref[...], cross_low, NN))
    output_grad_ref[...] = low(dot(mixed_ref[...], cross_low, NT))
    mask = source_mask(limit_ref[1:2, 0:1], half, size)

    def first_of(rows):
        return normed_ref[rows] * columns_ref[rows, 0:1] + columns_ref[rows, 1:2]

    attend_backward(
        query_ref, keys_ref, values_ref, mixed_ref, totals_ref, incoming_ref, mask, False,
        query_grad_ref, keys_grad_ref, values_grad_ref, 0, CROSS_FIRST, scratch,
        norm_sums(back_ref, second_normed_ref, part_grad_ref, first_of, columns_ref, 3, sums_ref),
    )
    stats_ref[...] = put_columns(
        stats_in_ref[...], [(7, sums_ref[0]), (10, sums_ref[1]), (13, sums_ref[2]), (5, sums_ref[3])]
    )


def cross_rest_kernel(
    limit_ref, normed_ref, memory_t_ref, query_ref, keys_ref, values_ref, mixed_ref, totals_ref,
    maps_ref, gain_ref, shift_ref, part_grad_ref, incoming_ref, output_grad_ref, stats_in_ref,
    query_half_ref, keys_half_ref, values_half_ref,
    first_grad_ref, own_ref, away_ref, stats_ref, keep_ref, send_ref,
    query_grad_ref, keys_grad_ref, values_grad_ref, held_ref, *scratch, shift,
):
    me, across = ranks(shift)
    columns = columns_of([gain_ref[0:1], shift_ref[0:1]])
    size = own_ref.shape[1]
    width = normed_ref.shape[0]
    mask = source_mask(limit_ref[1:2, 0:1], lax.axis_index("half"), size)
    attend_backward(
        query_ref, keys_ref, values_ref, mixed_ref, totals_ref, incoming_ref, mask, False,
        query_grad_ref, keys_grad_ref, values_grad_ref, CROSS_FIRST, HEADS, scratch,
    )
    top = slice(0, CROSS_FIRST * HEAD)
    query_grad_ref[top] = query_half_ref[top]
    keys_grad_ref[top] = keys_half_ref[top]
    values_grad_ref[top] = values_half_ref[top]
    query_grad, keys_grad, values_grad = query_grad_ref[...], keys_grad_ref[...], values_grad_ref[...]
    first_low = low(normed_ref[...] * columns[:, 0:1] + columns[:, 1:2])
    pack(keep_ref, send_ref, held_ref, output_grad_ref[...], 3 * width, me, across)
    pack(keep_ref, send_ref, held_ref, dot(first_low, query_grad, NT), 0, me, across)
    pack(keep_ref, send_ref, held_ref, dot(memory_t_ref[...], keys_grad, NT), width, me, across)
    pack(keep_ref, send_ref, held_ref, dot(memory_t_ref[...], values_grad, NT), 2 * width, me, across)
    first_grad_ref[...] = part_grad_ref[...] + dot(maps_ref[0], query_grad, NN)
    memory_grad = dot(maps_ref[1], keys_grad, NN) + dot(maps_ref[2], values_grad, NN)
    own_ref[...] = memory_grad[:, :size]
    away_ref[...] = low(memory_grad[:, size:])
    stats_ref[...] = put_columns(
        stats_in_ref[...],
        [(3, over_tokens(wide(query_grad))), (4, over_tokens(wide(values_grad)))],
    )


def self_back_kernel(
    limit_ref, input_t_ref, normed_ref, scaled_ref, first_grad_ref, qkv_ref, mixed_ref, totals_ref,
    output_ref, gain_ref, omega_ref, stats_in_ref,
    part_grad_ref, incoming_ref, stats_ref, query_grad_ref, keys_grad_ref, values_grad_ref,
    keep_ref, send_ref, held_ref, *scratch, shift,
):
    me, _ = ranks(shift)
    columns = columns_of([gain_ref[0:1], omega_ref[0:1]])
    *scratch, columns_ref, sums_ref = scratch
    columns_ref[...] = columns
    width, span = input_t_ref.shape
    sum_grad = norm_grad(first_grad_ref[...], normed_ref[...], scaled_ref[...], columns[:, 0:1])
    part_grad_ref[...] = sum_grad
    self_low = low(sum_grad)
    inputs = input_t_ref[...]
    incoming_ref[...] = low(dot(output_ref[...], self_low, NN))
    output_grad = dot(mixed_ref[...], self_low, NT)
    position = lax.broadcasted_iota(jnp.int32, (1, span), 1)
    mask = jnp.where(wide(position) < limit_ref[0:1, 0:1], 0.0, far)
    attend_backward(
        qkv_ref.at[0:width], qkv_ref.at[width : 2 * width], qkv_ref.at[2 * width :],
        mixed_ref, totals_ref, incoming_ref, mask, True,
        query_grad_ref, keys_grad_ref, values_grad_ref, 0, HEADS // 2, scratch,
        norm_sums(
            first_grad_ref, normed_ref, part_grad_ref, lambda rows: wide(input_t_ref[rows]),
            columns_ref, 1, sums_ref,
        ),
    )
    stats_ref[...] = put_columns(
        stats_in_ref[...], [(6, sums_ref[0]), (9, sums_ref[1]), (12, sums_ref[2]), (2, sums_ref[3])]
    )
    pack(keep_ref, send_ref, held_ref, output_grad, 3 * width // 2, me, None)
    pack_maps(
        keep_ref, send_ref, held_ref, inputs, (query_grad_ref, keys_grad_ref, values_grad_ref),
        slice(0, width // 2), me,
    )


def pack_maps(keep_ref, send_ref, held_ref, inputs, grads, rows, me):
    for at, ref in enumerate(grads):
        part = dot(inputs, ref[rows], NT)
        pack(keep_ref, send_ref, held_ref, part, at * part.shape[1], me, None)


def self_heads_kernel(
    limit_ref, qkv_ref, mixed_ref, totals_ref, incoming_ref,
    query_half_ref, keys_half_ref, values_half_ref,
    query_grad_ref, keys_grad_ref, values_grad_ref, *scratch,
):
    width, span = mixed_ref.shape
    position = lax.broadcasted_iota(jnp.int32, (1, span), 1)
    mask = jnp.where(wide(position) < limit_ref[0:1, 0:1], 0.0, far)
    attend_backward(
        qkv_ref.at[0:width], qkv_ref.at[width : 2 * width], qkv_ref.at[2 * width :],
        mixed_ref, totals_ref, incoming_ref, mask, True,
        query_grad_ref, keys_grad_ref, values_grad_ref, HEADS // 2, HEADS, scratch,
    )
    top = slice(0, width // 2)
    query_grad_ref[top] = query_half_ref[top]
    keys_grad_ref[top] = keys_half_ref[top]
    values_grad_ref[top] = values_half_ref[top]


def self_rest_kernel(
    input_t_ref, stats_in_ref, query_grad_ref, keys_grad_ref, values_grad_ref,
    keep_ref, send_ref, held_ref, *, shift,
):
    me, _ = ranks(shift)
    width = input_t_ref.shape[0]
    pack_maps(
        keep_ref, send_ref, held_ref, input_t_ref[...], (query_grad_ref, keys_grad_ref, values_grad_ref),
        slice(width // 2, width), me,
    )
    stats = put_columns(
        stats_in_ref[...],
        [(0, over_tokens(wide(query_grad_ref[...]))), (1, over_tokens(wide(values_grad_ref[...])))],
    )
    pack(keep_ref, send_ref, held_ref, stats, 3 * width // 2, me, None)


def input_kernel(
    part_grad_ref, query_grad_ref, keys_grad_ref, values_grad_ref, maps_ref, input_grad_ref, token_ref
):
    token_ref[...] = jnp.zeros(token_ref.shape, single)
    input_grad_ref[0, 0] = (
        part_grad_ref[...]
        + dot(maps_ref[0], query_grad_ref[...], NN)
        + dot(maps_ref[1], keys_grad_ref[...], NN)
        + dot(maps_ref[2], values_grad_ref[...], NN)
    ).T


def halve_kernel(kept_ref, arrived_ref, sent_out_ref, kept_out_ref):
    part = kept_ref.shape[0] // 2
    at = slice(part, None) if part > 1 else 1
    sent_out_ref[...] = low(wide(kept_ref[at]) + wide(arrived_ref[at]))
    at = slice(0, part) if part > 1 else 0
    kept_out_ref[...] = low(wide(kept_ref[at]) + wide(arrived_ref[at]))


def sum_kernel(kept_ref, arrived_ref, out_ref):
    out_ref[...] = low(wide(kept_ref[...]) + wide(arrived_ref[...]))


def memory_kernel(own_ref, returned_ref, rest_ref, out_ref, token_ref):
    token_ref[...] = jnp.zeros(token_ref.shape, single)
    half = lax.axis_index("half")
    out_ref[half, 0] = own_ref[...].T + rest_ref[half, 0]
    out_ref[1 - half, 0] = wide(returned_ref[...]).T + rest_ref[1 - half, 0]


def finish(ffn, cross, early, late, width):
    features = ffn.shape[1] // 2
    part = width // 2
    maps = [
        jnp.concatenate([v[:, i * part : (i + 1) * part] for v in (early, late)], axis=1)
        for i in range(3)
    ]
    cross_maps = [cross[:, i * width : (i + 1) * width] for i in range(3)]
    shrink = jnp.concatenate(
        [ffn[:, features + i * width : features + (i + 1) * width] for i in range(4)], axis=0
    )
    stats = late[:, 3 * part :].T
    return (
        maps, early[:, 3 * part :], cross_maps, cross[:, 3 * width :],
        stats[0:6], ffn[:, :features],
        jnp.concatenate([stats[16 + i : 17 + i] for i in range(4)], axis=1).reshape(-1), shrink,
        stats[15:16].reshape(-1), stats[6:9], stats[9:12], stats[12:15],
    )


def finish_kernel(*refs, shift):
    ins, outs, held = refs[:8], refs[8:-4], refs[-4:]
    half = lax.axis_index("half")
    width = outs[1].shape[1]
    for i in range(4):
        own, other = wide(ins[2 * i][...]), wide(ins[2 * i + 1][...])
        if shift or i >= 2:
            held[i][...] = own + other
        else:
            rows = own.shape[0]
            held[i][pl.ds(pl.multiple_of(half * rows, rows), rows)] = own
            held[i][pl.ds(pl.multiple_of((1 - half) * rows, rows), rows)] = other
    for ref, value in zip(outs, finish(*(ref[...] for ref in held), width)):
        if isinstance(value, list):
            for at, item in enumerate(value):
                ref[at] = item.reshape(ref.shape[1:])
        else:
            ref[...] = value


TIMES = {
    "opening": 6, "self_forward": 9, "cross_forward": 13, "ffn": 20, "cross_back": 7, "cross_rest": 18,
    "self_back": 10, "self_heads": 7, "self_rest": 1, "input_grad": 3, "memory_grad": 2,
}
MICROSECOND = 1_000_000_000


def call(kernel, name, outs, scratch=(), after=(), vmem=13, **options):
    def entry(*refs):
        kernel(*refs[len(after) :], **options)

    return lambda *args: pl.pallas_call(
        entry,
        name=name,
        out_shape=outs,
        in_specs=[pl.BlockSpec(memory_space=pl.ANY)] * len(after) + [VM] * len(args),
        out_specs=jax.tree.map(lambda _: VM, outs),
        scratch_shapes=scratch,
        compiler_params=pltpu.CompilerParams(vmem_limit_bytes=int(vmem * 1024 * 1024)),
        cost_estimate=pl.CostEstimate(
            flops=TIMES.get(name, 0) * MICROSECOND, bytes_accessed=1, transcendentals=0
        ),
    )(*after, *args)


def shards(
    block_input, memory, memory_grad_rest, output_grad, target_length, source_length,
    self_maps, self_output, cross_maps, cross_output, attention_bias,
    expand_weight, expand_bias, shrink_weight, shrink_bias, norm_gain, norm_bias, residual_scale,
    *, devices,
):
    span, width = block_input.shape[2:]
    size = memory.shape[2]
    source = 2 * size
    features = expand_weight.shape[1]
    shift = int(math.log2(devices // GROUPS))
    assert GROUPS << shift == devices
    rows = width // GROUPS
    half = lax.axis_index("half")

    def swap_half(value):
        return lax.ppermute(value, "half", [(0, 1), (1, 0)])

    def swap(value, bits):
        return lax.ppermute(value, "batch", [(i, i ^ bits) for i in range(devices)])

    def halve(kept, arrived, *after):
        part = kept.shape[0] // 2
        shape = kept.shape[1:] if part == 1 else (part, *kept.shape[1:])
        return call(halve_kernel, "halve", [sds(shape, bfloat)] * 2, after=after)(kept, arrived)

    def joined(kept, arrived, *after):
        return call(sum_kernel, "join", sds(kept.shape, bfloat), after=after)(kept, arrived)

    CORE, NEAR, NEXT, AWAY = 1, 2, 4, 8

    def scattered(keep, send, pieces=None):
        packet = jnp.stack([keep, send])
        if packet.ndim == 6:
            packet = packet.transpose(3, 1, 0, 2, 4, 5)
        else:
            packet = packet.transpose(2, 1, 0, 3, 4)
        packet = packet.reshape(2, 2, 4, rows, -1).swapaxes(0, 1)
        packet = packet.reshape(GROUPS, rows, -1)
        if pieces:
            start, stop = pieces
            part = packet[..., start:stop].reshape(GROUPS, rows, 4, -1).swapaxes(1, 2)
            part = part.reshape(GROUPS, 1 << shift, 4, rows >> shift, -1).swapaxes(2, 3)
            part = part.reshape(GROUPS, rows, stop - start)
            packet = jnp.concatenate([packet[..., :start], part, packet[..., stop:]], axis=-1)
        total = lax.psum_scatter(
            packet.reshape(width, -1), "batch", scatter_dimension=0, tiled=True
        )
        return total, swap_half(total)

    arrived = swap_half(lax.dynamic_index_in_dim(memory, 1 - half, 0, keepdims=False)[0])
    tall = sds((width, span), bfloat)
    tall_wide = sds((width, span), single)
    packet = lambda lanes: [sds((2, 2, 4, rows // 2, lanes), bfloat)] * 2
    simple = lambda lanes: [sds((2, 4, rows, lanes), bfloat)] * 2
    limits = jnp.broadcast_to(
        jnp.concatenate([target_length, source_length]).astype(single), (2, LANES)
    )
    opening = call(opening_kernel, "opening", sds((8, LANES), single))()
    input_t, qkv = call(
        projection_kernel, "projections", [tall, sds((3 * width, span), bfloat)], after=(opening,),
    )(block_input, self_maps, attention_bias)
    mixed, totals, normed, scaled = call(
        self_forward_kernel, "self_forward",
        [tall, sds((HEADS, span), single), tall_wide, sds((1, span), single)],
        scratch=forward_scratch(span),
    )(limits, input_t, qkv, self_output, attention_bias, residual_scale)
    source_tall = sds((width, source), bfloat)
    (
        memory_t, query, keys, values, cross_mixed, cross_totals, second_normed, second_scaled,
    ) = call(
        cross_forward_kernel, "cross_forward",
        [source_tall, tall, source_tall, source_tall, tall, sds((HEADS, span), single),
         tall_wide, sds((1, span), single)],
        scratch=forward_scratch(span),
    )(
        limits, normed, memory, arrived, cross_maps, cross_output, attention_bias,
        norm_gain, norm_bias, residual_scale,
    )
    layer_output, second_grad, stats, ffn_keep, ffn_send = call(
        ffn_kernel, "ffn",
        [sds((1, 1, span, width), single), tall_wide, sds((width, LANES), single)]
        + packet(2 * features),
        scratch=[pltpu.VMEM((features, span), bfloat)] * 2
        + [pltpu.VMEM((width, features), bfloat), pltpu.VMEM((features, width), bfloat)],
        shift=shift, vmem=31.125,
    )(
        second_normed, norm_gain, norm_bias, residual_scale, expand_weight,
        expand_bias, shrink_weight, shrink_bias, output_grad,
    )
    grads = [pltpu.VMEM((width, span), bfloat)] + [pltpu.VMEM((width, source), bfloat)] * 2
    held = pltpu.VMEM((width, width), bfloat)
    square = sds((width, width), bfloat)
    stats_shape = sds((width, LANES), single)
    part_grad, incoming, output_part, stats, *halves = call(
        cross_back_kernel, "cross_back",
        [tall_wide, tall, square, stats_shape, tall, source_tall, source_tall],
        scratch=backward_scratch(span) + sums_scratch(width),
    )(
        limits, normed, second_normed, second_scaled, second_grad,
        query, keys, values, cross_mixed, cross_totals, cross_output,
        norm_gain, norm_bias, residual_scale, stats,
    )
    if not shift:
        ffn = halve(ffn_keep, swap(ffn_send, CORE), part_grad)
    first_grad, own, away, stats, cross_keep, cross_send = call(
        cross_rest_kernel, "cross_rest",
        [tall_wide, sds((width, size), single), sds((width, size), bfloat), stats_shape]
        + packet(4 * width),
        scratch=grads + [held] + backward_scratch(span), after=() if shift else ffn, shift=shift,
    )(
        limits, normed, memory_t, query, keys, values, cross_mixed, cross_totals, cross_maps,
        norm_gain, norm_bias, part_grad, incoming, output_part, stats, *halves,
    )
    returned = swap_half(away)
    part_grad, incoming, stats, *rest_of = call(
        self_back_kernel, "self_back",
        [tall_wide, tall, stats_shape, tall, tall, tall] + simple(5 * width // 2),
        scratch=[held] + backward_scratch(span) + sums_scratch(width),
        shift=shift,
    )(
        limits, input_t, normed, scaled, first_grad, qkv, mixed, totals,
        self_output, norm_gain, residual_scale, stats,
    )
    *halves, early_keep, early_send = rest_of
    before = ()
    if not shift:
        ffn = halve(ffn[1], swap(ffn[0], NEAR), stats)
        cross = halve(cross_keep, swap(cross_send, CORE), *ffn)
        before = (*ffn, *cross, returned)
    grads_out = call(
        self_heads_kernel, "self_heads", [tall] * 3,
        scratch=backward_scratch(span), after=before,
    )(limits, qkv, mixed, totals, incoming, *halves)
    before = ()
    if not shift:
        early = halve(early_keep, swap(early_send, CORE), grads_out[0])
        before = early
    late_keep, late_send = call(
        self_rest_kernel, "self_rest", simple(3 * width // 2 + LANES),
        scratch=[held], after=before, shift=shift,
    )(input_t, stats, *grads_out)
    def to_memory(*after):
        return call(
            memory_kernel, "memory_grad",
            [sds(memory_grad_rest.shape, single), sds((8, LANES), single)], after=after,
        )(own, returned, memory_grad_rest)

    def to_input(*after):
        return call(
            input_kernel, "input_grad", [sds((1, 1, span, width), single), sds((8, LANES), single)],
            after=after,
        )(part_grad, *grads_out, self_maps)

    if shift:
        input_grad, _ = to_input()
        memory_grad, token = to_memory()
        start = 3 * width // 2 + 16
        parts = (
            *scattered(ffn_keep, ffn_send, (features, 2 * features)),
            *scattered(cross_keep, cross_send),
            *scattered(early_keep, early_send),
            *scattered(late_keep, late_send, (start, start + 4)),
        )
    else:
        ffn = halve(ffn[1], swap_half(ffn[0]), late_keep)
        cross = halve(cross[1], swap(cross[0], NEAR), *ffn)
        late = halve(late_keep, swap(late_send, CORE), *cross)
        input_grad, token = to_input(*late)
        early = halve(early[1], swap(early[0], NEAR), token)
        ffn = halve(ffn[1], swap(ffn[0], NEXT), *early)
        cross = halve(cross[1], swap_half(cross[0]), *ffn)
        late = halve(late[1], swap(late[0], NEAR), *cross)
        early = halve(early[1], swap(early[0], NEXT), *late)
        ffn = joined(ffn[1], swap(ffn[0], AWAY), *early)
        cross = halve(cross[1], swap(cross[0], NEXT), ffn)
        late = halve(late[1], swap(late[0], NEXT), *cross)
        early = joined(early[1], swap(early[0], AWAY), *late)
        cross = joined(cross[1], swap(cross[0], AWAY), early)
        late = joined(late[1], swap(late[0], AWAY), cross)
        memory_grad, token = to_memory(late)
        parts = tuple(
            part for value in (ffn, cross, early, late) for part in (value, swap_half(value))
        )
    mine = rows >> shift
    outs = [
        sds((3, mine, width), single), sds((mine, width), single), sds((3, mine, width), single),
        sds((mine, width), single), sds((6, mine), single), sds((mine, features), single),
        sds((4 * mine,), single), sds((4 * mine, width), single), sds((mine,), single),
        sds((3, mine), single), sds((3, mine), single), sds((3, mine), single),
    ]
    done = list(
        call(
            finish_kernel, "finish", outs, shift=shift, after=(token,),
            scratch=[
                pltpu.VMEM((mine, lanes), single)
                for lanes in (2 * features, 4 * width, 5 * width // 2, 3 * width // 2 + LANES)
            ],
        )(*parts)
    )
    return (layer_output, input_grad, memory_grad, *done)


def solution(mesh):
    rows = P("half", "batch", None, None)
    sources = P(None, "batch", "half", None)
    placed = (rows, sources, sources, rows, P("half", "batch"), P("half", "batch")) + (P(),) * 12
    return jax.shard_map(
        partial(shards, devices=mesh.shape["batch"]),
        mesh=mesh,
        in_specs=placed,
        out_specs=(
            rows, rows, sources,
            P(None, "batch", None), P("batch", None), P(None, "batch", None), P("batch", None),
            P(None, "batch"), P("batch", None), P("batch"), P("batch", None), P("batch"),
            P(None, "batch"), P(None, "batch"), P(None, "batch"),
        ),
        check_vma=False,
    )
```
